32 devices in a mesh: replica: 4 (over z), shard: 8 (over y, x, core).
Axes of the slice: x: 2, y: 2, z: 4, core: 2. Of those that a mesh axis runs over, the one named last changes fastest.
Arguments:
- hidden_in: bfloat16 [6144, 2304], P(('replica', 'shard')), may hold values from -16 to 16
- cotangent: bfloat16 [6144, 2304], P(('replica', 'shard')), may hold values from -6 to 6
- token_segment: int32 [6144], P('replica'), may hold values from 0 to 12, as said below
- token_valid: int32 [6144], P('replica'), may hold values from 0 to 1, as said below
- segment_parent: int32 [4, 13], P('replica'), may hold values from 0 to 4, as said below
- query_weight: bfloat16 [2048, 2304], P('shard'), may hold values from -0.125 to 0.125
- key_weight: bfloat16 [1024, 2304], P('shard'), may hold values from -0.125 to 0.125
- value_weight: bfloat16 [1024, 2304], P('shard'), may hold values from -0.125 to 0.125
- output_weight: bfloat16 [2048, 2304], P('shard'), may hold values from -0.125 to 0.125
- gate_weight: bfloat16 [9216, 2304], P('shard'), may hold values from -0.125 to 0.125
- up_weight: bfloat16 [9216, 2304], P('shard'), may hold values from -0.125 to 0.125
- down_weight: bfloat16 [9216, 2304], P('shard'), may hold values from -0.0625 to 0.0625
- attention_gain: float32 [2304], replicated, may hold values from -1.2 to 1.2
- attention_post_gain: float32 [2304], replicated, may hold values from -1.2 to 1.2
- feedforward_gain: float32 [2304], replicated, may hold values from -1.2 to 1.2
- feedforward_post_gain: float32 [2304], replicated, may hold values from -1.2 to 1.2
Outputs:
- block_out: bfloat16 [6144, 2304], P(('replica', 'shard'))
- input_grad: float32 [6144, 2304], P(('replica', 'shard'))
- query_grad: float32 [2048, 2304], P('shard')
- key_grad: float32 [1024, 2304], P('shard')
- value_grad: float32 [1024, 2304], P('shard')
- output_grad: float32 [2048, 2304], P('shard')
- gate_grad: float32 [9216, 2304], P('shard')
- up_grad: float32 [9216, 2304], P('shard')
- down_grad: float32 [9216, 2304], P('shard')
- attention_gain_grad: float32 [2304], replicated
- attention_post_gain_grad: float32 [2304], replicated
- feedforward_gain_grad: float32 [2304], replicated
- feedforward_post_gain_grad: float32 [2304], replicated
- stream_rms: float32 [4], replicated
The draws below stay inside these ranges and needn't reach their ends.
Inputs may be any that keep to these rules, and one draw needn't show every extreme that they name: `token_segment`: segment numbers never fall along a tree's 1536 token slots; each segment has one or more valid tokens; tokens with valid 0 stand at the end of their tree, in segment 13 - 1. `token_valid`: each tree ends in one or more padding tokens. `segment_parent`: row b is tree b's table: segment 0 is the trunk and its own parent, segments 1 to 4 are branches with parent 0, and each branch is the parent of exactly two of the leaves 5 to 12.
All inputs are finite; a program needn't handle non-finite values.
Results may differ from the reference program's by a relative error of at most 0.015.
Values may be sent and summed in bfloat16 or wider, within the bound.
A program may use at most 320 MiB of HBM per device.

```python
import math
import jax
import jax.numpy as jnp
from jax import lax

D = 2304
HEADS = 8
KV_HEADS = 4
HEAD = 256
FF = 9216
SEGS = 13
QW = 2048
KVW = 1024
TREE_TOK = 1536
TREES = 4
TOKENS = 6144


def tree_layout(key):

    def one_tree(tree_key):
        pad_key, trunk_key, other_key = jax.random.split(tree_key, 3)
        padding = jax.random.randint(pad_key, (), 1, TREE_TOK // 8 + 1)
        live_count = TREE_TOK - padding
        trunk_share = jax.random.randint(trunk_key, (1,), 24, 41)
        other_share = jax.random.randint(other_key, (SEGS - 1,), 2, 7)
        shares = jnp.concatenate([trunk_share, other_share])
        spare_count = live_count - SEGS
        portions = spare_count * shares // jnp.sum(shares)
        labels = jnp.arange(SEGS, dtype=jnp.int32)
        lengths = 1 + portions + jnp.where(labels == 0, spare_count - jnp.sum(portions), 0)
        segment_ends = jnp.cumsum(lengths)
        token_index = jnp.arange(TREE_TOK, dtype=jnp.int32)
        segment = jnp.sum((token_index[:, None] >= segment_ends[None, :SEGS - 1]).astype(jnp.int32), axis=1)
        valid_mask = (token_index < live_count).astype(jnp.int32)
        return (segment, valid_mask)
    segment, valid_mask = jax.vmap(one_tree)(jax.random.split(key, TREES))
    return (segment.reshape(-1), valid_mask.reshape(-1))


def draw_token_segment(key, part):
    segment, valid_mask = tree_layout(key)
    return segment


def draw_token_valid(key, part):
    segment, valid_mask = tree_layout(key)
    return valid_mask


def draw_segment_parent(key, part):
    key = jax.random.fold_in(key, 7)

    def one_table(tree_key):
        leaf_order = jax.random.permutation(tree_key, jnp.arange(8, dtype=jnp.int32))
        return jnp.concatenate([jnp.zeros((5,), jnp.int32), 1 + leaf_order // 2])
    return jax.vmap(one_table)(jax.random.split(key, TREES))


def draw_hidden_in(key, part):
    key = jax.random.fold_in(key, 11)
    base_key = jax.random.fold_in(key, 0)
    token_index = jnp.arange(TOKENS, dtype=jnp.float32)
    rising = jnp.exp(math.log(3.0) * token_index / (TOKENS - 1))
    base_values = jax.random.truncated_normal(base_key, -4.0, 4.0, (TOKENS, D), jnp.float32)
    return (base_values * rising[:, None]).astype(jnp.bfloat16)


def steps_of(stream_key, dims, shards, smallest, top_value):
    loudness = 1.0
    for axis_at, blocks in shards:
        heights = jax.random.uniform(jax.random.fold_in(jax.random.fold_in(stream_key, 6), axis_at), (blocks,), jnp.float32, smallest / len(shards), top_value / len(shards))
        loudness = loudness * jnp.repeat(jnp.exp(heights), dims[axis_at] // blocks).reshape((-1,) + (1,) * (len(dims) - 1 - axis_at))
    return loudness


def centred(rng, extent, spread, reach, shards=(), kind=jnp.bfloat16):
    entries = jax.random.normal(rng, extent, jnp.float32) * spread
    if len(shards) > 0:
        entries = steps_of(rng, extent, shards, -0.22, 0.18) * entries
    return jnp.clip(entries, min=-reach, max=reach).astype(kind)


def setup_inputs(seed: int = 0) -> dict:
    splits = jax.random.split(jax.random.key(seed), 17)
    return {
        "hidden_in": draw_hidden_in(jax.random.fold_in(splits[16], 71), 0),
        "cotangent": centred(splits[1], (TOKENS, D), 1.0, 6.0, ((0, 32),)),
        "token_segment": draw_token_segment(jax.random.fold_in(splits[16], 71), 0),
        "token_valid": draw_token_valid(jax.random.fold_in(splits[16], 71), 0),
        "segment_parent": draw_segment_parent(jax.random.fold_in(splits[16], 71), 0),
        "query_weight": centred(splits[5], (QW, D), D ** -0.5, 0.125, ((0, 8),)),
        "key_weight": centred(splits[6], (KVW, D), D ** -0.5, 0.125, ((0, 8),)),
        "value_weight": centred(splits[7], (KVW, D), D ** -0.5, 0.125, ((0, 8),)),
        "output_weight": centred(splits[8], (QW, D), QW ** -0.5, 0.125, ((0, 8),)),
        "gate_weight": centred(splits[9], (FF, D), D ** -0.5, 0.125, ((0, 8),)),
        "up_weight": centred(splits[10], (FF, D), D ** -0.5, 0.125, ((0, 8),)),
        "down_weight": centred(splits[11], (FF, D), FF ** -0.5, 0.0625, ((0, 8),)),
        "attention_gain": centred(splits[12], (D,), 0.3, 1.2, (), jnp.float32),
        "attention_post_gain": centred(splits[13], (D,), 0.3, 1.2, (), jnp.float32),
        "feedforward_gain": centred(splits[14], (D,), 0.3, 1.2, (), jnp.float32),
        "feedforward_post_gain": centred(splits[15], (D,), 0.3, 1.2, (), jnp.float32),
    }


@jax.custom_vjp
def low(v):
    return lax.optimization_barrier(v.astype(jnp.bfloat16)).astype(jnp.float32)

@jax.custom_vjp
def low_back(v):
    return v

def low_keep(v):
    return (low(v), None)

def low_pass(kept, grad):
    return (grad,)

def back_keep(v):
    return (v, None)

def back_low(kept, grad):
    return (low(grad),)
low.defvjp(low_keep, low_pass)
low_back.defvjp(back_keep, back_low)
HIGHEST = lax.Precision.HIGHEST
norm_eps = 1e-06
score_cap = 50.0

def norm_rows(stream, norm_gain):
    factor = lax.rsqrt(lax.optimization_barrier(jnp.mean(stream * stream, axis=-1, keepdims=True)) + norm_eps)
    return stream * factor * (1.0 + norm_gain)

def rotate(values, cos_table, sin_table):
    half_width = values.shape[-1] // 2
    turned = jnp.concatenate([-values[..., half_width:], values[..., :half_width]], axis=-1)
    return values * cos_table + turned * sin_table

def rope_tables(position, head_size):
    half_width = head_size // 2
    frequency = jnp.power(10000.0, -jnp.arange(half_width, dtype=jnp.float32) * 2.0 / head_size)
    angles = position.astype(jnp.float32)[:, None] * frequency[None, :]
    angles = jnp.concatenate([angles, angles], axis=-1)[:, None, :]
    return (jnp.cos(angles), jnp.sin(angles))

def tree_tables(segment, valid_mask, parent):
    labels = jnp.arange(parent.shape[0], dtype=jnp.int32)
    member = (segment[:, None] == labels[None, :]).astype(jnp.int32)
    lengths = lax.optimization_barrier(jnp.sum(member * valid_mask[:, None], axis=0))
    starts = lax.optimization_barrier(jnp.sum((segment[:, None] < labels[None, :]).astype(jnp.int32), axis=0))
    parent_of = (parent[:, None] == labels[None, :]).astype(jnp.int32)
    grandparent = lax.optimization_barrier(jnp.sum(parent_of * parent[None, :], axis=1))
    parent_len = lax.optimization_barrier(jnp.sum(parent_of * lengths[None, :], axis=1))
    grand_of = (grandparent[:, None] == labels[None, :]).astype(jnp.int32)
    grand_len = lax.optimization_barrier(jnp.sum(grand_of * lengths[None, :], axis=1))
    offsets = jnp.where(parent != labels, parent_len, 0) + jnp.where(grandparent != parent, grand_len, 0)
    token_index = jnp.arange(segment.shape[0], dtype=jnp.int32)
    position = lax.optimization_barrier(jnp.sum(member * (offsets - starts)[None, :], axis=1)) + token_index
    parent_tok = lax.optimization_barrier(jnp.sum(member * parent[None, :], axis=1))
    grand_tok = lax.optimization_barrier(jnp.sum(member * grandparent[None, :], axis=1))
    return (position, parent_tok, grand_tok)

def allowed_mask(query_index, query_seg, query_parent, query_grand, key_index, key_seg, key_valid):
    lineage = (key_seg[None, :] == query_seg[:, None]) | (key_seg[None, :] == query_parent[:, None]) | (key_seg[None, :] == query_grand[:, None])
    earlier = (key_seg[None, :] != query_seg[:, None]) | (key_index[None, :] < query_index[:, None])
    itself = key_index[None, :] == query_index[:, None]
    return itself | (key_valid[None, :] == 1) & lineage & earlier

def capped_softmax(scores, allowed):
    capped = score_cap * jnp.tanh(scores / score_cap)
    held = jnp.where(allowed, capped, -1000000000.0)
    largest = lax.optimization_barrier(jnp.max(held, axis=-1, keepdims=True))
    raised = jnp.where(allowed, jnp.exp(held - largest), 0.0)
    return raised / lax.optimization_barrier(jnp.sum(raised, axis=-1, keepdims=True))

def matmul(left, right):
    return jnp.dot(left, right, precision=HIGHEST, preferred_element_type=jnp.float32)

def tree_layer(stream, weights, segment, valid_mask, parent):
    query_weight, key_weight, value_weight, output_weight, gate_weight, up_weight, down_weight, attention_gain, attention_post_gain, feedforward_gain, feedforward_post_gain = weights
    token_count = stream.shape[0]
    group_size = HEADS // KV_HEADS
    position, parent_tok, grand_tok = tree_tables(segment, valid_mask, parent)
    token_index = jnp.arange(token_count, dtype=jnp.int32)
    allowed = allowed_mask(token_index, segment, parent_tok, grand_tok, token_index, segment, valid_mask)
    cos_table, sin_table = rope_tables(position, HEAD)
    query_scale = HEAD ** (-0.5)
    normed_in = low(norm_rows(stream, attention_gain))
    query_lin = low_back(matmul(normed_in, query_weight.T))
    key_lin = low_back(matmul(normed_in, key_weight.T))
    value_lin = low_back(matmul(normed_in, value_weight.T))
    queries = low(rotate(query_lin.reshape(token_count, HEADS, HEAD), cos_table, sin_table) * query_scale)
    keys = low(rotate(key_lin.reshape(token_count, KV_HEADS, HEAD), cos_table, sin_table))
    values = low(value_lin.reshape(token_count, KV_HEADS, HEAD))
    query_groups = queries.reshape(token_count, KV_HEADS, group_size, HEAD).transpose(1, 2, 0, 3)
    key_groups = keys.transpose(1, 0, 2)
    value_groups = values.transpose(1, 0, 2)

    def one_head(blocks):
        query_block, key_block, value_block = blocks
        scores = low_back(jnp.einsum('rqd,kd->rqk', query_block, key_block, precision=HIGHEST))
        probs = low(capped_softmax(scores, allowed[None]))
        return jnp.einsum('rqk,kd->rqd', probs, value_block, precision=HIGHEST)
    attended = lax.map(jax.checkpoint(one_head), (query_groups, key_groups, value_groups))
    attended = low_back(low(attended.transpose(2, 0, 1, 3).reshape(token_count, HEADS * HEAD)))
    attention_pre = low_back(matmul(attended, output_weight))
    attention_branch = norm_rows(attention_pre, attention_post_gain)
    middle = stream + attention_branch
    normed_mid = low(norm_rows(middle, feedforward_gain))
    gate_lin = low_back(matmul(normed_mid, gate_weight.T))
    up_lin = low_back(matmul(normed_mid, up_weight.T))
    hidden = low_back(low(jax.nn.gelu(gate_lin, approximate=True) * up_lin))
    feedforward_pre = low_back(matmul(hidden, down_weight))
    feedforward_branch = norm_rows(feedforward_pre, feedforward_post_gain)
    result = middle + feedforward_branch
    row_weight = valid_mask.astype(jnp.float32)[:, None]
    squares = jnp.stack([jnp.sum(row_weight * summand * summand) for summand in (stream, attention_branch, feedforward_branch, result)])
    return (result, squares)

def reference(hidden_in, cotangent, token_segment, token_valid, segment_parent, query_weight, key_weight, value_weight, output_weight, gate_weight, up_weight, down_weight, attention_gain, attention_post_gain, feedforward_gain, feedforward_post_gain):
    tree_count = segment_parent.shape[0]
    model_width = hidden_in.shape[1]
    streams = hidden_in.astype(jnp.float32).reshape(tree_count, -1, model_width)
    segments = token_segment.reshape(tree_count, -1)
    valids = token_valid.reshape(tree_count, -1)
    params = (query_weight.astype(jnp.float32), key_weight.astype(jnp.float32), value_weight.astype(jnp.float32), output_weight.astype(jnp.float32), gate_weight.astype(jnp.float32), up_weight.astype(jnp.float32), down_weight.astype(jnp.float32), attention_gain, attention_post_gain, feedforward_gain, feedforward_post_gain)

    def forward(stream_all, weights):

        def one_tree(inputs):
            stream, segment, valid_mask, parent = inputs
            return tree_layer(stream, weights, segment, valid_mask, parent)
        return lax.map(jax.checkpoint(one_tree), (stream_all, segments, valids, segment_parent))
    (result, squares), pull_back = jax.vjp(forward, streams, params)
    seed_grad = cotangent.astype(jnp.float32).reshape(streams.shape) * valids.astype(jnp.float32)[:, :, None]
    input_grad, weight_grads = pull_back((seed_grad, jnp.zeros_like(squares)))
    total_count = jnp.sum(token_valid.astype(jnp.float32)) * model_width
    stream_rms = jnp.sqrt(lax.optimization_barrier(jnp.sum(squares, axis=0)) / total_count)
    return (result.reshape(hidden_in.shape).astype(jnp.bfloat16), input_grad.reshape(hidden_in.shape), weight_grads[0], weight_grads[1], weight_grads[2], weight_grads[3], weight_grads[4], weight_grads[5], weight_grads[6], weight_grads[7], weight_grads[8], weight_grads[9], weight_grads[10], stream_rms)
```

```python
import math

import jax
import jax.numpy as jnp
from jax import lax
from jax.sharding import PartitionSpec as P

HEADS = 8
KV_HEADS = 4
HEAD = 256


norm_eps = 1e-06
score_cap = 50.0


def norm_rows(stream, norm_gain):
    factor = lax.rsqrt(jnp.mean(stream * stream, axis=-1, keepdims=True) + norm_eps)
    return stream * factor * (1.0 + norm_gain)


def rotate(values, cos_table, sin_table):
    half_width = values.shape[-1] // 2
    turned = jnp.concatenate([-values[..., half_width:], values[..., :half_width]], axis=-1)
    return values * cos_table + turned * sin_table


def rotate_back(gradient, cos_table, sin_table):
    half_width = gradient.shape[-1] // 2
    shifted = gradient * sin_table
    unturned = jnp.concatenate([shifted[..., half_width:], -shifted[..., :half_width]], axis=-1)
    return gradient * cos_table + unturned


def rope_tables(position, head_size):
    half_width = head_size // 2
    frequency = jnp.power(10000.0, -jnp.arange(half_width, dtype=jnp.float32) * 2.0 / head_size)
    angles = position.astype(jnp.float32)[:, None] * frequency[None, :]
    angles = jnp.concatenate([angles, angles], axis=-1)[:, None, :]
    return (jnp.cos(angles), jnp.sin(angles))


def tree_tables(segment, valid_mask, parent):
    labels = jnp.arange(parent.shape[0], dtype=jnp.int32)
    member = (segment[:, None] == labels[None, :]).astype(jnp.int32)
    lengths = jnp.sum(member * valid_mask[:, None], axis=0)
    starts = jnp.sum((segment[:, None] < labels[None, :]).astype(jnp.int32), axis=0)
    parent_of = (parent[:, None] == labels[None, :]).astype(jnp.int32)
    grandparent = jnp.sum(parent_of * parent[None, :], axis=1)
    parent_len = jnp.sum(parent_of * lengths[None, :], axis=1)
    grand_of = (grandparent[:, None] == labels[None, :]).astype(jnp.int32)
    grand_len = jnp.sum(grand_of * lengths[None, :], axis=1)
    offsets = jnp.where(parent != labels, parent_len, 0) + jnp.where(
        grandparent != parent, grand_len, 0
    )
    token_index = jnp.arange(segment.shape[0], dtype=jnp.int32)
    position = jnp.sum(member * (offsets - starts)[None, :], axis=1) + token_index
    parent_tok = jnp.sum(member * parent[None, :], axis=1)
    grand_tok = jnp.sum(member * grandparent[None, :], axis=1)
    return (position, parent_tok, grand_tok)


def allowed_mask(query_index, query_seg, query_parent, query_grand, key_index, key_seg, key_valid):
    lineage = (
        (key_seg[None, :] == query_seg[:, None])
        | (key_seg[None, :] == query_parent[:, None])
        | (key_seg[None, :] == query_grand[:, None])
    )
    earlier = (key_seg[None, :] != query_seg[:, None]) | (key_index[None, :] < query_index[:, None])
    itself = key_index[None, :] == query_index[:, None]
    return itself | (key_valid[None, :] == 1) & lineage & earlier


def softmax_parts(scores, allowed):
    capped = score_cap * jnp.tanh(scores / score_cap)
    held = jnp.where(allowed, capped, -1000000000.0)
    largest = jnp.max(held, axis=-1, keepdims=True)
    raised = jnp.where(allowed, jnp.exp(held - largest), 0.0)
    total_mass = jnp.sum(raised, axis=-1, keepdims=True)
    return (raised / total_mass, largest + jnp.log(total_mass))


def gated_gelu(gate_lin, up_lin):
    return jax.nn.gelu(gate_lin, approximate=True) * up_lin


def collect_attention(query_weight, key_weight, value_weight, output_weight):
    return (
        lax.all_gather(query_weight, "shard", axis=0, tiled=True),
        lax.all_gather(key_weight, "shard", axis=0, tiled=True),
        lax.all_gather(value_weight, "shard", axis=0, tiled=True),
        lax.all_gather(output_weight, "shard", axis=0, tiled=True),
    )


def group_rows(values):
    return lax.all_gather(values, "shard", axis=0, tiled=True)


def group_sums(values):
    return lax.psum_scatter(values, "shard", scatter_dimension=0, tiled=True)


def shards_generic(
    hidden_in,
    cotangent,
    token_segment,
    token_valid,
    segment_parent,
    query_weight,
    key_weight,
    value_weight,
    output_weight,
    gate_weight,
    up_weight,
    down_weight,
    attention_gain,
    attention_post_gain,
    feedforward_gain,
    feedforward_post_gain,
):
    row_count, model_width = hidden_in.shape
    group_size = HEADS // KV_HEADS
    row_start = lax.axis_index("shard") * row_count
    tree_size = token_segment.shape[0]
    position, parent_tok, grand_tok = tree_tables(token_segment, token_valid, segment_parent[0])
    key_index = jnp.arange(tree_size, dtype=jnp.int32)

    def own_rows(table):
        return lax.dynamic_slice_in_dim(table, row_start, row_count)

    allowed = allowed_mask(
        own_rows(key_index),
        own_rows(token_segment),
        own_rows(parent_tok),
        own_rows(grand_tok),
        key_index,
        token_segment,
        token_valid,
    )
    mask_full = allowed[None, None]
    cos_table, sin_table = rope_tables(own_rows(position), HEAD)
    query_scale = HEAD ** (-0.5)
    valid_rows = own_rows(token_valid).astype(jnp.float32)
    stream = hidden_in.astype(jnp.float32)
    query_all, key_all, value_all, output_all = collect_attention(
        query_weight, key_weight, value_weight, output_weight
    )
    normed_in = norm_rows(stream, attention_gain).astype(jnp.bfloat16)
    query_lin = jnp.einsum("td,qd->tq", normed_in, query_all, preferred_element_type=jnp.float32)
    key_lin = jnp.einsum("td,qd->tq", normed_in, key_all, preferred_element_type=jnp.float32)
    value_lin = jnp.einsum("td,qd->tq", normed_in, value_all, preferred_element_type=jnp.float32)
    queries = (
        rotate(query_lin.reshape(row_count, HEADS, HEAD), cos_table, sin_table) * query_scale
    ).astype(jnp.bfloat16)
    keys_own = (
        rotate(key_lin.reshape(row_count, KV_HEADS, HEAD), cos_table, sin_table)
        .astype(jnp.bfloat16)
        .reshape(row_count, KV_HEADS * HEAD)
    )
    values_own = value_lin.astype(jnp.bfloat16)
    key_tree, value_tree = (
        lax.all_gather(keys_own, "shard", axis=0, tiled=True),
        lax.all_gather(values_own, "shard", axis=0, tiled=True),
    )
    query_groups = queries.reshape(row_count, KV_HEADS, group_size, HEAD)
    key_groups = key_tree.reshape(tree_size, KV_HEADS, HEAD)
    value_groups = value_tree.reshape(tree_size, KV_HEADS, HEAD)
    scores = jnp.einsum(
        "qgrd,kgd->grqk", query_groups, key_groups, preferred_element_type=jnp.float32
    )
    probs, log_total = softmax_parts(scores, mask_full)
    attended = jnp.einsum(
        "grqk,kgd->qgrd",
        probs.astype(jnp.bfloat16),
        value_groups,
        preferred_element_type=jnp.float32,
    )
    attended = attended.astype(jnp.bfloat16).reshape(row_count, HEADS * HEAD)
    attention_pre = jnp.dot(attended, output_all, preferred_element_type=jnp.float32)
    attention_branch = norm_rows(attention_pre, attention_post_gain)
    middle = stream + attention_branch
    normed_mid = norm_rows(middle, feedforward_gain).astype(jnp.bfloat16)
    mid_tree = group_rows(normed_mid)
    gate_lin = jnp.einsum("td,fd->tf", mid_tree, gate_weight, preferred_element_type=jnp.float32)
    up_lin = jnp.einsum("td,fd->tf", mid_tree, up_weight, preferred_element_type=jnp.float32)
    hidden = gated_gelu(gate_lin, up_lin).astype(jnp.bfloat16)
    feedforward_pre = group_sums(jnp.dot(hidden, down_weight, preferred_element_type=jnp.float32))
    feedforward_branch = norm_rows(feedforward_pre, feedforward_post_gain)
    result = middle + feedforward_branch
    squares = jnp.stack(
        [
            jnp.sum(valid_rows[:, None] * summand * summand)
            for summand in (stream, attention_branch, feedforward_branch, result)
        ]
    )
    valid_total = jnp.sum(valid_rows) * model_width
    squares_all, valid_all = lax.psum((squares, valid_total), ("replica", "shard"))
    seed_grad = cotangent.astype(jnp.float32) * valid_rows[:, None]
    unused_four, pull_four = jax.vjp(norm_rows, feedforward_pre, feedforward_post_gain)
    ffpre_back, grad_four = pull_four(seed_grad)
    ffpre_low = ffpre_back.astype(jnp.bfloat16)
    ffpre_tree = group_rows(ffpre_low)
    hidden_back = jnp.einsum(
        "td,fd->tf", ffpre_tree, down_weight, preferred_element_type=jnp.float32
    ).astype(jnp.bfloat16)
    unused_glu, pull_glu = jax.vjp(gated_gelu, gate_lin, up_lin)
    gate_back, up_back = pull_glu(hidden_back.astype(jnp.float32))
    gate_back = gate_back.astype(jnp.bfloat16)
    up_back = up_back.astype(jnp.bfloat16)
    mid_terms = jnp.dot(gate_back, gate_weight, preferred_element_type=jnp.float32) + jnp.dot(
        up_back, up_weight, preferred_element_type=jnp.float32
    )
    mid_back = group_sums(mid_terms)
    gate_grad = jnp.einsum("tf,td->fd", gate_back, mid_tree, preferred_element_type=jnp.float32)
    up_grad = jnp.einsum("tf,td->fd", up_back, mid_tree, preferred_element_type=jnp.float32)
    down_grad = jnp.einsum("tf,td->fd", hidden, ffpre_tree, preferred_element_type=jnp.float32)
    unused_three, pull_three = jax.vjp(norm_rows, middle, feedforward_gain)
    middle_part, grad_three = pull_three(mid_back)
    middle_back = seed_grad + middle_part
    unused_two, pull_two = jax.vjp(norm_rows, attention_pre, attention_post_gain)
    attention_pre_back, grad_two = pull_two(middle_back)
    pre_low = attention_pre_back.astype(jnp.bfloat16)
    query_all, key_all, value_all, output_all = collect_attention(
        query_weight, key_weight, value_weight, output_weight
    )
    attended_back = jnp.einsum(
        "td,qd->tq", pre_low, output_all, preferred_element_type=jnp.float32
    ).astype(jnp.bfloat16)
    scores = jnp.einsum(
        "qgrd,kgd->grqk", query_groups, key_groups, preferred_element_type=jnp.float32
    )
    tanh_value = jnp.tanh(scores / score_cap)
    probs_back = jnp.where(
        mask_full,
        jnp.exp(jnp.where(mask_full, score_cap * tanh_value - log_total, -1000000000.0)),
        0.0,
    )
    back_groups = attended_back.reshape(row_count, KV_HEADS, group_size, HEAD)
    prob_grads = jnp.einsum(
        "qgrd,kgd->grqk", back_groups, value_groups, preferred_element_type=jnp.float32
    )
    inner_sum = jnp.sum(probs_back * prob_grads, axis=-1, keepdims=True)
    score_back = (probs_back * (prob_grads - inner_sum) * (1.0 - tanh_value * tanh_value)).astype(
        jnp.bfloat16
    )
    query_back = jnp.einsum(
        "grqk,kgd->qgrd", score_back, key_groups, preferred_element_type=jnp.float32
    ).reshape(row_count, HEADS, HEAD)
    key_back = jnp.einsum(
        "grqk,qgrd->kgd", score_back, query_groups, preferred_element_type=jnp.float32
    ).reshape(tree_size, KV_HEADS * HEAD)
    value_back = jnp.einsum(
        "grqk,qgrd->kgd",
        probs_back.astype(jnp.bfloat16),
        back_groups,
        preferred_element_type=jnp.float32,
    ).reshape(tree_size, KV_HEADS * HEAD)
    key_sum, value_sum = (
        lax.psum_scatter(key_back, "shard", scatter_dimension=0, tiled=True),
        lax.psum_scatter(value_back, "shard", scatter_dimension=0, tiled=True),
    )
    query_low = (
        rotate_back(query_back * query_scale, cos_table, sin_table)
        .astype(jnp.bfloat16)
        .reshape(row_count, HEADS * HEAD)
    )
    key_low = (
        rotate_back(key_sum.reshape(row_count, KV_HEADS, HEAD), cos_table, sin_table)
        .astype(jnp.bfloat16)
        .reshape(row_count, KV_HEADS * HEAD)
    )
    value_low = value_sum.astype(jnp.bfloat16)
    normed_back = (
        jnp.dot(query_low, query_all, preferred_element_type=jnp.float32)
        + jnp.dot(key_low, key_all, preferred_element_type=jnp.float32)
        + jnp.dot(value_low, value_all, preferred_element_type=jnp.float32)
    )
    output_local = jnp.einsum("tq,td->qd", attended, pre_low, preferred_element_type=jnp.float32)
    query_local = jnp.einsum("tq,td->qd", query_low, normed_in, preferred_element_type=jnp.float32)
    key_local = jnp.einsum("tq,td->qd", key_low, normed_in, preferred_element_type=jnp.float32)
    value_local = jnp.einsum("tq,td->qd", value_low, normed_in, preferred_element_type=jnp.float32)
    query_part, key_part, value_part, output_part = (
        lax.psum_scatter(query_local, "shard", scatter_dimension=0, tiled=True),
        lax.psum_scatter(key_local, "shard", scatter_dimension=0, tiled=True),
        lax.psum_scatter(value_local, "shard", scatter_dimension=0, tiled=True),
        lax.psum_scatter(output_local, "shard", scatter_dimension=0, tiled=True),
    )
    unused_one, pull_one = jax.vjp(norm_rows, stream, attention_gain)
    stream_part, grad_one = pull_one(normed_back)
    input_grad = middle_back + stream_part
    query_sum, key_total, value_total, output_sum, gate_sum, up_sum, down_sum = lax.psum(
        (query_part, key_part, value_part, output_part, gate_grad, up_grad, down_grad), "replica"
    )
    gain_one, gain_two, gain_three, gain_four = lax.psum(
        (grad_one, grad_two, grad_three, grad_four), ("replica", "shard")
    )
    stream_rms = jnp.sqrt(squares_all / valid_all)
    return (
        result.astype(jnp.bfloat16),
        input_grad,
        query_sum,
        key_total,
        value_total,
        output_sum,
        gate_sum,
        up_sum,
        down_sum,
        gain_one,
        gain_two,
        gain_three,
        gain_four,
        stream_rms,
    )


def norm_factor(stream):
    return lax.rsqrt(jnp.mean(stream * stream, axis=-1, keepdims=True) + norm_eps)


def norm_back(stream, norm_gain, gradient):
    factor = norm_factor(stream)
    weighted = gradient * (1.0 + norm_gain)
    inner = jnp.mean(weighted * stream, axis=-1, keepdims=True)
    back = factor * weighted - stream * (factor * factor * factor * inner)
    gain_back = jnp.sum(gradient * stream * factor, axis=0)
    return back, gain_back


def dot_nt(left, right):
    return lax.dot_general(
        left, right, (((1,), (1,)), ((), ())), preferred_element_type=jnp.float32
    )


def dot_nn(left, right):
    return lax.dot_general(
        left, right, (((1,), (0,)), ((), ())), preferred_element_type=jnp.float32
    )


def dot_tn(left, right):
    return lax.dot_general(
        left, right, (((0,), (0,)), ((), ())), preferred_element_type=jnp.float32
    )


def sum_low(values):
    return lax.psum_scatter(
        values.astype(jnp.bfloat16), "shard", scatter_dimension=0, tiled=True
    ).astype(jnp.float32)


def gelu_parts(gate_lin):
    root = math.sqrt(2.0 / math.pi)
    square = gate_lin * gate_lin
    tanh_value = jnp.tanh(root * gate_lin * (1.0 + 0.044715 * square))
    half_up = 0.5 * (1.0 + tanh_value)
    slope = half_up + 0.5 * gate_lin * (1.0 - tanh_value * tanh_value) * root * (
        1.0 + 3.0 * 0.044715 * square
    )
    return gate_lin * half_up, slope


def shards_heads(
    hidden_in,
    cotangent,
    token_segment,
    token_valid,
    segment_parent,
    query_weight,
    key_weight,
    value_weight,
    output_weight,
    gate_weight,
    up_weight,
    down_weight,
    attention_gain,
    attention_post_gain,
    feedforward_gain,
    feedforward_post_gain,
):
    low = jnp.bfloat16
    row_count, model_width = hidden_in.shape
    shard_count = lax.axis_size("shard")
    tree_count = lax.axis_size("replica")
    shard = lax.axis_index("shard")
    row_start = shard * row_count
    tree_size = token_segment.shape[0]
    position, parent_tok, grand_tok = tree_tables(token_segment, token_valid, segment_parent[0])
    key_index = jnp.arange(tree_size, dtype=jnp.int32)
    allowed = allowed_mask(
        key_index, token_segment, parent_tok, grand_tok, key_index, token_segment, token_valid
    )
    cos_table, sin_table = rope_tables(position, HEAD)
    cos_table, sin_table = cos_table[:, 0], sin_table[:, 0]
    query_scale = HEAD ** (-0.5)
    valid_rows = lax.dynamic_slice_in_dim(token_valid, row_start, row_count).astype(jnp.float32)
    stream = hidden_in.astype(jnp.float32)
    second_core = lax.rem(shard, 2) == 1
    pairs = [(i, i ^ 1) for i in range(shard_count)]

    def both_halves(own):
        other = lax.ppermute(own, "shard", pairs)
        return jnp.where(
            second_core, jnp.concatenate([other, own]), jnp.concatenate([own, other])
        )

    key_head = both_halves(key_weight)
    value_head = both_halves(value_weight)
    normed_in = group_rows(norm_rows(stream, attention_gain).astype(low))
    queries = (
        rotate(dot_nt(normed_in, query_weight), cos_table, sin_table) * query_scale
    ).astype(low)
    keys = rotate(dot_nt(normed_in, key_head), cos_table, sin_table).astype(low)
    values = dot_nt(normed_in, value_head).astype(low)
    tanh_value = jnp.tanh(dot_nt(queries, keys) / score_cap)
    raised = jnp.where(allowed, jnp.exp(score_cap * tanh_value), 0.0)
    scale = 1.0 / jnp.sum(raised, axis=-1, keepdims=True)
    attended = dot_nn((raised * scale).astype(low), values).astype(low)
    attention_pre = sum_low(dot_nn(attended, output_weight))
    attention_branch = norm_rows(attention_pre, attention_post_gain)
    middle = stream + attention_branch
    normed_mid = norm_rows(middle, feedforward_gain).astype(low)
    mid_tree = group_rows(normed_mid)
    gate_lin = dot_nt(mid_tree, gate_weight)
    up_lin = dot_nt(mid_tree, up_weight)
    gelu_value, gelu_slope = gelu_parts(gate_lin)
    hidden = (gelu_value * up_lin).astype(low)
    feedforward_pre = sum_low(dot_nn(hidden, down_weight))
    feedforward_branch = norm_rows(feedforward_pre, feedforward_post_gain)
    result = middle + feedforward_branch
    squares = jnp.stack(
        [
            jnp.sum(valid_rows[:, None] * summand * summand)
            for summand in (stream, attention_branch, feedforward_branch, result)
        ]
    )
    valid_total = jnp.sum(valid_rows) * model_width
    seed_grad = cotangent.astype(jnp.float32) * valid_rows[:, None]
    ffpre_back, grad_four = norm_back(feedforward_pre, feedforward_post_gain, seed_grad)
    ffpre_low = ffpre_back.astype(low)
    ffpre_tree = group_rows(ffpre_low)
    mid_every = lax.all_gather(normed_mid, ("replica", "shard"), axis=0, tiled=True)
    ffpre_every = lax.all_gather(ffpre_low, ("replica", "shard"), axis=0, tiled=True)

    def hidden_grads(gate_lin, up_lin, gelu_value, gelu_slope, ffpre_rows):
        hidden_back = dot_nt(ffpre_rows, down_weight).astype(low).astype(jnp.float32)
        gate_back = (hidden_back * up_lin * gelu_slope).astype(low)
        up_back = (hidden_back * gelu_value).astype(low)
        return gate_back, up_back

    gate_back, up_back = hidden_grads(gate_lin, up_lin, gelu_value, gelu_slope, ffpre_tree)
    mid_back = sum_low(dot_nn(gate_back, gate_weight) + dot_nn(up_back, up_weight))
    middle_part, grad_three = norm_back(middle, feedforward_gain, mid_back)
    middle_back = seed_grad + middle_part
    attention_pre_back, grad_two = norm_back(attention_pre, attention_post_gain, middle_back)
    pre_tree = group_rows(attention_pre_back.astype(low))
    attended_back = dot_nt(pre_tree, output_weight).astype(low)
    probs_back = raised * scale
    prob_grads = dot_nt(attended_back, values)
    inner_sum = jnp.sum(probs_back * prob_grads, axis=-1, keepdims=True)
    score_back = (probs_back * (prob_grads - inner_sum) * (1.0 - tanh_value * tanh_value)).astype(
        low
    )
    query_back = dot_nn(score_back, keys)
    key_back = dot_tn(score_back, queries)
    value_back = dot_tn(probs_back.astype(low), attended_back)
    key_back, value_back = (
        key_back + lax.ppermute(key_back, "shard", pairs),
        value_back + lax.ppermute(value_back, "shard", pairs),
    )
    query_low = rotate_back(query_back * query_scale, cos_table, sin_table).astype(low)
    key_low = rotate_back(key_back, cos_table, sin_table).astype(low)
    value_low = value_back.astype(low)
    half = HEAD // 2
    key_low = jnp.where(second_core, key_low[:, half:], key_low[:, :half])
    value_low = jnp.where(second_core, value_low[:, half:], value_low[:, :half])
    normed_back = sum_low(
        dot_nn(query_low, query_weight) + dot_nn(key_low, key_weight) + dot_nn(value_low, value_weight)
    )
    stream_part, grad_one = norm_back(stream, attention_gain, normed_back)
    input_grad = middle_back + stream_part
    attention_grads = jnp.concatenate(
        [
            dot_tn(query_low, normed_in),
            dot_tn(key_low, normed_in),
            dot_tn(value_low, normed_in),
            dot_tn(attended, pre_tree),
        ]
    ).astype(low)
    attention_grads = lax.psum(attention_grads, "replica").astype(jnp.float32)
    sizes = [query_weight.shape[0], key_weight.shape[0], value_weight.shape[0]]
    query_sum, key_sum, value_sum, output_sum = jnp.split(
        attention_grads, [sizes[0], sizes[0] + sizes[1], sum(sizes)]
    )
    gate_sum = dot_tn(gate_back, mid_tree)
    up_sum = dot_tn(up_back, mid_tree)
    down_sum = dot_tn(hidden, ffpre_tree)
    for step in range(1, tree_count):
        tree = lax.rem(lax.axis_index("replica") + step, tree_count)
        mid_rows = lax.dynamic_slice_in_dim(mid_every, tree * tree_size, tree_size)
        ffpre_rows = lax.dynamic_slice_in_dim(ffpre_every, tree * tree_size, tree_size)
        gate_lin = dot_nt(mid_rows, gate_weight)
        up_lin = dot_nt(mid_rows, up_weight)
        gelu_value, gelu_slope = gelu_parts(gate_lin)
        hidden = (gelu_value * up_lin).astype(low)
        gate_back, up_back = hidden_grads(gate_lin, up_lin, gelu_value, gelu_slope, ffpre_rows)
        gate_sum += dot_tn(gate_back, mid_rows)
        up_sum += dot_tn(up_back, mid_rows)
        down_sum += dot_tn(hidden, ffpre_rows)
    gain_one, gain_two, gain_three, gain_four, squares_all, valid_all = lax.psum(
        (grad_one, grad_two, grad_three, grad_four, squares, valid_total), ("replica", "shard")
    )
    stream_rms = jnp.sqrt(squares_all / valid_all)
    return (
        result.astype(low),
        input_grad,
        query_sum,
        key_sum,
        value_sum,
        output_sum,
        gate_sum,
        up_sum,
        down_sum,
        gain_one,
        gain_two,
        gain_three,
        gain_four,
        stream_rms,
    )


def solution(mesh):
    heads_fit = mesh.shape["shard"] == HEADS
    return jax.shard_map(
        shards_heads if heads_fit else shards_generic,
        mesh=mesh,
        in_specs=(
            P(("replica", "shard"), None),
            P(("replica", "shard"), None),
            P("replica"),
            P("replica"),
            P("replica", None),
            P("shard", None),
            P("shard", None),
            P("shard", None),
            P("shard", None),
            P("shard", None),
            P("shard", None),
            P("shard", None),
            P(),
            P(),
            P(),
            P(),
        ),
        out_specs=(
            P(("replica", "shard"), None),
            P(("replica", "shard"), None),
            P("shard", None),
            P("shard", None),
            P("shard", None),
            P("shard", None),
            P("shard", None),
            P("shard", None),
            P("shard", None),
            P(),
            P(),
            P(),
            P(),
            P(),
        ),
        check_vma=False,
    )
```

```python
import functools
import math

import jax
import jax.numpy as jnp
from jax import lax
from jax.experimental import pallas as pl
from jax.experimental.pallas import tpu as pltpu
from jax.sharding import PartitionSpec as P

HEADS = 8
KV_HEADS = 4
HEAD = 256


norm_eps = 1e-06
score_cap = 50.0


def norm_rows(stream, norm_gain):
    factor = lax.rsqrt(jnp.mean(stream * stream, axis=-1, keepdims=True) + norm_eps)
    return stream * factor * (1.0 + norm_gain)


def rotate(values, cos_table, sin_table):
    half_width = values.shape[-1] // 2
    turned = jnp.concatenate([-values[..., half_width:], values[..., :half_width]], axis=-1)
    return values * cos_table + turned * sin_table


def rotate_back(gradient, cos_table, sin_table):
    half_width = gradient.shape[-1] // 2
    shifted = gradient * sin_table
    unturned = jnp.concatenate([shifted[..., half_width:], -shifted[..., :half_width]], axis=-1)
    return gradient * cos_table + unturned


def rope_tables(position, head_size):
    half_width = head_size // 2
    frequency = jnp.power(10000.0, -jnp.arange(half_width, dtype=jnp.float32) * 2.0 / head_size)
    angles = position.astype(jnp.float32)[:, None] * frequency[None, :]
    angles = jnp.concatenate([angles, angles], axis=-1)[:, None, :]
    return (jnp.cos(angles), jnp.sin(angles))


def tree_tables(segment, valid_mask, parent):
    labels = jnp.arange(parent.shape[0], dtype=jnp.int32)
    member = (segment[:, None] == labels[None, :]).astype(jnp.int32)
    lengths = jnp.sum(member * valid_mask[:, None], axis=0)
    starts = jnp.sum((segment[:, None] < labels[None, :]).astype(jnp.int32), axis=0)
    parent_of = (parent[:, None] == labels[None, :]).astype(jnp.int32)
    grandparent = jnp.sum(parent_of * parent[None, :], axis=1)
    parent_len = jnp.sum(parent_of * lengths[None, :], axis=1)
    grand_of = (grandparent[:, None] == labels[None, :]).astype(jnp.int32)
    grand_len = jnp.sum(grand_of * lengths[None, :], axis=1)
    offsets = jnp.where(parent != labels, parent_len, 0) + jnp.where(
        grandparent != parent, grand_len, 0
    )
    token_index = jnp.arange(segment.shape[0], dtype=jnp.int32)
    position = jnp.sum(member * (offsets - starts)[None, :], axis=1) + token_index
    parent_tok = jnp.sum(member * parent[None, :], axis=1)
    grand_tok = jnp.sum(member * grandparent[None, :], axis=1)
    return (position, parent_tok, grand_tok)


def allowed_mask(query_index, query_seg, query_parent, query_grand, key_index, key_seg, key_valid):
    lineage = (
        (key_seg[None, :] == query_seg[:, None])
        | (key_seg[None, :] == query_parent[:, None])
        | (key_seg[None, :] == query_grand[:, None])
    )
    earlier = (key_seg[None, :] != query_seg[:, None]) | (key_index[None, :] < query_index[:, None])
    itself = key_index[None, :] == query_index[:, None]
    return itself | (key_valid[None, :] == 1) & lineage & earlier


def softmax_parts(scores, allowed):
    capped = score_cap * jnp.tanh(scores / score_cap)
    held = jnp.where(allowed, capped, -1000000000.0)
    largest = jnp.max(held, axis=-1, keepdims=True)
    raised = jnp.where(allowed, jnp.exp(held - largest), 0.0)
    total_mass = jnp.sum(raised, axis=-1, keepdims=True)
    return (raised / total_mass, largest + jnp.log(total_mass))


def gated_gelu(gate_lin, up_lin):
    return jax.nn.gelu(gate_lin, approximate=True) * up_lin


def collect_attention(query_weight, key_weight, value_weight, output_weight):
    return (
        lax.all_gather(query_weight, "shard", axis=0, tiled=True),
        lax.all_gather(key_weight, "shard", axis=0, tiled=True),
        lax.all_gather(value_weight, "shard", axis=0, tiled=True),
        lax.all_gather(output_weight, "shard", axis=0, tiled=True),
    )


def group_rows(values):
    return lax.all_gather(values, "shard", axis=0, tiled=True)


def group_sums(values):
    return lax.psum_scatter(values, "shard", scatter_dimension=0, tiled=True)


def shards_generic(
    hidden_in,
    cotangent,
    token_segment,
    token_valid,
    segment_parent,
    query_weight,
    key_weight,
    value_weight,
    output_weight,
    gate_weight,
    up_weight,
    down_weight,
    attention_gain,
    attention_post_gain,
    feedforward_gain,
    feedforward_post_gain,
):
    row_count, model_width = hidden_in.shape
    group_size = HEADS // KV_HEADS
    row_start = lax.axis_index("shard") * row_count
    tree_size = token_segment.shape[0]
    position, parent_tok, grand_tok = tree_tables(token_segment, token_valid, segment_parent[0])
    key_index = jnp.arange(tree_size, dtype=jnp.int32)

    def own_rows(table):
        return lax.dynamic_slice_in_dim(table, row_start, row_count)

    allowed = allowed_mask(
        own_rows(key_index),
        own_rows(token_segment),
        own_rows(parent_tok),
        own_rows(grand_tok),
        key_index,
        token_segment,
        token_valid,
    )
    mask_full = allowed[None, None]
    cos_table, sin_table = rope_tables(own_rows(position), HEAD)
    query_scale = HEAD ** (-0.5)
    valid_rows = own_rows(token_valid).astype(jnp.float32)
    stream = hidden_in.astype(jnp.float32)
    query_all, key_all, value_all, output_all = collect_attention(
        query_weight, key_weight, value_weight, output_weight
    )
    normed_in = norm_rows(stream, attention_gain).astype(jnp.bfloat16)
    query_lin = jnp.einsum("td,qd->tq", normed_in, query_all, preferred_element_type=jnp.float32)
    key_lin = jnp.einsum("td,qd->tq", normed_in, key_all, preferred_element_type=jnp.float32)
    value_lin = jnp.einsum("td,qd->tq", normed_in, value_all, preferred_element_type=jnp.float32)
    queries = (
        rotate(query_lin.reshape(row_count, HEADS, HEAD), cos_table, sin_table) * query_scale
    ).astype(jnp.bfloat16)
    keys_own = (
        rotate(key_lin.reshape(row_count, KV_HEADS, HEAD), cos_table, sin_table)
        .astype(jnp.bfloat16)
        .reshape(row_count, KV_HEADS * HEAD)
    )
    values_own = value_lin.astype(jnp.bfloat16)
    key_tree, value_tree = (
        lax.all_gather(keys_own, "shard", axis=0, tiled=True),
        lax.all_gather(values_own, "shard", axis=0, tiled=True),
    )
    query_groups = queries.reshape(row_count, KV_HEADS, group_size, HEAD)
    key_groups = key_tree.reshape(tree_size, KV_HEADS, HEAD)
    value_groups = value_tree.reshape(tree_size, KV_HEADS, HEAD)
    scores = jnp.einsum(
        "qgrd,kgd->grqk", query_groups, key_groups, preferred_element_type=jnp.float32
    )
    probs, log_total = softmax_parts(scores, mask_full)
    attended = jnp.einsum(
        "grqk,kgd->qgrd",
        probs.astype(jnp.bfloat16),
        value_groups,
        preferred_element_type=jnp.float32,
    )
    attended = attended.astype(jnp.bfloat16).reshape(row_count, HEADS * HEAD)
    attention_pre = jnp.dot(attended, output_all, preferred_element_type=jnp.float32)
    attention_branch = norm_rows(attention_pre, attention_post_gain)
    middle = stream + attention_branch
    normed_mid = norm_rows(middle, feedforward_gain).astype(jnp.bfloat16)
    mid_tree = group_rows(normed_mid)
    gate_lin = jnp.einsum("td,fd->tf", mid_tree, gate_weight, preferred_element_type=jnp.float32)
    up_lin = jnp.einsum("td,fd->tf", mid_tree, up_weight, preferred_element_type=jnp.float32)
    hidden = gated_gelu(gate_lin, up_lin).astype(jnp.bfloat16)
    feedforward_pre = group_sums(jnp.dot(hidden, down_weight, preferred_element_type=jnp.float32))
    feedforward_branch = norm_rows(feedforward_pre, feedforward_post_gain)
    result = middle + feedforward_branch
    squares = jnp.stack(
        [
            jnp.sum(valid_rows[:, None] * summand * summand)
            for summand in (stream, attention_branch, feedforward_branch, result)
        ]
    )
    valid_total = jnp.sum(valid_rows) * model_width
    squares_all, valid_all = lax.psum((squares, valid_total), ("replica", "shard"))
    seed_grad = cotangent.astype(jnp.float32) * valid_rows[:, None]
    unused_four, pull_four = jax.vjp(norm_rows, feedforward_pre, feedforward_post_gain)
    ffpre_back, grad_four = pull_four(seed_grad)
    ffpre_low = ffpre_back.astype(jnp.bfloat16)
    ffpre_tree = group_rows(ffpre_low)
    hidden_back = jnp.einsum(
        "td,fd->tf", ffpre_tree, down_weight, preferred_element_type=jnp.float32
    ).astype(jnp.bfloat16)
    unused_glu, pull_glu = jax.vjp(gated_gelu, gate_lin, up_lin)
    gate_back, up_back = pull_glu(hidden_back.astype(jnp.float32))
    gate_back = gate_back.astype(jnp.bfloat16)
    up_back = up_back.astype(jnp.bfloat16)
    mid_terms = jnp.dot(gate_back, gate_weight, preferred_element_type=jnp.float32) + jnp.dot(
        up_back, up_weight, preferred_element_type=jnp.float32
    )
    mid_back = group_sums(mid_terms)
    gate_grad = jnp.einsum("tf,td->fd", gate_back, mid_tree, preferred_element_type=jnp.float32)
    up_grad = jnp.einsum("tf,td->fd", up_back, mid_tree, preferred_element_type=jnp.float32)
    down_grad = jnp.einsum("tf,td->fd", hidden, ffpre_tree, preferred_element_type=jnp.float32)
    unused_three, pull_three = jax.vjp(norm_rows, middle, feedforward_gain)
    middle_part, grad_three = pull_three(mid_back)
    middle_back = seed_grad + middle_part
    unused_two, pull_two = jax.vjp(norm_rows, attention_pre, attention_post_gain)
    attention_pre_back, grad_two = pull_two(middle_back)
    pre_low = attention_pre_back.astype(jnp.bfloat16)
    query_all, key_all, value_all, output_all = collect_attention(
        query_weight, key_weight, value_weight, output_weight
    )
    attended_back = jnp.einsum(
        "td,qd->tq", pre_low, output_all, preferred_element_type=jnp.float32
    ).astype(jnp.bfloat16)
    scores = jnp.einsum(
        "qgrd,kgd->grqk", query_groups, key_groups, preferred_element_type=jnp.float32
    )
    tanh_value = jnp.tanh(scores / score_cap)
    probs_back = jnp.where(
        mask_full,
        jnp.exp(jnp.where(mask_full, score_cap * tanh_value - log_total, -1000000000.0)),
        0.0,
    )
    back_groups = attended_back.reshape(row_count, KV_HEADS, group_size, HEAD)
    prob_grads = jnp.einsum(
        "qgrd,kgd->grqk", back_groups, value_groups, preferred_element_type=jnp.float32
    )
    inner_sum = jnp.sum(probs_back * prob_grads, axis=-1, keepdims=True)
    score_back = (probs_back * (prob_grads - inner_sum) * (1.0 - tanh_value * tanh_value)).astype(
        jnp.bfloat16
    )
    query_back = jnp.einsum(
        "grqk,kgd->qgrd", score_back, key_groups, preferred_element_type=jnp.float32
    ).reshape(row_count, HEADS, HEAD)
    key_back = jnp.einsum(
        "grqk,qgrd->kgd", score_back, query_groups, preferred_element_type=jnp.float32
    ).reshape(tree_size, KV_HEADS * HEAD)
    value_back = jnp.einsum(
        "grqk,qgrd->kgd",
        probs_back.astype(jnp.bfloat16),
        back_groups,
        preferred_element_type=jnp.float32,
    ).reshape(tree_size, KV_HEADS * HEAD)
    key_sum, value_sum = (
        lax.psum_scatter(key_back, "shard", scatter_dimension=0, tiled=True),
        lax.psum_scatter(value_back, "shard", scatter_dimension=0, tiled=True),
    )
    query_low = (
        rotate_back(query_back * query_scale, cos_table, sin_table)
        .astype(jnp.bfloat16)
        .reshape(row_count, HEADS * HEAD)
    )
    key_low = (
        rotate_back(key_sum.reshape(row_count, KV_HEADS, HEAD), cos_table, sin_table)
        .astype(jnp.bfloat16)
        .reshape(row_count, KV_HEADS * HEAD)
    )
    value_low = value_sum.astype(jnp.bfloat16)
    normed_back = (
        jnp.dot(query_low, query_all, preferred_element_type=jnp.float32)
        + jnp.dot(key_low, key_all, preferred_element_type=jnp.float32)
        + jnp.dot(value_low, value_all, preferred_element_type=jnp.float32)
    )
    output_local = jnp.einsum("tq,td->qd", attended, pre_low, preferred_element_type=jnp.float32)
    query_local = jnp.einsum("tq,td->qd", query_low, normed_in, preferred_element_type=jnp.float32)
    key_local = jnp.einsum("tq,td->qd", key_low, normed_in, preferred_element_type=jnp.float32)
    value_local = jnp.einsum("tq,td->qd", value_low, normed_in, preferred_element_type=jnp.float32)
    query_part, key_part, value_part, output_part = (
        lax.psum_scatter(query_local, "shard", scatter_dimension=0, tiled=True),
        lax.psum_scatter(key_local, "shard", scatter_dimension=0, tiled=True),
        lax.psum_scatter(value_local, "shard", scatter_dimension=0, tiled=True),
        lax.psum_scatter(output_local, "shard", scatter_dimension=0, tiled=True),
    )
    unused_one, pull_one = jax.vjp(norm_rows, stream, attention_gain)
    stream_part, grad_one = pull_one(normed_back)
    input_grad = middle_back + stream_part
    query_sum, key_total, value_total, output_sum, gate_sum, up_sum, down_sum = lax.psum(
        (query_part, key_part, value_part, output_part, gate_grad, up_grad, down_grad), "replica"
    )
    gain_one, gain_two, gain_three, gain_four = lax.psum(
        (grad_one, grad_two, grad_three, grad_four), ("replica", "shard")
    )
    stream_rms = jnp.sqrt(squares_all / valid_all)
    return (
        result.astype(jnp.bfloat16),
        input_grad,
        query_sum,
        key_total,
        value_total,
        output_sum,
        gate_sum,
        up_sum,
        down_sum,
        gain_one,
        gain_two,
        gain_three,
        gain_four,
        stream_rms,
    )


def norm_factor(stream):
    return lax.rsqrt(jnp.mean(stream * stream, axis=-1, keepdims=True) + norm_eps)


def norm_back(stream, norm_gain, gradient):
    factor = norm_factor(stream)
    weighted = gradient * (1.0 + norm_gain)
    inner = jnp.mean(weighted * stream, axis=-1, keepdims=True)
    back = factor * weighted - stream * (factor * factor * factor * inner)
    gain_back = jnp.sum(gradient * stream * factor, axis=0)
    return back, gain_back


def dot_nt(left, right):
    return lax.dot_general(
        left, right, (((1,), (1,)), ((), ())), preferred_element_type=jnp.float32
    )


def dot_nn(left, right):
    return lax.dot_general(
        left, right, (((1,), (0,)), ((), ())), preferred_element_type=jnp.float32
    )


def dot_tn(left, right):
    return lax.dot_general(
        left, right, (((0,), (0,)), ((), ())), preferred_element_type=jnp.float32
    )


def sum_low(values):
    return lax.psum_scatter(
        values.astype(jnp.bfloat16), "shard", scatter_dimension=0, tiled=True
    ).astype(jnp.float32)


def gelu_parts(gate_lin):
    root = math.sqrt(2.0 / math.pi)
    square = gate_lin * gate_lin
    tanh_value = jnp.tanh(root * gate_lin * (1.0 + 0.044715 * square))
    half_up = 0.5 * (1.0 + tanh_value)
    slope = half_up + 0.5 * gate_lin * (1.0 - tanh_value * tanh_value) * root * (
        1.0 + 3.0 * 0.044715 * square
    )
    return gate_lin * half_up, slope


MESH_ID = pl.DeviceIdType.MESH
VMEM_BYTES = 62 * 2**20
ROOT = math.sqrt(2.0 / math.pi)


class Plane:
    def __init__(self):
        self.me = lax.axis_index("shard")
        core = lax.rem(self.me, 2)
        x = lax.rem(lax.div(self.me, 2), 2)
        y = lax.div(self.me, 4)
        self.core = core
        self.own_chip = 2 * y + x
        self.x_chip = 2 * y + 1 - x
        self.y_chip = 2 * (1 - y) + x
        self.diag_chip = 2 * (1 - y) + 1 - x
        self.mate = self.me + 1 - 2 * core
        self.x_dev = 2 * self.x_chip + core
        self.y_dev = 2 * self.y_chip + core
        self.diag_dev = 2 * self.diag_chip + core

    def near(self):
        return [{"shard": dev} for dev in (self.mate, self.x_dev, self.y_dev)]


class Wires:
    def __init__(self, send_sem, recv_sem):
        self.send_sem, self.recv_sem = send_sem, recv_sem
        self.sent = []

    def send(self, source, target, device):
        at = len(self.sent)
        copy = pltpu.make_async_remote_copy(
            src_ref=source,
            dst_ref=target,
            send_sem=self.send_sem.at[at],
            recv_sem=self.recv_sem.at[at],
            device_id=device if isinstance(device, dict) else {"shard": device},
            device_id_type=MESH_ID,
        )
        copy.start()
        self.sent.append(copy)
        return copy

    def finish(self):
        for copy in self.sent:
            copy.wait_send()


def greet(devices):
    barrier = pltpu.get_barrier_semaphore()
    for device in devices:
        pl.semaphore_signal(barrier, inc=1, device_id=device, device_id_type=MESH_ID)
    pl.semaphore_wait(barrier, len(devices))


def block_rows(ref, start, size, step=16):
    return ref.at[pl.ds(pl.multiple_of(start, step), size)]


def by_rows(count, body, size=32):
    def step(at, carry):
        body(pl.ds(pl.multiple_of(at * size, size), size))
        return carry

    lax.fori_loop(0, count // size, step, 0)


def column_tile(width):
    return max(t for t in range(128, 769, 128) if width % t == 0)


def by_columns(width, body):
    tile = column_tile(width)

    def step(at, carry):
        body(pl.ds(pl.multiple_of(at * tile, 128), tile))
        return carry

    lax.fori_loop(0, width // tile, step, 0)


def gather_tree(wires, plane, own, tree, rows, use):
    half = rows // 2

    def part(dev, start, size):
        return block_rows(tree, dev * rows + start, size)

    def own_part(start, size):
        return own.at[pl.ds(start, size)]

    me, mate = plane.me, plane.mate
    first_x = wires.send(own_part(0, half), part(me, 0, half), plane.x_dev)
    first_y = wires.send(own_part(half, half), part(me, half, half), plane.y_dev)
    to_mate = wires.send(own_part(0, rows), part(me, 0, rows), mate)
    rest_x = wires.send(own_part(half, half), part(me, half, half), plane.x_dev)
    rest_y = wires.send(own_part(0, half), part(me, 0, half), plane.y_dev)
    to_mate.wait_recv()
    use(plane.own_chip)
    first_x.wait_recv()
    turn_y = wires.send(part(plane.x_dev, 0, half), part(plane.x_dev, 0, half), plane.y_dev)
    first_y.wait_recv()
    turn_x = wires.send(part(plane.y_dev, half, half), part(plane.y_dev, half, half), plane.x_dev)
    rest_x.wait_recv()
    mate_x = wires.send(part(plane.x_dev, 0, rows), part(plane.x_dev, 0, rows), mate)
    rest_y.wait_recv()
    mate_y = wires.send(part(plane.y_dev, 0, rows), part(plane.y_dev, 0, rows), mate)
    mate_x.wait_recv()
    use(plane.x_chip)
    turn_y.wait_recv()
    turn_x.wait_recv()
    mate_diag = wires.send(part(plane.diag_dev, 0, rows), part(plane.diag_dev, 0, rows), mate)
    mate_y.wait_recv()
    use(plane.y_chip)
    mate_diag.wait_recv()
    use(plane.diag_chip)


GATHER_COPIES = 10


def scatter_scratch(rows, width):
    half = rows // 2
    low = jnp.bfloat16
    return [
        pltpu.VMEM((3, rows, width), jnp.float32),
        pltpu.VMEM((2 * rows, column_tile(width)), jnp.float32),
        pltpu.VMEM((2, rows, width), low),
        pltpu.VMEM((4, rows, width), low),
        pltpu.VMEM((3, half, width), low),
        pltpu.VMEM((3, half, width), low),
        pltpu.VMEM((3, half, width), low),
        pltpu.VMEM((3, half, width), low),
    ]


def scatter_sum(wires, plane, scratch, product, total):
    sums, piece, mate_out, mate_in, x_out, x_in, y_out, y_in = scratch
    rows, width = total.shape
    half = rows // 2
    low, full = jnp.bfloat16, jnp.float32

    def produce(slot, out_slot, in_slot, chip):
        def tile(columns):
            piece[...] = product(chip, columns)
            sums[slot, :, columns] = piece[block_at(plane.core * rows, rows), :]
            mate_out[out_slot, :, columns] = piece[
                block_at((1 - plane.core) * rows, rows), :
            ].astype(low)

        by_columns(width, tile)
        return wires.send(mate_out.at[out_slot], mate_in.at[in_slot], plane.mate)

    def low_part(out, out_slot, slot, in_slot, start, more=None):
        def step(at):
            there = pl.ds(pl.multiple_of(start + at.start, 16), at.size)
            value = sums[slot, there, :] + mate_in[in_slot, there, :].astype(full)
            if more is not None:
                value += more[0, at, :].astype(full)
            out[out_slot, at, :] = value.astype(low)

        by_rows(half, step)

    diag = produce(0, 0, 0, plane.diag_chip)
    to_x = produce(1, 1, 1, plane.x_chip)
    diag.wait_recv()
    low_part(x_out, 0, 0, 0, 0)
    x_first = wires.send(x_out.at[0], x_in.at[0], plane.x_dev)
    low_part(y_out, 0, 0, 0, half)
    y_first = wires.send(y_out.at[0], y_in.at[0], plane.y_dev)
    diag.wait_send()
    to_y = produce(2, 0, 2, plane.y_chip)
    to_x.wait_recv()
    low_part(x_out, 1, 1, 1, 0)
    x_next = wires.send(x_out.at[1], x_in.at[1], plane.x_dev)
    to_x.wait_send()
    to_own = produce(0, 1, 3, plane.own_chip)
    to_y.wait_recv()
    low_part(y_out, 1, 2, 2, half)
    y_next = wires.send(y_out.at[1], y_in.at[1], plane.y_dev)
    y_first.wait_recv()
    low_part(x_out, 2, 1, 1, half, y_in)
    x_last = wires.send(x_out.at[2], x_in.at[2], plane.x_dev)
    x_first.wait_recv()
    low_part(y_out, 2, 2, 2, 0, x_in)
    y_last = wires.send(y_out.at[2], y_in.at[2], plane.y_dev)
    to_own.wait_recv()
    for copy in (x_next, y_next, x_last, y_last):
        copy.wait_recv()
    for start, x_slot, y_slot in ((0, 1, 2), (half, 2, 1)):

        def step(at, start=start, x_slot=x_slot, y_slot=y_slot):
            there = pl.ds(pl.multiple_of(start + at.start, 16), at.size)
            total[there, :] = (
                sums[0, there, :]
                + mate_in[3, there, :].astype(full)
                + x_in[x_slot, at, :].astype(full)
                + y_in[y_slot, at, :].astype(full)
            )

        by_rows(half, step)
    for copy in (to_y, to_own, x_first, x_next, x_last, y_first, y_next, y_last):
        copy.wait_send()


SCATTER_COPIES = 10


def block_at(start, size):
    return pl.ds(pl.multiple_of(start, 16), size)


def load(source, target, sem):
    copy = pltpu.make_async_copy(source, target, sem)
    copy.start()
    return copy


def replica_peers(replicas):
    z = lax.axis_index("replica")
    return z, [{"replica": lax.rem(z + step, replicas)} for step in range(1, replicas)]


def forward_kernel(
    replicas,
    own,
    gate_hbm,
    up_hbm,
    down_hbm,
    tree_out,
    hidden_out,
    mix_out,
    gelu_out,
    every_out,
    total,
    tree,
    gate_w,
    up_w,
    down_w,
    hidden,
    mix,
    gelu,
    gate_lin,
    up_lin,
    send_sem,
    recv_sem,
    local_sem,
    *scratch,
):
    plane = Plane()
    rows = own.shape[0]
    wires = Wires(send_sem, recv_sem)
    loads = [
        load(gate_hbm, gate_w, local_sem.at[0]),
        load(up_hbm, up_w, local_sem.at[1]),
        load(down_hbm, down_w, local_sem.at[2]),
    ]
    z, others = replica_peers(replicas)
    greet(plane.near() + others)
    tree[block_at(plane.me * rows, rows), :] = own[...]
    stores = []

    def use(chip):
        order = len(stores) // 3
        slot = order % 2
        if order == 0:
            loads[0].wait()
            loads[1].wait()
        if order >= 2:
            stores[3 * (order - 2) + 1].wait()
            stores[3 * (order - 2) + 2].wait()
        there = block_at(chip * 2 * rows, 2 * rows)
        gate_lin[...] = dot_nt(tree[there, :], gate_w[...])
        up_lin[...] = dot_nt(tree[there, :], up_w[...])

        def step(at):
            gelu_value, slope = gelu_parts(gate_lin[at, :])
            up_value = up_lin[at, :]
            mix[slot, at, :] = (up_value * slope).astype(jnp.bfloat16)
            gelu[slot, at, :] = gelu_value.astype(jnp.bfloat16)
            hidden[block_at(chip * 2 * rows + at.start, at.size), :] = (
                gelu_value * up_value
            ).astype(jnp.bfloat16)

        by_rows(2 * rows, step, 16)
        base = 3 + 3 * order
        stores.append(load(hidden.at[there], hidden_out.at[there], local_sem.at[base]))
        stores.append(load(mix.at[slot], mix_out.at[there], local_sem.at[base + 1]))
        stores.append(load(gelu.at[slot], gelu_out.at[there], local_sem.at[base + 2]))

    over = [wires.send(own, every_out.at[z], other) for other in others]
    gather_tree(wires, plane, own, tree, rows, use)
    tree_store = load(tree, tree_out, local_sem.at[15])
    loads[2].wait()

    def product(chip, columns):
        return dot_nn(hidden[block_at(chip * 2 * rows, 2 * rows), :], down_w[:, columns])

    gathered = list(wires.sent)
    scatter_sum(wires, plane, scratch, product, total)
    for copy in over:
        copy.wait_recv()
    for copy in gathered:
        copy.wait_send()
    for copy in stores[0:1] + stores[3:4] + stores[6:] + [tree_store]:
        copy.wait()


def any_specs(count):
    return [pl.BlockSpec(memory_space=pl.ANY)] * count


def vmem_specs(count):
    return [pl.BlockSpec(memory_space=pltpu.VMEM)] * count


def remote_params(identity):
    return pltpu.CompilerParams(
        collective_id=identity, has_side_effects=True, vmem_limit_bytes=VMEM_BYTES
    )


def feedforward_forward(own, gate_weight, up_weight, down_weight):
    rows, width = own.shape
    units = gate_weight.shape[0]
    replicas, count = lax.axis_size("replica"), lax.axis_size("shard")
    tree_rows = count * rows
    low, full = jnp.bfloat16, jnp.float32
    copies = GATHER_COPIES + SCATTER_COPIES + replicas - 1
    return pl.pallas_call(
        functools.partial(forward_kernel, replicas),
        out_shape=(
            jax.ShapeDtypeStruct((tree_rows, width), low),
            jax.ShapeDtypeStruct((tree_rows, units), low),
            jax.ShapeDtypeStruct((tree_rows, units), low),
            jax.ShapeDtypeStruct((tree_rows, units), low),
            jax.ShapeDtypeStruct((replicas, rows, width), low),
            jax.ShapeDtypeStruct((rows, width), full),
        ),
        in_specs=vmem_specs(1) + any_specs(3),
        out_specs=tuple(any_specs(5) + vmem_specs(1)),
        scratch_shapes=[
            pltpu.VMEM((tree_rows, width), low),
            pltpu.VMEM((units, width), low),
            pltpu.VMEM((units, width), low),
            pltpu.VMEM((units, width), low),
            pltpu.VMEM((tree_rows, units), low),
            pltpu.VMEM((2, 2 * rows, units), low),
            pltpu.VMEM((2, 2 * rows, units), low),
            pltpu.VMEM((2 * rows, units), full),
            pltpu.VMEM((2 * rows, units), full),
            pltpu.SemaphoreType.DMA((copies,)),
            pltpu.SemaphoreType.DMA((copies,)),
            pltpu.SemaphoreType.DMA((16,)),
        ]
        + scatter_scratch(rows, width),
        compiler_params=remote_params(1),
        cost_estimate=pl.CostEstimate(
            flops=6 * tree_rows * units * width, bytes_accessed=40 * 2**20, transcendentals=0
        ),
    )(own, gate_weight, up_weight, down_weight)


def backward_kernel(
    replicas,
    own,
    gate_hbm,
    up_hbm,
    down_hbm,
    mix_hbm,
    gelu_hbm,
    tree_out,
    gate_out,
    up_out,
    every_out,
    total,
    tree,
    gate_w,
    up_w,
    down_w,
    gate_back,
    up_back,
    mix,
    gelu,
    hidden_back,
    send_sem,
    recv_sem,
    local_sem,
    *scratch,
):
    plane = Plane()
    rows = own.shape[0]
    wires = Wires(send_sem, recv_sem)
    chips = [plane.own_chip, plane.x_chip, plane.y_chip, plane.diag_chip]

    def fetch(order):
        there = block_at(chips[order] * 2 * rows, 2 * rows)
        return [
            load(mix_hbm.at[there], mix.at[order % 2], local_sem.at[3 + 2 * order]),
            load(gelu_hbm.at[there], gelu.at[order % 2], local_sem.at[4 + 2 * order]),
        ]

    loads = [load(down_hbm, down_w, local_sem.at[2])]
    fetched = [fetch(0), fetch(1)]
    loads += [
        load(gate_hbm, gate_w, local_sem.at[0]),
        load(up_hbm, up_w, local_sem.at[1]),
    ]
    z, others = replica_peers(replicas)
    greet(plane.near() + others)
    tree[block_at(plane.me * rows, rows), :] = own[...]
    stores = []

    def use(chip):
        order = len(stores) // 2
        slot = order % 2
        if order == 0:
            loads[0].wait()
        there = block_at(chip * 2 * rows, 2 * rows)
        hidden_back[...] = dot_nt(tree[there, :], down_w[...])
        for copy in fetched[order]:
            copy.wait()

        def step(at):
            value = hidden_back[at, :].astype(jnp.bfloat16).astype(jnp.float32)
            here = block_at(chip * 2 * rows + at.start, at.size)
            gate_back[here, :] = (value * mix[slot, at, :].astype(jnp.float32)).astype(jnp.bfloat16)
            up_back[here, :] = (value * gelu[slot, at, :].astype(jnp.float32)).astype(jnp.bfloat16)

        by_rows(2 * rows, step, 16)
        if order + 2 < 4:
            fetched.append(fetch(order + 2))
        base = 11 + 2 * order
        stores.append(load(gate_back.at[there], gate_out.at[there], local_sem.at[base]))
        stores.append(load(up_back.at[there], up_out.at[there], local_sem.at[base + 1]))

    over = [wires.send(own, every_out.at[z], other) for other in others]
    gather_tree(wires, plane, own, tree, rows, use)
    tree_store = load(tree, tree_out, local_sem.at[19])
    loads[1].wait()
    loads[2].wait()

    def product(chip, columns):
        there = block_at(chip * 2 * rows, 2 * rows)
        return dot_nn(gate_back[there, :], gate_w[:, columns]) + dot_nn(
            up_back[there, :], up_w[:, columns]
        )

    gathered = list(wires.sent)
    scatter_sum(wires, plane, scratch, product, total)
    for copy in over:
        copy.wait_recv()
    for copy in gathered:
        copy.wait_send()
    for copy in stores + [tree_store]:
        copy.wait()


def feedforward_backward(own, gate_weight, up_weight, down_weight, mix, gelu):
    rows, width = own.shape
    units = gate_weight.shape[0]
    replicas, count = lax.axis_size("replica"), lax.axis_size("shard")
    tree_rows = count * rows
    low, full = jnp.bfloat16, jnp.float32
    copies = GATHER_COPIES + SCATTER_COPIES + replicas - 1
    return pl.pallas_call(
        functools.partial(backward_kernel, replicas),
        out_shape=(
            jax.ShapeDtypeStruct((tree_rows, width), low),
            jax.ShapeDtypeStruct((tree_rows, units), low),
            jax.ShapeDtypeStruct((tree_rows, units), low),
            jax.ShapeDtypeStruct((replicas, rows, width), low),
            jax.ShapeDtypeStruct((rows, width), full),
        ),
        in_specs=vmem_specs(1) + any_specs(5),
        out_specs=tuple(any_specs(4) + vmem_specs(1)),
        scratch_shapes=[
            pltpu.VMEM((tree_rows, width), low),
            pltpu.VMEM((units, width), low),
            pltpu.VMEM((units, width), low),
            pltpu.VMEM((units, width), low),
            pltpu.VMEM((tree_rows, units), low),
            pltpu.VMEM((tree_rows, units), low),
            pltpu.VMEM((2, 2 * rows, units), low),
            pltpu.VMEM((2, 2 * rows, units), low),
            pltpu.VMEM((2 * rows, units), full),
            pltpu.SemaphoreType.DMA((copies,)),
            pltpu.SemaphoreType.DMA((copies,)),
            pltpu.SemaphoreType.DMA((20,)),
        ]
        + scatter_scratch(rows, width),
        compiler_params=remote_params(2),
        cost_estimate=pl.CostEstimate(
            flops=6 * tree_rows * units * width, bytes_accessed=40 * 2**20, transcendentals=0
        ),
    )(own, gate_weight, up_weight, down_weight, mix, gelu)


def shards_heads(
    hidden_in,
    cotangent,
    token_segment,
    token_valid,
    segment_parent,
    query_weight,
    key_weight,
    value_weight,
    output_weight,
    gate_weight,
    up_weight,
    down_weight,
    attention_gain,
    attention_post_gain,
    feedforward_gain,
    feedforward_post_gain,
):
    low = jnp.bfloat16
    row_count, model_width = hidden_in.shape
    shard_count = lax.axis_size("shard")
    tree_count = lax.axis_size("replica")
    shard = lax.axis_index("shard")
    row_start = shard * row_count
    tree_size = token_segment.shape[0]
    position, parent_tok, grand_tok = tree_tables(token_segment, token_valid, segment_parent[0])
    key_index = jnp.arange(tree_size, dtype=jnp.int32)
    allowed = allowed_mask(
        key_index, token_segment, parent_tok, grand_tok, key_index, token_segment, token_valid
    )
    cos_table, sin_table = rope_tables(position, HEAD)
    cos_table, sin_table = cos_table[:, 0], sin_table[:, 0]
    query_scale = HEAD ** (-0.5)
    valid_rows = lax.dynamic_slice_in_dim(token_valid, row_start, row_count).astype(jnp.float32)
    stream = hidden_in.astype(jnp.float32)
    second_core = lax.rem(shard, 2) == 1
    pairs = [(i, i ^ 1) for i in range(shard_count)]

    def both_halves(own):
        other = lax.ppermute(own, "shard", pairs)
        return jnp.where(
            second_core, jnp.concatenate([other, own]), jnp.concatenate([own, other])
        )

    key_head = both_halves(key_weight)
    value_head = both_halves(value_weight)
    normed_in = group_rows(norm_rows(stream, attention_gain).astype(low))
    queries = (
        rotate(dot_nt(normed_in, query_weight), cos_table, sin_table) * query_scale
    ).astype(low)
    keys = rotate(dot_nt(normed_in, key_head), cos_table, sin_table).astype(low)
    values = dot_nt(normed_in, value_head).astype(low)
    tanh_value = jnp.tanh(dot_nt(queries, keys) / score_cap)
    raised = jnp.where(allowed, jnp.exp(score_cap * tanh_value), 0.0)
    scale = 1.0 / jnp.sum(raised, axis=-1, keepdims=True)
    attended = dot_nn((raised * scale).astype(low), values).astype(low)
    attention_pre = sum_low(dot_nn(attended, output_weight))
    attention_branch = norm_rows(attention_pre, attention_post_gain)
    middle = stream + attention_branch
    normed_mid = norm_rows(middle, feedforward_gain).astype(low)
    mid_tree, hidden, mix, gelu_value, mid_every, feedforward_pre = feedforward_forward(
        normed_mid, gate_weight, up_weight, down_weight
    )
    feedforward_branch = norm_rows(feedforward_pre, feedforward_post_gain)
    result = middle + feedforward_branch
    squares = jnp.stack(
        [
            jnp.sum(valid_rows[:, None] * summand * summand)
            for summand in (stream, attention_branch, feedforward_branch, result)
        ]
    )
    valid_total = jnp.sum(valid_rows) * model_width
    seed_grad = cotangent.astype(jnp.float32) * valid_rows[:, None]
    ffpre_back, grad_four = norm_back(feedforward_pre, feedforward_post_gain, seed_grad)
    ffpre_low = ffpre_back.astype(low)
    ffpre_tree, gate_back, up_back, ffpre_every, mid_back = feedforward_backward(
        ffpre_low, gate_weight, up_weight, down_weight, mix, gelu_value
    )
    mid_every = lax.all_gather(mid_every, "shard", axis=1, tiled=True)
    ffpre_every = lax.all_gather(ffpre_every, "shard", axis=1, tiled=True)

    def hidden_grads(gate_lin, up_lin, gelu_value, gelu_slope, ffpre_rows):
        hidden_back = dot_nt(ffpre_rows, down_weight).astype(low).astype(jnp.float32)
        gate_back = (hidden_back * up_lin * gelu_slope).astype(low)
        up_back = (hidden_back * gelu_value).astype(low)
        return gate_back, up_back

    middle_part, grad_three = norm_back(middle, feedforward_gain, mid_back)
    middle_back = seed_grad + middle_part
    attention_pre_back, grad_two = norm_back(attention_pre, attention_post_gain, middle_back)
    pre_tree = group_rows(attention_pre_back.astype(low))
    attended_back = dot_nt(pre_tree, output_weight).astype(low)
    probs_back = raised * scale
    prob_grads = dot_nt(attended_back, values)
    inner_sum = jnp.sum(probs_back * prob_grads, axis=-1, keepdims=True)
    score_back = (probs_back * (prob_grads - inner_sum) * (1.0 - tanh_value * tanh_value)).astype(
        low
    )
    query_back = dot_nn(score_back, keys)
    key_back = dot_tn(score_back, queries)
    value_back = dot_tn(probs_back.astype(low), attended_back)
    key_back, value_back = (
        key_back + lax.ppermute(key_back, "shard", pairs),
        value_back + lax.ppermute(value_back, "shard", pairs),
    )
    query_low = rotate_back(query_back * query_scale, cos_table, sin_table).astype(low)
    key_low = rotate_back(key_back, cos_table, sin_table).astype(low)
    value_low = value_back.astype(low)
    half = HEAD // 2
    key_low = jnp.where(second_core, key_low[:, half:], key_low[:, :half])
    value_low = jnp.where(second_core, value_low[:, half:], value_low[:, :half])
    normed_back = sum_low(
        dot_nn(query_low, query_weight) + dot_nn(key_low, key_weight) + dot_nn(value_low, value_weight)
    )
    stream_part, grad_one = norm_back(stream, attention_gain, normed_back)
    input_grad = middle_back + stream_part
    attention_grads = jnp.concatenate(
        [
            dot_tn(query_low, normed_in),
            dot_tn(key_low, normed_in),
            dot_tn(value_low, normed_in),
            dot_tn(attended, pre_tree),
        ]
    ).astype(low)
    attention_grads = lax.psum(attention_grads, "replica").astype(jnp.float32)
    sizes = [query_weight.shape[0], key_weight.shape[0], value_weight.shape[0]]
    query_sum, key_sum, value_sum, output_sum = jnp.split(
        attention_grads, [sizes[0], sizes[0] + sizes[1], sum(sizes)]
    )
    gate_sum = dot_tn(gate_back, mid_tree)
    up_sum = dot_tn(up_back, mid_tree)
    down_sum = dot_tn(hidden, ffpre_tree)
    for step in range(1, tree_count):
        tree = lax.rem(lax.axis_index("replica") + step, tree_count)
        mid_rows = lax.dynamic_index_in_dim(mid_every, tree, 0, False)
        ffpre_rows = lax.dynamic_index_in_dim(ffpre_every, tree, 0, False)
        gate_lin = dot_nt(mid_rows, gate_weight)
        up_lin = dot_nt(mid_rows, up_weight)
        gelu_value, gelu_slope = gelu_parts(gate_lin)
        hidden = (gelu_value * up_lin).astype(low)
        gate_back, up_back = hidden_grads(gate_lin, up_lin, gelu_value, gelu_slope, ffpre_rows)
        gate_sum += dot_tn(gate_back, mid_rows)
        up_sum += dot_tn(up_back, mid_rows)
        down_sum += dot_tn(hidden, ffpre_rows)
    gain_one, gain_two, gain_three, gain_four, squares_all, valid_all = lax.psum(
        (grad_one, grad_two, grad_three, grad_four, squares, valid_total), ("replica", "shard")
    )
    stream_rms = jnp.sqrt(squares_all / valid_all)
    return (
        result.astype(low),
        input_grad,
        query_sum,
        key_sum,
        value_sum,
        output_sum,
        gate_sum,
        up_sum,
        down_sum,
        gain_one,
        gain_two,
        gain_three,
        gain_four,
        stream_rms,
    )


def solution(mesh):
    heads_fit = mesh.shape["shard"] == HEADS
    return jax.shard_map(
        shards_heads if heads_fit else shards_generic,
        mesh=mesh,
        in_specs=(
            P(("replica", "shard"), None),
            P(("replica", "shard"), None),
            P("replica"),
            P("replica"),
            P("replica", None),
            P("shard", None),
            P("shard", None),
            P("shard", None),
            P("shard", None),
            P("shard", None),
            P("shard", None),
            P("shard", None),
            P(),
            P(),
            P(),
            P(),
        ),
        out_specs=(
            P(("replica", "shard"), None),
            P(("replica", "shard"), None),
            P("shard", None),
            P("shard", None),
            P("shard", None),
            P("shard", None),
            P("shard", None),
            P("shard", None),
            P("shard", None),
            P(),
            P(),
            P(),
            P(),
            P(),
        ),
        check_vma=False,
    )
```

```python
import functools
import math

import jax
import jax.numpy as jnp
from jax import lax
from jax.experimental import pallas as pl
from jax.experimental.pallas import tpu as pltpu
from jax.sharding import PartitionSpec as P

HEADS = 8
KV_HEADS = 4
HEAD = 256


norm_eps = 1e-06
score_cap = 50.0


def norm_rows(stream, norm_gain):
    factor = lax.rsqrt(jnp.mean(stream * stream, axis=-1, keepdims=True) + norm_eps)
    return stream * factor * (1.0 + norm_gain)


def rotate(values, cos_table, sin_table):
    half_width = values.shape[-1] // 2
    turned = jnp.concatenate([-values[..., half_width:], values[..., :half_width]], axis=-1)
    return values * cos_table + turned * sin_table


def rotate_back(gradient, cos_table, sin_table):
    half_width = gradient.shape[-1] // 2
    shifted = gradient * sin_table
    unturned = jnp.concatenate([shifted[..., half_width:], -shifted[..., :half_width]], axis=-1)
    return gradient * cos_table + unturned


def rope_tables(position, head_size):
    half_width = head_size // 2
    frequency = jnp.power(10000.0, -jnp.arange(half_width, dtype=jnp.float32) * 2.0 / head_size)
    angles = position.astype(jnp.float32)[:, None] * frequency[None, :]
    angles = jnp.concatenate([angles, angles], axis=-1)[:, None, :]
    return (jnp.cos(angles), jnp.sin(angles))


def tree_tables(segment, valid_mask, parent):
    labels = jnp.arange(parent.shape[0], dtype=jnp.int32)
    member = (segment[:, None] == labels[None, :]).astype(jnp.int32)
    lengths = jnp.sum(member * valid_mask[:, None], axis=0)
    starts = jnp.sum((segment[:, None] < labels[None, :]).astype(jnp.int32), axis=0)
    parent_of = (parent[:, None] == labels[None, :]).astype(jnp.int32)
    grandparent = jnp.sum(parent_of * parent[None, :], axis=1)
    parent_len = jnp.sum(parent_of * lengths[None, :], axis=1)
    grand_of = (grandparent[:, None] == labels[None, :]).astype(jnp.int32)
    grand_len = jnp.sum(grand_of * lengths[None, :], axis=1)
    offsets = jnp.where(parent != labels, parent_len, 0) + jnp.where(
        grandparent != parent, grand_len, 0
    )
    token_index = jnp.arange(segment.shape[0], dtype=jnp.int32)
    position = jnp.sum(member * (offsets - starts)[None, :], axis=1) + token_index
    parent_tok = jnp.sum(member * parent[None, :], axis=1)
    grand_tok = jnp.sum(member * grandparent[None, :], axis=1)
    return (position, parent_tok, grand_tok)


def allowed_mask(query_index, query_seg, query_parent, query_grand, key_index, key_seg, key_valid):
    lineage = (
        (key_seg[None, :] == query_seg[:, None])
        | (key_seg[None, :] == query_parent[:, None])
        | (key_seg[None, :] == query_grand[:, None])
    )
    earlier = (key_seg[None, :] != query_seg[:, None]) | (key_index[None, :] < query_index[:, None])
    itself = key_index[None, :] == query_index[:, None]
    return itself | (key_valid[None, :] == 1) & lineage & earlier


def softmax_parts(scores, allowed):
    capped = score_cap * jnp.tanh(scores / score_cap)
    held = jnp.where(allowed, capped, -1000000000.0)
    largest = jnp.max(held, axis=-1, keepdims=True)
    raised = jnp.where(allowed, jnp.exp(held - largest), 0.0)
    total_mass = jnp.sum(raised, axis=-1, keepdims=True)
    return (raised / total_mass, largest + jnp.log(total_mass))


def gated_gelu(gate_lin, up_lin):
    return jax.nn.gelu(gate_lin, approximate=True) * up_lin


def collect_attention(query_weight, key_weight, value_weight, output_weight):
    return (
        lax.all_gather(query_weight, "shard", axis=0, tiled=True),
        lax.all_gather(key_weight, "shard", axis=0, tiled=True),
        lax.all_gather(value_weight, "shard", axis=0, tiled=True),
        lax.all_gather(output_weight, "shard", axis=0, tiled=True),
    )


def group_rows(values):
    return lax.all_gather(values, "shard", axis=0, tiled=True)


def group_sums(values):
    return lax.psum_scatter(values, "shard", scatter_dimension=0, tiled=True)


def shards_generic(
    hidden_in,
    cotangent,
    token_segment,
    token_valid,
    segment_parent,
    query_weight,
    key_weight,
    value_weight,
    output_weight,
    gate_weight,
    up_weight,
    down_weight,
    attention_gain,
    attention_post_gain,
    feedforward_gain,
    feedforward_post_gain,
):
    row_count, model_width = hidden_in.shape
    group_size = HEADS // KV_HEADS
    row_start = lax.axis_index("shard") * row_count
    tree_size = token_segment.shape[0]
    position, parent_tok, grand_tok = tree_tables(token_segment, token_valid, segment_parent[0])
    key_index = jnp.arange(tree_size, dtype=jnp.int32)

    def own_rows(table):
        return lax.dynamic_slice_in_dim(table, row_start, row_count)

    allowed = allowed_mask(
        own_rows(key_index),
        own_rows(token_segment),
        own_rows(parent_tok),
        own_rows(grand_tok),
        key_index,
        token_segment,
        token_valid,
    )
    mask_full = allowed[None, None]
    cos_table, sin_table = rope_tables(own_rows(position), HEAD)
    query_scale = HEAD ** (-0.5)
    valid_rows = own_rows(token_valid).astype(jnp.float32)
    stream = hidden_in.astype(jnp.float32)
    query_all, key_all, value_all, output_all = collect_attention(
        query_weight, key_weight, value_weight, output_weight
    )
    normed_in = norm_rows(stream, attention_gain).astype(jnp.bfloat16)
    query_lin = jnp.einsum("td,qd->tq", normed_in, query_all, preferred_element_type=jnp.float32)
    key_lin = jnp.einsum("td,qd->tq", normed_in, key_all, preferred_element_type=jnp.float32)
    value_lin = jnp.einsum("td,qd->tq", normed_in, value_all, preferred_element_type=jnp.float32)
    queries = (
        rotate(query_lin.reshape(row_count, HEADS, HEAD), cos_table, sin_table) * query_scale
    ).astype(jnp.bfloat16)
    keys_own = (
        rotate(key_lin.reshape(row_count, KV_HEADS, HEAD), cos_table, sin_table)
        .astype(jnp.bfloat16)
        .reshape(row_count, KV_HEADS * HEAD)
    )
    values_own = value_lin.astype(jnp.bfloat16)
    key_tree, value_tree = (
        lax.all_gather(keys_own, "shard", axis=0, tiled=True),
        lax.all_gather(values_own, "shard", axis=0, tiled=True),
    )
    query_groups = queries.reshape(row_count, KV_HEADS, group_size, HEAD)
    key_groups = key_tree.reshape(tree_size, KV_HEADS, HEAD)
    value_groups = value_tree.reshape(tree_size, KV_HEADS, HEAD)
    scores = jnp.einsum(
        "qgrd,kgd->grqk", query_groups, key_groups, preferred_element_type=jnp.float32
    )
    probs, log_total = softmax_parts(scores, mask_full)
    attended = jnp.einsum(
        "grqk,kgd->qgrd",
        probs.astype(jnp.bfloat16),
        value_groups,
        preferred_element_type=jnp.float32,
    )
    attended = attended.astype(jnp.bfloat16).reshape(row_count, HEADS * HEAD)
    attention_pre = jnp.dot(attended, output_all, preferred_element_type=jnp.float32)
    attention_branch = norm_rows(attention_pre, attention_post_gain)
    middle = stream + attention_branch
    normed_mid = norm_rows(middle, feedforward_gain).astype(jnp.bfloat16)
    mid_tree = group_rows(normed_mid)
    gate_lin = jnp.einsum("td,fd->tf", mid_tree, gate_weight, preferred_element_type=jnp.float32)
    up_lin = jnp.einsum("td,fd->tf", mid_tree, up_weight, preferred_element_type=jnp.float32)
    hidden = gated_gelu(gate_lin, up_lin).astype(jnp.bfloat16)
    feedforward_pre = group_sums(jnp.dot(hidden, down_weight, preferred_element_type=jnp.float32))
    feedforward_branch = norm_rows(feedforward_pre, feedforward_post_gain)
    result = middle + feedforward_branch
    squares = jnp.stack(
        [
            jnp.sum(valid_rows[:, None] * summand * summand)
            for summand in (stream, attention_branch, feedforward_branch, result)
        ]
    )
    valid_total = jnp.sum(valid_rows) * model_width
    squares_all, valid_all = lax.psum((squares, valid_total), ("replica", "shard"))
    seed_grad = cotangent.astype(jnp.float32) * valid_rows[:, None]
    unused_four, pull_four = jax.vjp(norm_rows, feedforward_pre, feedforward_post_gain)
    ffpre_back, grad_four = pull_four(seed_grad)
    ffpre_low = ffpre_back.astype(jnp.bfloat16)
    ffpre_tree = group_rows(ffpre_low)
    hidden_back = jnp.einsum(
        "td,fd->tf", ffpre_tree, down_weight, preferred_element_type=jnp.float32
    ).astype(jnp.bfloat16)
    unused_glu, pull_glu = jax.vjp(gated_gelu, gate_lin, up_lin)
    gate_back, up_back = pull_glu(hidden_back.astype(jnp.float32))
    gate_back = gate_back.astype(jnp.bfloat16)
    up_back = up_back.astype(jnp.bfloat16)
    mid_terms = jnp.dot(gate_back, gate_weight, preferred_element_type=jnp.float32) + jnp.dot(
        up_back, up_weight, preferred_element_type=jnp.float32
    )
    mid_back = group_sums(mid_terms)
    gate_grad = jnp.einsum("tf,td->fd", gate_back, mid_tree, preferred_element_type=jnp.float32)
    up_grad = jnp.einsum("tf,td->fd", up_back, mid_tree, preferred_element_type=jnp.float32)
    down_grad = jnp.einsum("tf,td->fd", hidden, ffpre_tree, preferred_element_type=jnp.float32)
    unused_three, pull_three = jax.vjp(norm_rows, middle, feedforward_gain)
    middle_part, grad_three = pull_three(mid_back)
    middle_back = seed_grad + middle_part
    unused_two, pull_two = jax.vjp(norm_rows, attention_pre, attention_post_gain)
    attention_pre_back, grad_two = pull_two(middle_back)
    pre_low = attention_pre_back.astype(jnp.bfloat16)
    query_all, key_all, value_all, output_all = collect_attention(
        query_weight, key_weight, value_weight, output_weight
    )
    attended_back = jnp.einsum(
        "td,qd->tq", pre_low, output_all, preferred_element_type=jnp.float32
    ).astype(jnp.bfloat16)
    scores = jnp.einsum(
        "qgrd,kgd->grqk", query_groups, key_groups, preferred_element_type=jnp.float32
    )
    tanh_value = jnp.tanh(scores / score_cap)
    probs_back = jnp.where(
        mask_full,
        jnp.exp(jnp.where(mask_full, score_cap * tanh_value - log_total, -1000000000.0)),
        0.0,
    )
    back_groups = attended_back.reshape(row_count, KV_HEADS, group_size, HEAD)
    prob_grads = jnp.einsum(
        "qgrd,kgd->grqk", back_groups, value_groups, preferred_element_type=jnp.float32
    )
    inner_sum = jnp.sum(probs_back * prob_grads, axis=-1, keepdims=True)
    score_back = (probs_back * (prob_grads - inner_sum) * (1.0 - tanh_value * tanh_value)).astype(
        jnp.bfloat16
    )
    query_back = jnp.einsum(
        "grqk,kgd->qgrd", score_back, key_groups, preferred_element_type=jnp.float32
    ).reshape(row_count, HEADS, HEAD)
    key_back = jnp.einsum(
        "grqk,qgrd->kgd", score_back, query_groups, preferred_element_type=jnp.float32
    ).reshape(tree_size, KV_HEADS * HEAD)
    value_back = jnp.einsum(
        "grqk,qgrd->kgd",
        probs_back.astype(jnp.bfloat16),
        back_groups,
        preferred_element_type=jnp.float32,
    ).reshape(tree_size, KV_HEADS * HEAD)
    key_sum, value_sum = (
        lax.psum_scatter(key_back, "shard", scatter_dimension=0, tiled=True),
        lax.psum_scatter(value_back, "shard", scatter_dimension=0, tiled=True),
    )
    query_low = (
        rotate_back(query_back * query_scale, cos_table, sin_table)
        .astype(jnp.bfloat16)
        .reshape(row_count, HEADS * HEAD)
    )
    key_low = (
        rotate_back(key_sum.reshape(row_count, KV_HEADS, HEAD), cos_table, sin_table)
        .astype(jnp.bfloat16)
        .reshape(row_count, KV_HEADS * HEAD)
    )
    value_low = value_sum.astype(jnp.bfloat16)
    normed_back = (
        jnp.dot(query_low, query_all, preferred_element_type=jnp.float32)
        + jnp.dot(key_low, key_all, preferred_element_type=jnp.float32)
        + jnp.dot(value_low, value_all, preferred_element_type=jnp.float32)
    )
    output_local = jnp.einsum("tq,td->qd", attended, pre_low, preferred_element_type=jnp.float32)
    query_local = jnp.einsum("tq,td->qd", query_low, normed_in, preferred_element_type=jnp.float32)
    key_local = jnp.einsum("tq,td->qd", key_low, normed_in, preferred_element_type=jnp.float32)
    value_local = jnp.einsum("tq,td->qd", value_low, normed_in, preferred_element_type=jnp.float32)
    query_part, key_part, value_part, output_part = (
        lax.psum_scatter(query_local, "shard", scatter_dimension=0, tiled=True),
        lax.psum_scatter(key_local, "shard", scatter_dimension=0, tiled=True),
        lax.psum_scatter(value_local, "shard", scatter_dimension=0, tiled=True),
        lax.psum_scatter(output_local, "shard", scatter_dimension=0, tiled=True),
    )
    unused_one, pull_one = jax.vjp(norm_rows, stream, attention_gain)
    stream_part, grad_one = pull_one(normed_back)
    input_grad = middle_back + stream_part
    query_sum, key_total, value_total, output_sum, gate_sum, up_sum, down_sum = lax.psum(
        (query_part, key_part, value_part, output_part, gate_grad, up_grad, down_grad), "replica"
    )
    gain_one, gain_two, gain_three, gain_four = lax.psum(
        (grad_one, grad_two, grad_three, grad_four), ("replica", "shard")
    )
    stream_rms = jnp.sqrt(squares_all / valid_all)
    return (
        result.astype(jnp.bfloat16),
        input_grad,
        query_sum,
        key_total,
        value_total,
        output_sum,
        gate_sum,
        up_sum,
        down_sum,
        gain_one,
        gain_two,
        gain_three,
        gain_four,
        stream_rms,
    )


def norm_factor(stream):
    return lax.rsqrt(jnp.mean(stream * stream, axis=-1, keepdims=True) + norm_eps)


def norm_back(stream, norm_gain, gradient):
    factor = norm_factor(stream)
    weighted = gradient * (1.0 + norm_gain)
    inner = jnp.mean(weighted * stream, axis=-1, keepdims=True)
    back = factor * weighted - stream * (factor * factor * factor * inner)
    gain_back = jnp.sum(gradient * stream * factor, axis=0)
    return back, gain_back


def dot_nt(left, right):
    return lax.dot_general(
        left, right, (((1,), (1,)), ((), ())), preferred_element_type=jnp.float32
    )


def dot_nn(left, right):
    return lax.dot_general(
        left, right, (((1,), (0,)), ((), ())), preferred_element_type=jnp.float32
    )


def dot_tn(left, right):
    return lax.dot_general(
        left, right, (((0,), (0,)), ((), ())), preferred_element_type=jnp.float32
    )


def sum_low(values):
    return lax.psum_scatter(
        values.astype(jnp.bfloat16), "shard", scatter_dimension=0, tiled=True
    ).astype(jnp.float32)


def gelu_parts(gate_lin):
    root = math.sqrt(2.0 / math.pi)
    square = gate_lin * gate_lin
    tanh_value = jnp.tanh(root * gate_lin * (1.0 + 0.044715 * square))
    half_up = 0.5 * (1.0 + tanh_value)
    slope = half_up + 0.5 * gate_lin * (1.0 - tanh_value * tanh_value) * root * (
        1.0 + 3.0 * 0.044715 * square
    )
    return gate_lin * half_up, slope


MESH_ID = pl.DeviceIdType.MESH
VMEM_BYTES = 62 * 2**20
ROOT = math.sqrt(2.0 / math.pi)


class Plane:
    def __init__(self):
        self.me = lax.axis_index("shard")
        core = lax.rem(self.me, 2)
        x = lax.rem(lax.div(self.me, 2), 2)
        y = lax.div(self.me, 4)
        self.core = core
        self.own_chip = 2 * y + x
        self.x_chip = 2 * y + 1 - x
        self.y_chip = 2 * (1 - y) + x
        self.diag_chip = 2 * (1 - y) + 1 - x
        self.mate = self.me + 1 - 2 * core
        self.x_dev = 2 * self.x_chip + core
        self.y_dev = 2 * self.y_chip + core
        self.diag_dev = 2 * self.diag_chip + core

    def near(self):
        return [{"shard": dev} for dev in (self.mate, self.x_dev, self.y_dev)]


class Wires:
    def __init__(self, send_sem, recv_sem):
        self.send_sem, self.recv_sem = send_sem, recv_sem
        self.sent = []

    def send(self, source, target, device):
        at = len(self.sent)
        copy = pltpu.make_async_remote_copy(
            src_ref=source,
            dst_ref=target,
            send_sem=self.send_sem.at[at],
            recv_sem=self.recv_sem.at[at],
            device_id=device if isinstance(device, dict) else {"shard": device},
            device_id_type=MESH_ID,
        )
        copy.start()
        self.sent.append(copy)
        return copy

    def finish(self):
        for copy in self.sent:
            copy.wait_send()


def greet(devices):
    barrier = pltpu.get_barrier_semaphore()
    for device in devices:
        pl.semaphore_signal(barrier, inc=1, device_id=device, device_id_type=MESH_ID)
    pl.semaphore_wait(barrier, len(devices))


def block_rows(ref, start, size, step=16):
    return ref.at[pl.ds(pl.multiple_of(start, step), size)]


def by_rows(count, body, size=32):
    def step(at, carry):
        body(pl.ds(pl.multiple_of(at * size, size), size))
        return carry

    lax.fori_loop(0, count // size, step, 0)


def column_tile(width):
    return max(t for t in range(128, 769, 128) if width % t == 0)


def by_columns(width, body):
    tile = column_tile(width)

    def step(at, carry):
        body(pl.ds(pl.multiple_of(at * tile, 128), tile))
        return carry

    lax.fori_loop(0, width // tile, step, 0)


def gather_tree(wires, plane, own, tree, rows, use):
    half = rows // 2

    def part(dev, start, size):
        return block_rows(tree, dev * rows + start, size)

    def own_part(start, size):
        return own.at[pl.ds(start, size)]

    me, mate = plane.me, plane.mate
    first_x = wires.send(own_part(0, half), part(me, 0, half), plane.x_dev)
    first_y = wires.send(own_part(half, half), part(me, half, half), plane.y_dev)
    to_mate = wires.send(own_part(0, rows), part(me, 0, rows), mate)
    rest_x = wires.send(own_part(half, half), part(me, half, half), plane.x_dev)
    rest_y = wires.send(own_part(0, half), part(me, 0, half), plane.y_dev)
    to_mate.wait_recv()
    use(plane.own_chip)
    first_x.wait_recv()
    turn_y = wires.send(part(plane.x_dev, 0, half), part(plane.x_dev, 0, half), plane.y_dev)
    first_y.wait_recv()
    turn_x = wires.send(part(plane.y_dev, half, half), part(plane.y_dev, half, half), plane.x_dev)
    rest_x.wait_recv()
    mate_x = wires.send(part(plane.x_dev, 0, rows), part(plane.x_dev, 0, rows), mate)
    rest_y.wait_recv()
    mate_y = wires.send(part(plane.y_dev, 0, rows), part(plane.y_dev, 0, rows), mate)
    mate_x.wait_recv()
    use(plane.x_chip)
    turn_y.wait_recv()
    turn_x.wait_recv()
    mate_diag = wires.send(part(plane.diag_dev, 0, rows), part(plane.diag_dev, 0, rows), mate)
    mate_y.wait_recv()
    use(plane.y_chip)
    mate_diag.wait_recv()
    use(plane.diag_chip)


GATHER_COPIES = 10


def scatter_scratch(rows, width):
    half = rows // 2
    low = jnp.bfloat16
    return [
        pltpu.VMEM((3, rows, width), jnp.float32),
        pltpu.VMEM((2 * rows, column_tile(width)), jnp.float32),
        pltpu.VMEM((2, rows, width), low),
        pltpu.VMEM((4, rows, width), low),
        pltpu.VMEM((3, half, width), low),
        pltpu.VMEM((3, half, width), low),
        pltpu.VMEM((3, half, width), low),
        pltpu.VMEM((3, half, width), low),
    ]


def scatter_sum(wires, plane, scratch, product, total, before=None):
    sums, piece, mate_out, mate_in, x_out, x_in, y_out, y_in = scratch
    rows, width = total.shape
    half = rows // 2
    low, full = jnp.bfloat16, jnp.float32

    def produce(slot, out_slot, in_slot, chip):
        if before is not None:
            before(chip)

        def tile(columns):
            piece[...] = product(chip, columns)
            sums[slot, :, columns] = piece[block_at(plane.core * rows, rows), :]
            mate_out[out_slot, :, columns] = piece[
                block_at((1 - plane.core) * rows, rows), :
            ].astype(low)

        by_columns(width, tile)
        return wires.send(mate_out.at[out_slot], mate_in.at[in_slot], plane.mate)

    def low_part(out, out_slot, slot, in_slot, start, more=None):
        def step(at):
            there = pl.ds(pl.multiple_of(start + at.start, 16), at.size)
            value = sums[slot, there, :] + mate_in[in_slot, there, :].astype(full)
            if more is not None:
                value += more[0, at, :].astype(full)
            out[out_slot, at, :] = value.astype(low)

        by_rows(half, step)

    diag = produce(0, 0, 0, plane.diag_chip)
    to_x = produce(1, 1, 1, plane.x_chip)
    diag.wait_recv()
    low_part(x_out, 0, 0, 0, 0)
    x_first = wires.send(x_out.at[0], x_in.at[0], plane.x_dev)
    low_part(y_out, 0, 0, 0, half)
    y_first = wires.send(y_out.at[0], y_in.at[0], plane.y_dev)
    diag.wait_send()
    to_y = produce(2, 0, 2, plane.y_chip)
    to_x.wait_recv()
    low_part(x_out, 1, 1, 1, 0)
    x_next = wires.send(x_out.at[1], x_in.at[1], plane.x_dev)
    to_x.wait_send()
    to_own = produce(0, 1, 3, plane.own_chip)
    to_y.wait_recv()
    low_part(y_out, 1, 2, 2, half)
    y_next = wires.send(y_out.at[1], y_in.at[1], plane.y_dev)
    y_first.wait_recv()
    low_part(x_out, 2, 1, 1, half, y_in)
    x_last = wires.send(x_out.at[2], x_in.at[2], plane.x_dev)
    x_first.wait_recv()
    low_part(y_out, 2, 2, 2, 0, x_in)
    y_last = wires.send(y_out.at[2], y_in.at[2], plane.y_dev)
    to_own.wait_recv()
    for copy in (x_next, y_next, x_last, y_last):
        copy.wait_recv()
    for start, x_slot, y_slot in ((0, 1, 2), (half, 2, 1)):

        def step(at, start=start, x_slot=x_slot, y_slot=y_slot):
            there = pl.ds(pl.multiple_of(start + at.start, 16), at.size)
            total[there, :] = (
                sums[0, there, :]
                + mate_in[3, there, :].astype(full)
                + x_in[x_slot, at, :].astype(full)
                + y_in[y_slot, at, :].astype(full)
            )

        by_rows(half, step)
    for copy in (to_y, to_own, x_first, x_next, x_last, y_first, y_next, y_last):
        copy.wait_send()


SCATTER_COPIES = 10


def block_at(start, size):
    return pl.ds(pl.multiple_of(start, 16), size)


def load(source, target, sem):
    copy = pltpu.make_async_copy(source, target, sem)
    copy.start()
    return copy


def replica_peers(replicas):
    z = lax.axis_index("replica")
    return z, [{"replica": lax.rem(z + step, replicas)} for step in range(1, replicas)]


def forward_kernel(
    replicas,
    own,
    gate_hbm,
    up_hbm,
    down_hbm,
    tree_out,
    hidden_out,
    mix_out,
    gelu_out,
    every_out,
    total,
    tree,
    gate_w,
    up_w,
    down_w,
    hidden,
    mix,
    gelu,
    gate_lin,
    up_lin,
    send_sem,
    recv_sem,
    local_sem,
    *scratch,
):
    plane = Plane()
    rows = own.shape[0]
    wires = Wires(send_sem, recv_sem)
    loads = [
        load(gate_hbm, gate_w, local_sem.at[0]),
        load(up_hbm, up_w, local_sem.at[1]),
        load(down_hbm, down_w, local_sem.at[2]),
    ]
    z, others = replica_peers(replicas)
    greet(plane.near() + others)
    tree[block_at(plane.me * rows, rows), :] = own[...]
    stores = []

    def use(chip):
        order = len(stores) // 3
        slot = order % 2
        if order == 0:
            loads[0].wait()
            loads[1].wait()
        if order >= 2:
            stores[3 * (order - 2) + 1].wait()
            stores[3 * (order - 2) + 2].wait()
        there = block_at(chip * 2 * rows, 2 * rows)
        gate_lin[...] = dot_nt(tree[there, :], gate_w[...])
        up_lin[...] = dot_nt(tree[there, :], up_w[...])

        def step(at):
            gelu_value, slope = gelu_parts(gate_lin[at, :])
            up_value = up_lin[at, :]
            mix[slot, at, :] = (up_value * slope).astype(jnp.bfloat16)
            gelu[slot, at, :] = gelu_value.astype(jnp.bfloat16)
            hidden[block_at(chip * 2 * rows + at.start, at.size), :] = (
                gelu_value * up_value
            ).astype(jnp.bfloat16)

        by_rows(2 * rows, step, 16)
        base = 3 + 3 * order
        stores.append(load(hidden.at[there], hidden_out.at[there], local_sem.at[base]))
        stores.append(load(mix.at[slot], mix_out.at[there], local_sem.at[base + 1]))
        stores.append(load(gelu.at[slot], gelu_out.at[there], local_sem.at[base + 2]))

    over = [wires.send(own, every_out.at[z], other) for other in others]
    gather_tree(wires, plane, own, tree, rows, use)
    tree_store = load(tree, tree_out, local_sem.at[15])
    loads[2].wait()

    def product(chip, columns):
        return dot_nn(hidden[block_at(chip * 2 * rows, 2 * rows), :], down_w[:, columns])

    gathered = list(wires.sent)
    scatter_sum(wires, plane, scratch, product, total)
    for copy in over:
        copy.wait_recv()
    for copy in gathered:
        copy.wait_send()
    for copy in stores[0:1] + stores[3:4] + stores[6:] + [tree_store]:
        copy.wait()


def any_specs(count):
    return [pl.BlockSpec(memory_space=pl.ANY)] * count


def vmem_specs(count):
    return [pl.BlockSpec(memory_space=pltpu.VMEM)] * count


def remote_params(identity):
    return pltpu.CompilerParams(
        collective_id=identity, has_side_effects=True, vmem_limit_bytes=VMEM_BYTES
    )


def feedforward_forward(own, gate_weight, up_weight, down_weight):
    rows, width = own.shape
    units = gate_weight.shape[0]
    replicas, count = lax.axis_size("replica"), lax.axis_size("shard")
    tree_rows = count * rows
    low, full = jnp.bfloat16, jnp.float32
    copies = GATHER_COPIES + SCATTER_COPIES + replicas - 1
    return pl.pallas_call(
        functools.partial(forward_kernel, replicas),
        out_shape=(
            jax.ShapeDtypeStruct((tree_rows, width), low),
            jax.ShapeDtypeStruct((tree_rows, units), low),
            jax.ShapeDtypeStruct((tree_rows, units), low),
            jax.ShapeDtypeStruct((tree_rows, units), low),
            jax.ShapeDtypeStruct((replicas, rows, width), low),
            jax.ShapeDtypeStruct((rows, width), full),
        ),
        in_specs=vmem_specs(1) + any_specs(3),
        out_specs=tuple(any_specs(5) + vmem_specs(1)),
        scratch_shapes=[
            pltpu.VMEM((tree_rows, width), low),
            pltpu.VMEM((units, width), low),
            pltpu.VMEM((units, width), low),
            pltpu.VMEM((units, width), low),
            pltpu.VMEM((tree_rows, units), low),
            pltpu.VMEM((2, 2 * rows, units), low),
            pltpu.VMEM((2, 2 * rows, units), low),
            pltpu.VMEM((2 * rows, units), full),
            pltpu.VMEM((2 * rows, units), full),
            pltpu.SemaphoreType.DMA((copies,)),
            pltpu.SemaphoreType.DMA((copies,)),
            pltpu.SemaphoreType.DMA((16,)),
        ]
        + scatter_scratch(rows, width),
        compiler_params=remote_params(1),
        cost_estimate=pl.CostEstimate(
            flops=6 * tree_rows * units * width, bytes_accessed=40 * 2**20, transcendentals=0
        ),
    )(own, gate_weight, up_weight, down_weight)


def backward_kernel(
    replicas,
    own,
    gate_hbm,
    up_hbm,
    down_hbm,
    mix_hbm,
    gelu_hbm,
    tree_out,
    gate_out,
    up_out,
    every_out,
    total,
    tree,
    gate_w,
    up_w,
    down_w,
    gate_back,
    up_back,
    mix,
    gelu,
    hidden_back,
    send_sem,
    recv_sem,
    local_sem,
    *scratch,
):
    plane = Plane()
    rows = own.shape[0]
    wires = Wires(send_sem, recv_sem)
    chips = [plane.own_chip, plane.x_chip, plane.y_chip, plane.diag_chip]

    def fetch(order):
        there = block_at(chips[order] * 2 * rows, 2 * rows)
        return [
            load(mix_hbm.at[there], mix.at[order % 2], local_sem.at[3 + 2 * order]),
            load(gelu_hbm.at[there], gelu.at[order % 2], local_sem.at[4 + 2 * order]),
        ]

    loads = [load(down_hbm, down_w, local_sem.at[2])]
    fetched = [fetch(0), fetch(1)]
    loads += [
        load(gate_hbm, gate_w, local_sem.at[0]),
        load(up_hbm, up_w, local_sem.at[1]),
    ]
    z, others = replica_peers(replicas)
    greet(plane.near() + others)
    tree[block_at(plane.me * rows, rows), :] = own[...]
    stores = []

    def use(chip):
        order = len(stores) // 2
        slot = order % 2
        if order == 0:
            loads[0].wait()
        there = block_at(chip * 2 * rows, 2 * rows)
        hidden_back[...] = dot_nt(tree[there, :], down_w[...])
        for copy in fetched[order]:
            copy.wait()

        def step(at):
            value = hidden_back[at, :].astype(jnp.bfloat16).astype(jnp.float32)
            here = block_at(chip * 2 * rows + at.start, at.size)
            gate_back[here, :] = (value * mix[slot, at, :].astype(jnp.float32)).astype(jnp.bfloat16)
            up_back[here, :] = (value * gelu[slot, at, :].astype(jnp.float32)).astype(jnp.bfloat16)

        by_rows(2 * rows, step, 16)
        if order + 2 < 4:
            fetched.append(fetch(order + 2))
        base = 11 + 2 * order
        stores.append(load(gate_back.at[there], gate_out.at[there], local_sem.at[base]))
        stores.append(load(up_back.at[there], up_out.at[there], local_sem.at[base + 1]))

    over = [wires.send(own, every_out.at[z], other) for other in others]
    gather_tree(wires, plane, own, tree, rows, use)
    tree_store = load(tree, tree_out, local_sem.at[19])
    loads[1].wait()
    loads[2].wait()

    def product(chip, columns):
        there = block_at(chip * 2 * rows, 2 * rows)
        return dot_nn(gate_back[there, :], gate_w[:, columns]) + dot_nn(
            up_back[there, :], up_w[:, columns]
        )

    gathered = list(wires.sent)
    scatter_sum(wires, plane, scratch, product, total)
    for copy in over:
        copy.wait_recv()
    for copy in gathered:
        copy.wait_send()
    for copy in stores + [tree_store]:
        copy.wait()


def feedforward_backward(own, gate_weight, up_weight, down_weight, mix, gelu):
    rows, width = own.shape
    units = gate_weight.shape[0]
    replicas, count = lax.axis_size("replica"), lax.axis_size("shard")
    tree_rows = count * rows
    low, full = jnp.bfloat16, jnp.float32
    copies = GATHER_COPIES + SCATTER_COPIES + replicas - 1
    return pl.pallas_call(
        functools.partial(backward_kernel, replicas),
        out_shape=(
            jax.ShapeDtypeStruct((tree_rows, width), low),
            jax.ShapeDtypeStruct((tree_rows, units), low),
            jax.ShapeDtypeStruct((tree_rows, units), low),
            jax.ShapeDtypeStruct((replicas, rows, width), low),
            jax.ShapeDtypeStruct((rows, width), full),
        ),
        in_specs=vmem_specs(1) + any_specs(5),
        out_specs=tuple(any_specs(4) + vmem_specs(1)),
        scratch_shapes=[
            pltpu.VMEM((tree_rows, width), low),
            pltpu.VMEM((units, width), low),
            pltpu.VMEM((units, width), low),
            pltpu.VMEM((units, width), low),
            pltpu.VMEM((tree_rows, units), low),
            pltpu.VMEM((tree_rows, units), low),
            pltpu.VMEM((2, 2 * rows, units), low),
            pltpu.VMEM((2, 2 * rows, units), low),
            pltpu.VMEM((2 * rows, units), full),
            pltpu.SemaphoreType.DMA((copies,)),
            pltpu.SemaphoreType.DMA((copies,)),
            pltpu.SemaphoreType.DMA((20,)),
        ]
        + scatter_scratch(rows, width),
        compiler_params=remote_params(2),
        cost_estimate=pl.CostEstimate(
            flops=6 * tree_rows * units * width, bytes_accessed=40 * 2**20, transcendentals=0
        ),
    )(own, gate_weight, up_weight, down_weight, mix, gelu)


class Copy:
    def __init__(self, build):
        self.build = build

    def start(self):
        self.build().start()

    def wait_recv(self):
        self.build().wait_recv()

    def wait_send(self):
        self.build().wait_send()


class PlaneGather:
    def __init__(self, plane, own, tree, rows, send_sem, recv_sem, local_sem, base):
        half = rows // 2
        me, mate, x_dev, y_dev = plane.me, plane.mate, plane.x_dev, plane.y_dev
        diag = plane.diag_dev
        self.started = []

        def part(dev, start, size):
            return block_rows(tree, dev * rows + start, size)

        def copy(source, target, device):
            at = base + len(self.started)

            def build():
                return pltpu.make_async_remote_copy(
                    src_ref=source(),
                    dst_ref=target(),
                    send_sem=send_sem.at[at],
                    recv_sem=recv_sem.at[at],
                    device_id={"shard": device},
                    device_id_type=MESH_ID,
                )

            self.started.append(Copy(build))
            return self.started[-1]

        def from_own(start, size, device):
            return copy(
                lambda: own().at[pl.ds(start, size)], lambda: part(me, start, size), device
            )

        def onward(dev, start, size, device):
            return copy(lambda: part(dev, start, size), lambda: part(dev, start, size), device)

        self.first_x = from_own(0, half, x_dev)
        self.first_y = from_own(half, half, y_dev)
        self.to_mate = from_own(0, rows, mate)
        self.rest_x = from_own(half, half, x_dev)
        self.rest_y = from_own(0, half, y_dev)
        self.turn_y = onward(x_dev, 0, half, y_dev)
        self.turn_x = onward(y_dev, half, half, x_dev)
        self.mate_x = onward(x_dev, 0, rows, mate)
        self.mate_y = onward(y_dev, 0, rows, mate)
        self.mate_diag = onward(diag, 0, rows, mate)
        self.local = lambda: pltpu.make_async_copy(own(), part(me, 0, rows), local_sem)

    def begin(self):
        for copy in (self.first_x, self.first_y, self.to_mate, self.rest_x, self.rest_y):
            copy.start()
        self.local().start()

    def forward(self):
        self.first_x.wait_recv()
        self.turn_y.start()
        self.first_y.wait_recv()
        self.turn_x.start()
        self.rest_x.wait_recv()
        self.mate_x.start()
        self.rest_y.wait_recv()
        self.mate_y.start()

    def near_rows(self):
        self.local().wait()
        self.to_mate.wait_recv()
        self.mate_x.wait_recv()

    def turned(self):
        self.turn_y.wait_recv()
        self.turn_x.wait_recv()
        self.mate_diag.start()

    def far_rows(self):
        self.mate_y.wait_recv()
        self.mate_diag.wait_recv()

    def finish(self):
        for copy in self.started:
            copy.wait_send()


def grads_kernel(
    replicas,
    mid_every,
    back_every,
    mid_tree,
    back_tree,
    hidden_hbm,
    gate_back_hbm,
    up_back_hbm,
    gate_hbm,
    up_hbm,
    down_hbm,
    gate_out,
    up_out,
    down_out,
    mid_rows,
    back_rows,
    gate_sum,
    up_sum,
    down_sum,
    gate_w,
    up_w,
    down_w,
    mid,
    back,
    own_hidden,
    own_gate,
    own_up,
    hidden,
    gate_back,
    up_back,
    send_sem,
    recv_sem,
    local_sem,
    block_sem,
    weight_sem,
):
    plane = Plane()
    units, width = gate_w.shape
    size = mid.shape[1]
    rows = mid_every.shape[1]
    tree_rows = mid_tree.shape[0]
    blocks = tree_rows // size
    half_blocks = blocks // 2
    low = jnp.bfloat16
    z = lax.axis_index("replica")
    y = lax.div(plane.me, 4)
    others = replicas - 1
    last = (others + 1) * blocks - 1
    weights = [
        pltpu.make_async_copy(source, target, weight_sem.at[at])
        for at, (source, target) in enumerate(
            ((gate_hbm, gate_w), (up_hbm, up_w), (down_hbm, down_w))
        )
    ]
    gathers = []
    for step in range(others):
        pair = []
        for at, (every, tree) in enumerate(((mid_every, mid_rows), (back_every, back_rows))):
            count = 2 * step + at
            pair.append(
                PlaneGather(
                    plane,
                    lambda every=every, step=step: every.at[lax.rem(z + step + 1, replicas)],
                    tree.at[step],
                    rows,
                    send_sem,
                    recv_sem,
                    local_sem.at[count],
                    GATHER_COPIES * count,
                )
            )
        gathers.append(pair)

    def own_loads(block, slot):
        there = block_at(block * size, size)
        return [
            pltpu.make_async_copy(source.at[there], target.at[slot], block_sem.at[slot, at])
            for at, (source, target) in enumerate(
                (
                    (mid_tree, mid),
                    (back_tree, back),
                    (hidden_hbm, own_hidden),
                    (gate_back_hbm, own_gate),
                    (up_back_hbm, own_up),
                )
            )
        ]

    def other_loads(block, slot):
        tree = lax.div(block, blocks) - 1
        within = lax.rem(block, blocks)
        part = lax.div(within, half_blocks)
        start = (y + part - 2 * y * part) * half_blocks * size
        there = block_at(start + lax.rem(within, half_blocks) * size, size)
        return [
            pltpu.make_async_copy(source.at[tree, there], target.at[slot], block_sem.at[slot, at])
            for at, (source, target) in enumerate(((mid_rows, mid), (back_rows, back)))
        ]

    def add(total, dot, lhs, rhs, slot):
        def tile(columns):
            total[:, columns] += dot(lhs, rhs[slot, :, columns])

        by_columns(width, tile)

    events = {}

    def event(block, *actions):
        events.setdefault(block, []).extend(actions)

    for copy in weights:
        copy.start()
    for copy in own_loads(0, 0):
        copy.start()
    for total in (down_sum, gate_sum, up_sum):
        by_rows(units, lambda at, total=total: total.__setitem__((at, slice(None)), jnp.zeros((at.size, width), jnp.float32)))
    greet(plane.near())
    for gather in gathers[0]:
        gather.begin()
    for step in range(others):
        mid_gather, back_gather = gathers[step]
        base = step * blocks
        event(base + half_blocks - 2, mid_gather.forward)
        event(base + half_blocks, back_gather.forward)
        if step + 1 < others:
            event(base + half_blocks, *[gather.begin for gather in gathers[step + 1]])
        event(base + blocks - 1, mid_gather.near_rows, back_gather.near_rows)
        event(base + blocks, mid_gather.turned, back_gather.turned)
        event(base + blocks + half_blocks - 1, mid_gather.far_rows, back_gather.far_rows)

    def body(block, carry):
        slot = lax.rem(block, 2)
        is_own = block < blocks

        @pl.when(is_own)
        def _():
            for copy in own_loads(block, slot):
                copy.wait()

        @pl.when(block == blocks)
        def _():
            for copy in weights:
                copy.wait()

        @pl.when(block >= blocks)
        def _():
            for copy in other_loads(block, slot):
                copy.wait()
            tile = max(t for t in (384, 256, 128) if units % t == 0)
            for at in range(units // tile):
                there = pl.ds(at * tile, tile)
                gelu_value, slope = gelu_parts(dot_nt(gate_w[there, :], mid[slot]))
                up_lin = dot_nt(up_w[there, :], mid[slot])
                hidden_back = dot_nt(down_w[there, :], back[slot]).astype(low).astype(jnp.float32)
                hidden[there, :] = (gelu_value * up_lin).astype(low)
                gate_back[there, :] = (hidden_back * up_lin * slope).astype(low)
                up_back[there, :] = (hidden_back * gelu_value).astype(low)

        for when, actions in events.items():

            @pl.when(block == when)
            def _(actions=actions):
                for action in actions:
                    action()

        @pl.when(block + 1 < blocks)
        def _():
            for copy in own_loads(block + 1, 1 - slot):
                copy.start()

        @pl.when((block + 1 >= blocks) & (block < last))
        def _():
            for copy in other_loads(block + 1, 1 - slot):
                copy.start()

        @pl.when(is_own)
        def _():
            add(down_sum, dot_tn, own_hidden[slot], back, slot)
            add(gate_sum, dot_tn, own_gate[slot], mid, slot)
            add(up_sum, dot_tn, own_up[slot], mid, slot)

        @pl.when(block >= blocks)
        def _():
            stores = []
            for at, (total, lhs, rhs, out) in enumerate(
                (
                    (down_sum, hidden, back, down_out),
                    (gate_sum, gate_back, mid, gate_out),
                    (up_sum, up_back, mid, up_out),
                )
            ):
                add(total, dot_nn, lhs[...], rhs, slot)
                stores.append(pltpu.make_async_copy(total, out, weight_sem.at[3 + at]))
                pl.when(block == last)(stores[-1].start)

            @pl.when(block == last)
            def _():
                for copy in stores:
                    copy.wait()

        return carry

    lax.fori_loop(0, last + 1, body, 0)
    for pair in gathers:
        for gather in pair:
            gather.finish()


def feedforward_grads(
    mid_every, back_every, mid_tree, back_tree, hidden, gate_back, up_back, gate_w, up_w, down_w
):
    replicas, rows, width = mid_every.shape
    tree_rows = mid_tree.shape[0]
    units = gate_w.shape[0]
    size = tree_rows // 6
    low, full = jnp.bfloat16, jnp.float32
    copies = GATHER_COPIES * 2 * (replicas - 1)
    grad = jax.ShapeDtypeStruct((units, width), full)
    gathered = jax.ShapeDtypeStruct((replicas - 1, tree_rows, width), low)
    return pl.pallas_call(
        functools.partial(grads_kernel, replicas),
        out_shape=(grad, grad, grad, gathered, gathered),
        in_specs=any_specs(10),
        out_specs=tuple(any_specs(5)),
        scratch_shapes=[pltpu.VMEM((units, width), full)] * 3
        + [pltpu.VMEM((units, width), low)] * 3
        + [pltpu.VMEM((2, size, width), low)] * 2
        + [pltpu.VMEM((2, size, units), low)] * 3
        + [pltpu.VMEM((units, size), low)] * 3
        + [
            pltpu.SemaphoreType.DMA((copies,)),
            pltpu.SemaphoreType.DMA((copies,)),
            pltpu.SemaphoreType.DMA((2 * (replicas - 1),)),
            pltpu.SemaphoreType.DMA((2, 5)),
            pltpu.SemaphoreType.DMA((6,)),
        ],
        compiler_params=remote_params(5),
        cost_estimate=pl.CostEstimate(
            flops=2 * (6 * replicas - 3) * tree_rows * units * width,
            bytes_accessed=200 * 2**20,
            transcendentals=0,
        ),
    )(mid_every, back_every, mid_tree, back_tree, hidden, gate_back, up_back, gate_w, up_w, down_w)[:3]


def turn(values, cos, sin):
    half = values.shape[-1] // 2
    first, second = values[:, :half], values[:, half:]
    return first * cos - second * sin, second * cos + first * sin


def turn_back(values, cos, sin):
    half = values.shape[-1] // 2
    first, second = values[:, :half], values[:, half:]
    return first * cos + second * sin, second * cos - first * sin


def allowed_block(query_bits, key_bits, query_start, key_start):
    shape = (query_bits.shape[0], key_bits.shape[1])
    query = query_start + lax.broadcasted_iota(jnp.int32, shape, 0)
    key = key_start + lax.broadcasted_iota(jnp.int32, shape, 1)
    return (((query_bits & key_bits) != 0) & (key < query)) | (key == query)


def attention_forward_kernel(
    stream,
    gain,
    cos_ref,
    sin_ref,
    query_bits,
    key_bits,
    query_w,
    key_own,
    value_own,
    output_w,
    tree_out,
    query_out,
    key_out,
    value_out,
    attended_out,
    mass_out,
    total,
    own,
    tree,
    key_w,
    value_w,
    lin,
    send_sem,
    recv_sem,
    local_sem,
    *scratch,
):
    plane = Plane()
    rows, width = stream.shape
    head = query_w.shape[0]
    block = 2 * rows
    half = head // 2
    low, full = jnp.bfloat16, jnp.float32
    wires = Wires(send_sem, recv_sem)

    def normed(at):
        value = stream[at, :].astype(full)
        own[at, :] = norm_rows(value, gain[...]).astype(low)

    by_rows(rows, normed)
    greet(plane.near())
    mine = block_at(plane.core * half, half)
    key_w[mine, :] = key_own[...]
    value_w[mine, :] = value_own[...]
    tree[block_at(plane.me * rows, rows), :] = own[...]
    halves = [
        wires.send(key_own, key_w.at[mine], plane.mate),
        wires.send(value_own, value_w.at[mine], plane.mate),
    ]
    seen = []

    def use(chip):
        if not seen:
            for copy in halves:
                copy.wait_recv()
        seen.append(chip)
        there = block_at(chip * block, block)
        cos, sin = cos_ref[there, :], sin_ref[there, :]
        lin[...] = dot_nt(tree[there, :], query_w[...])
        first, second = turn(lin[...], cos, sin)
        query_out[there, :half] = (first * head**-0.5).astype(low)
        query_out[there, half:] = (second * head**-0.5).astype(low)
        lin[...] = dot_nt(tree[there, :], key_w[...])
        first, second = turn(lin[...], cos, sin)
        key_out[there, :half] = first.astype(low)
        key_out[there, half:] = second.astype(low)
        value_out[there, :] = dot_nt(tree[there, :], value_w[...]).astype(low)

    gather_tree(wires, plane, own, tree, rows, use)
    store = load(tree, tree_out, local_sem.at[0])
    gathered = list(wires.sent)

    def attend(chip):
        there = block_at(chip * block, block)
        bits = query_bits[there, :]

        def chunk(at, carry):
            result, mass = carry
            keys = block_at(at * block, block)
            scores = dot_nt(query_out[there, :], key_out[keys, :])
            allowed = allowed_block(
                bits, key_bits[:, pl.ds(pl.multiple_of(at * block, 128), block)], chip * block, at * block
            )
            raised = jnp.where(allowed, jnp.exp(score_cap * jnp.tanh(scores / score_cap)), 0.0)
            result += dot_nn(raised.astype(low), value_out[keys, :])
            return result, mass + jnp.sum(raised, axis=1, keepdims=True)

        result, mass = lax.fori_loop(
            0,
            chip + 1,
            chunk,
            (jnp.zeros((block, head), full), jnp.zeros((block, 1), full)),
        )
        scale = 1.0 / mass
        attended_out[there, :] = (result * scale).astype(low)
        mass_out[there, :] = jnp.broadcast_to(scale, (block, mass_out.shape[1]))

    def product(chip, columns):
        return dot_nn(attended_out[block_at(chip * block, block), :], output_w[:, columns])

    scatter_sum(wires, plane, scratch, product, total, attend)
    for copy in gathered:
        copy.wait_send()
    store.wait()


def attention_forward(
    stream, gain, cos, sin, query_bits, key_bits, query_weight, key_weight, value_weight, output_weight
):
    rows, width = stream.shape
    head = query_weight.shape[0]
    tree_rows = cos.shape[0]
    low, full = jnp.bfloat16, jnp.float32
    copies = GATHER_COPIES + SCATTER_COPIES + 2
    heads = jax.ShapeDtypeStruct((tree_rows, head), low)
    return pl.pallas_call(
        attention_forward_kernel,
        out_shape=(
            jax.ShapeDtypeStruct((tree_rows, width), low),
            heads,
            heads,
            heads,
            heads,
            jax.ShapeDtypeStruct((tree_rows, 128), full),
            jax.ShapeDtypeStruct((rows, width), full),
        ),
        in_specs=vmem_specs(10),
        out_specs=tuple(any_specs(1) + vmem_specs(6)),
        scratch_shapes=[
            pltpu.VMEM((rows, width), low),
            pltpu.VMEM((tree_rows, width), low),
            pltpu.VMEM((head, width), low),
            pltpu.VMEM((head, width), low),
            pltpu.VMEM((2 * rows, head), full),
            pltpu.SemaphoreType.DMA((copies,)),
            pltpu.SemaphoreType.DMA((copies,)),
            pltpu.SemaphoreType.DMA((1,)),
        ]
        + scatter_scratch(rows, width),
        compiler_params=remote_params(3),
        cost_estimate=pl.CostEstimate(
            flops=10 * tree_rows * head * width, bytes_accessed=20 * 2**20, transcendentals=0
        ),
    )(
        stream,
        gain[None],
        cos,
        sin,
        query_bits,
        key_bits,
        query_weight,
        key_weight,
        value_weight,
        output_weight,
    )


def attention_backward_kernel(
    own,
    cos_ref,
    sin_ref,
    query_bits,
    key_bits,
    weights,
    output_w,
    queries,
    keys_ref,
    values,
    attended,
    mass,
    tree_out,
    back_out,
    total,
    tree,
    attended_back,
    query_sum,
    key_sum,
    value_sum,
    mate_out,
    mate_in,
    send_sem,
    recv_sem,
    local_sem,
    *scratch,
):
    plane = Plane()
    rows, width = own.shape
    head = output_w.shape[0]
    half = head // 2
    block = 2 * rows
    low, full = jnp.bfloat16, jnp.float32
    wires = Wires(send_sem, recv_sem)
    greet(plane.near())
    tree[block_at(plane.me * rows, rows), :] = own[...]
    key_sum[...] = jnp.zeros_like(key_sum)
    value_sum[...] = jnp.zeros_like(value_sum)

    def use(chip):
        there = block_at(chip * block, block)
        attended_back[there, :] = dot_nt(tree[there, :], output_w[...]).astype(low)
        inner = jnp.sum(
            attended_back[there, :].astype(full) * attended[there, :].astype(full),
            axis=1,
            keepdims=True,
        )
        bits = query_bits[there, :]
        scale = mass[there, :1]

        def chunk(at, result):
            here = block_at(at * block, block)
            tanh_value = jnp.tanh(dot_nt(queries[there, :], keys_ref[here, :]) / score_cap)
            allowed = allowed_block(
                bits, key_bits[:, pl.ds(pl.multiple_of(at * block, 128), block)], chip * block, at * block
            )
            probs = jnp.where(allowed, jnp.exp(score_cap * tanh_value) * scale, 0.0)
            prob_grads = dot_nt(attended_back[there, :], values[here, :])
            score_back = (probs * (prob_grads - inner) * (1.0 - tanh_value * tanh_value)).astype(low)
            value_sum[here, :] += dot_tn(probs.astype(low), attended_back[there, :])
            key_sum[here, :] += dot_tn(score_back, queries[there, :])
            return result + dot_nn(score_back, keys_ref[here, :])

        result = lax.fori_loop(0, chip + 1, chunk, jnp.zeros((block, head), full))
        first, second = turn_back(result * head**-0.5, cos_ref[there, :], sin_ref[there, :])
        query_sum[there, :half] = first.astype(low)
        query_sum[there, half:] = second.astype(low)

    gather_tree(wires, plane, own, tree, rows, use)
    store = load(tree, tree_out, local_sem.at[0])
    back_out[:, :head] = query_sum[...]
    first_core = plane.core == 0

    def exchange(at):
        first, second = turn_back(key_sum[at, :], cos_ref[at, :], sin_ref[at, :])
        key_sum[at, :half] = jnp.where(first_core, first, second)
        mate_out[at, :half] = jnp.where(first_core, second, first)
        first, second = value_sum[at, :half], value_sum[at, half:]
        value_sum[at, :half] = jnp.where(first_core, first, second)
        mate_out[at, half:] = jnp.where(first_core, second, first)

    by_rows(tree.shape[0], exchange)
    swap = wires.send(mate_out, mate_in, plane.mate)
    swap.wait_recv()

    def finish(at):
        back_out[at, head : head + half] = (key_sum[at, :half] + mate_in[at, :half]).astype(low)
        back_out[at, head + half :] = (value_sum[at, :half] + mate_in[at, half:]).astype(low)

    by_rows(tree.shape[0], finish)
    gathered = list(wires.sent)

    def product(chip, columns):
        return dot_nn(back_out[block_at(chip * block, block), :], weights[:, columns])

    scatter_sum(wires, plane, scratch, product, total)
    for copy in gathered:
        copy.wait_send()
    store.wait()


def attention_backward(
    own, cos, sin, query_bits, key_bits, weights, output_weight, queries, keys, values, attended, mass
):
    rows, width = own.shape
    head = output_weight.shape[0]
    tree_rows = cos.shape[0]
    low, full = jnp.bfloat16, jnp.float32
    copies = GATHER_COPIES + SCATTER_COPIES + 1
    return pl.pallas_call(
        attention_backward_kernel,
        out_shape=(
            jax.ShapeDtypeStruct((tree_rows, width), low),
            jax.ShapeDtypeStruct((tree_rows, 2 * head), low),
            jax.ShapeDtypeStruct((rows, width), full),
        ),
        in_specs=vmem_specs(12),
        out_specs=tuple(any_specs(1) + vmem_specs(2)),
        scratch_shapes=[
            pltpu.VMEM((tree_rows, width), low),
            pltpu.VMEM((tree_rows, head), low),
            pltpu.VMEM((tree_rows, head), low),
            pltpu.VMEM((tree_rows, head), full),
            pltpu.VMEM((tree_rows, head), full),
            pltpu.VMEM((tree_rows, head), full),
            pltpu.VMEM((tree_rows, head), full),
            pltpu.SemaphoreType.DMA((copies,)),
            pltpu.SemaphoreType.DMA((copies,)),
            pltpu.SemaphoreType.DMA((1,)),
        ]
        + scatter_scratch(rows, width),
        compiler_params=remote_params(4),
        cost_estimate=pl.CostEstimate(
            flops=10 * tree_rows * head * width, bytes_accessed=20 * 2**20, transcendentals=0
        ),
    )(own, cos, sin, query_bits, key_bits, weights, output_weight, queries, keys, values, attended, mass)


def shards_heads(
    hidden_in,
    cotangent,
    token_segment,
    token_valid,
    segment_parent,
    query_weight,
    key_weight,
    value_weight,
    output_weight,
    gate_weight,
    up_weight,
    down_weight,
    attention_gain,
    attention_post_gain,
    feedforward_gain,
    feedforward_post_gain,
):
    low = jnp.bfloat16
    row_count, model_width = hidden_in.shape
    shard = lax.axis_index("shard")
    row_start = shard * row_count
    position, parent_tok, grand_tok = tree_tables(token_segment, token_valid, segment_parent[0])
    key_bits = jnp.where(token_valid == 1, 1 << token_segment, 0)[None]
    query_bits = ((1 << token_segment) | (1 << parent_tok) | (1 << grand_tok))[:, None]
    cos_table, sin_table = rope_tables(position, HEAD)
    cos_table, sin_table = cos_table[:, 0, : HEAD // 2], sin_table[:, 0, : HEAD // 2]
    valid_rows = lax.dynamic_slice_in_dim(token_valid, row_start, row_count).astype(jnp.float32)
    stream = hidden_in.astype(jnp.float32)
    normed_in, queries, keys, values, attended, mass, attention_pre = attention_forward(
        hidden_in,
        attention_gain,
        cos_table,
        sin_table,
        query_bits,
        key_bits,
        query_weight,
        key_weight,
        value_weight,
        output_weight,
    )
    attention_branch = norm_rows(attention_pre, attention_post_gain)
    middle = stream + attention_branch
    normed_mid = norm_rows(middle, feedforward_gain).astype(low)
    mid_tree, hidden, mix, gelu_value, mid_every, feedforward_pre = feedforward_forward(
        normed_mid, gate_weight, up_weight, down_weight
    )
    feedforward_branch = norm_rows(feedforward_pre, feedforward_post_gain)
    result = middle + feedforward_branch
    squares = jnp.stack(
        [
            jnp.sum(valid_rows[:, None] * summand * summand)
            for summand in (stream, attention_branch, feedforward_branch, result)
        ]
    )
    valid_total = jnp.sum(valid_rows) * model_width
    seed_grad = cotangent.astype(jnp.float32) * valid_rows[:, None]
    ffpre_back, grad_four = norm_back(feedforward_pre, feedforward_post_gain, seed_grad)
    ffpre_low = ffpre_back.astype(low)
    ffpre_tree, gate_back, up_back, ffpre_every, mid_back = feedforward_backward(
        ffpre_low, gate_weight, up_weight, down_weight, mix, gelu_value
    )
    middle_part, grad_three = norm_back(middle, feedforward_gain, mid_back)
    middle_back = seed_grad + middle_part
    attention_pre_back, grad_two = norm_back(attention_pre, attention_post_gain, middle_back)
    pre_tree, projection_back, normed_back = attention_backward(
        attention_pre_back.astype(low),
        cos_table,
        sin_table,
        query_bits,
        key_bits,
        jnp.concatenate([query_weight, key_weight, value_weight]),
        output_weight,
        queries,
        keys,
        values,
        attended,
        mass,
    )
    stream_part, grad_one = norm_back(stream, attention_gain, normed_back)
    input_grad = middle_back + stream_part
    attention_grads = jnp.concatenate(
        [
            dot_tn(projection_back, normed_in),
            dot_tn(attended, pre_tree),
        ]
    ).astype(low)
    attention_grads = lax.psum(attention_grads, "replica").astype(jnp.float32)
    sizes = [query_weight.shape[0], key_weight.shape[0], value_weight.shape[0]]
    query_sum, key_sum, value_sum, output_sum = jnp.split(
        attention_grads, [sizes[0], sizes[0] + sizes[1], sum(sizes)]
    )
    gate_sum, up_sum, down_sum = feedforward_grads(
        mid_every,
        ffpre_every,
        mid_tree,
        ffpre_tree,
        hidden,
        gate_back,
        up_back,
        gate_weight,
        up_weight,
        down_weight,
    )
    extras = jnp.pad(jnp.append(squares, valid_total), (0, model_width - 5))
    smalls = jnp.stack([grad_one, grad_two, grad_three, grad_four, extras])
    smalls = jnp.sum(lax.all_gather(smalls, ("replica", "shard")), axis=0)
    gain_one, gain_two, gain_three, gain_four = smalls[0], smalls[1], smalls[2], smalls[3]
    squares_all, valid_all = smalls[4, :4], smalls[4, 4]
    stream_rms = jnp.sqrt(squares_all / valid_all)
    return (
        result.astype(low),
        input_grad,
        query_sum,
        key_sum,
        value_sum,
        output_sum,
        gate_sum,
        up_sum,
        down_sum,
        gain_one,
        gain_two,
        gain_three,
        gain_four,
        stream_rms,
    )


def solution(mesh):
    heads_fit = mesh.shape["shard"] == HEADS
    return jax.shard_map(
        shards_heads if heads_fit else shards_generic,
        mesh=mesh,
        in_specs=(
            P(("replica", "shard"), None),
            P(("replica", "shard"), None),
            P("replica"),
            P("replica"),
            P("replica", None),
            P("shard", None),
            P("shard", None),
            P("shard", None),
            P("shard", None),
            P("shard", None),
            P("shard", None),
            P("shard", None),
            P(),
            P(),
            P(),
            P(),
        ),
        out_specs=(
            P(("replica", "shard"), None),
            P(("replica", "shard"), None),
            P("shard", None),
            P("shard", None),
            P("shard", None),
            P("shard", None),
            P("shard", None),
            P("shard", None),
            P("shard", None),
            P(),
            P(),
            P(),
            P(),
            P(),
        ),
        check_vma=False,
    )
```

```python
import functools
import math

import jax
import jax.numpy as jnp
from jax import lax
from jax.experimental import pallas as pl
from jax.experimental.pallas import tpu as pltpu
from jax.sharding import PartitionSpec as P

HEADS = 8
KV_HEADS = 4
HEAD = 256


norm_eps = 1e-06
score_cap = 50.0


def norm_rows(stream, norm_gain):
    factor = lax.rsqrt(jnp.mean(stream * stream, axis=-1, keepdims=True) + norm_eps)
    return stream * factor * (1.0 + norm_gain)


def rotate(values, cos_table, sin_table):
    half_width = values.shape[-1] // 2
    turned = jnp.concatenate([-values[..., half_width:], values[..., :half_width]], axis=-1)
    return values * cos_table + turned * sin_table


def rotate_back(gradient, cos_table, sin_table):
    half_width = gradient.shape[-1] // 2
    shifted = gradient * sin_table
    unturned = jnp.concatenate([shifted[..., half_width:], -shifted[..., :half_width]], axis=-1)
    return gradient * cos_table + unturned


def rope_tables(position, head_size):
    half_width = head_size // 2
    frequency = jnp.power(10000.0, -jnp.arange(half_width, dtype=jnp.float32) * 2.0 / head_size)
    angles = position.astype(jnp.float32)[:, None] * frequency[None, :]
    angles = jnp.concatenate([angles, angles], axis=-1)[:, None, :]
    return (jnp.cos(angles), jnp.sin(angles))


def tree_tables(segment, valid_mask, parent):
    labels = jnp.arange(parent.shape[0], dtype=jnp.int32)
    member = (segment[:, None] == labels[None, :]).astype(jnp.int32)
    lengths = jnp.sum(member * valid_mask[:, None], axis=0)
    starts = jnp.sum((segment[:, None] < labels[None, :]).astype(jnp.int32), axis=0)
    parent_of = (parent[:, None] == labels[None, :]).astype(jnp.int32)
    grandparent = jnp.sum(parent_of * parent[None, :], axis=1)
    parent_len = jnp.sum(parent_of * lengths[None, :], axis=1)
    grand_of = (grandparent[:, None] == labels[None, :]).astype(jnp.int32)
    grand_len = jnp.sum(grand_of * lengths[None, :], axis=1)
    offsets = jnp.where(parent != labels, parent_len, 0) + jnp.where(
        grandparent != parent, grand_len, 0
    )
    token_index = jnp.arange(segment.shape[0], dtype=jnp.int32)
    position = jnp.sum(member * (offsets - starts)[None, :], axis=1) + token_index
    parent_tok = jnp.sum(member * parent[None, :], axis=1)
    grand_tok = jnp.sum(member * grandparent[None, :], axis=1)
    return (position, parent_tok, grand_tok)


def allowed_mask(query_index, query_seg, query_parent, query_grand, key_index, key_seg, key_valid):
    lineage = (
        (key_seg[None, :] == query_seg[:, None])
        | (key_seg[None, :] == query_parent[:, None])
        | (key_seg[None, :] == query_grand[:, None])
    )
    earlier = (key_seg[None, :] != query_seg[:, None]) | (key_index[None, :] < query_index[:, None])
    itself = key_index[None, :] == query_index[:, None]
    return itself | (key_valid[None, :] == 1) & lineage & earlier


def softmax_parts(scores, allowed):
    capped = score_cap * jnp.tanh(scores / score_cap)
    held = jnp.where(allowed, capped, -1000000000.0)
    largest = jnp.max(held, axis=-1, keepdims=True)
    raised = jnp.where(allowed, jnp.exp(held - largest), 0.0)
    total_mass = jnp.sum(raised, axis=-1, keepdims=True)
    return (raised / total_mass, largest + jnp.log(total_mass))


def gated_gelu(gate_lin, up_lin):
    return jax.nn.gelu(gate_lin, approximate=True) * up_lin


def collect_attention(query_weight, key_weight, value_weight, output_weight):
    return (
        lax.all_gather(query_weight, "shard", axis=0, tiled=True),
        lax.all_gather(key_weight, "shard", axis=0, tiled=True),
        lax.all_gather(value_weight, "shard", axis=0, tiled=True),
        lax.all_gather(output_weight, "shard", axis=0, tiled=True),
    )


def group_rows(values):
    return lax.all_gather(values, "shard", axis=0, tiled=True)


def group_sums(values):
    return lax.psum_scatter(values, "shard", scatter_dimension=0, tiled=True)


def shards_generic(
    hidden_in,
    cotangent,
    token_segment,
    token_valid,
    segment_parent,
    query_weight,
    key_weight,
    value_weight,
    output_weight,
    gate_weight,
    up_weight,
    down_weight,
    attention_gain,
    attention_post_gain,
    feedforward_gain,
    feedforward_post_gain,
):
    row_count, model_width = hidden_in.shape
    group_size = HEADS // KV_HEADS
    row_start = lax.axis_index("shard") * row_count
    tree_size = token_segment.shape[0]
    position, parent_tok, grand_tok = tree_tables(token_segment, token_valid, segment_parent[0])
    key_index = jnp.arange(tree_size, dtype=jnp.int32)

    def own_rows(table):
        return lax.dynamic_slice_in_dim(table, row_start, row_count)

    allowed = allowed_mask(
        own_rows(key_index),
        own_rows(token_segment),
        own_rows(parent_tok),
        own_rows(grand_tok),
        key_index,
        token_segment,
        token_valid,
    )
    mask_full = allowed[None, None]
    cos_table, sin_table = rope_tables(own_rows(position), HEAD)
    query_scale = HEAD ** (-0.5)
    valid_rows = own_rows(token_valid).astype(jnp.float32)
    stream = hidden_in.astype(jnp.float32)
    query_all, key_all, value_all, output_all = collect_attention(
        query_weight, key_weight, value_weight, output_weight
    )
    normed_in = norm_rows(stream, attention_gain).astype(jnp.bfloat16)
    query_lin = jnp.einsum("td,qd->tq", normed_in, query_all, preferred_element_type=jnp.float32)
    key_lin = jnp.einsum("td,qd->tq", normed_in, key_all, preferred_element_type=jnp.float32)
    value_lin = jnp.einsum("td,qd->tq", normed_in, value_all, preferred_element_type=jnp.float32)
    queries = (
        rotate(query_lin.reshape(row_count, HEADS, HEAD), cos_table, sin_table) * query_scale
    ).astype(jnp.bfloat16)
    keys_own = (
        rotate(key_lin.reshape(row_count, KV_HEADS, HEAD), cos_table, sin_table)
        .astype(jnp.bfloat16)
        .reshape(row_count, KV_HEADS * HEAD)
    )
    values_own = value_lin.astype(jnp.bfloat16)
    key_tree, value_tree = (
        lax.all_gather(keys_own, "shard", axis=0, tiled=True),
        lax.all_gather(values_own, "shard", axis=0, tiled=True),
    )
    query_groups = queries.reshape(row_count, KV_HEADS, group_size, HEAD)
    key_groups = key_tree.reshape(tree_size, KV_HEADS, HEAD)
    value_groups = value_tree.reshape(tree_size, KV_HEADS, HEAD)
    scores = jnp.einsum(
        "qgrd,kgd->grqk", query_groups, key_groups, preferred_element_type=jnp.float32
    )
    probs, log_total = softmax_parts(scores, mask_full)
    attended = jnp.einsum(
        "grqk,kgd->qgrd",
        probs.astype(jnp.bfloat16),
        value_groups,
        preferred_element_type=jnp.float32,
    )
    attended = attended.astype(jnp.bfloat16).reshape(row_count, HEADS * HEAD)
    attention_pre = jnp.dot(attended, output_all, preferred_element_type=jnp.float32)
    attention_branch = norm_rows(attention_pre, attention_post_gain)
    middle = stream + attention_branch
    normed_mid = norm_rows(middle, feedforward_gain).astype(jnp.bfloat16)
    mid_tree = group_rows(normed_mid)
    gate_lin = jnp.einsum("td,fd->tf", mid_tree, gate_weight, preferred_element_type=jnp.float32)
    up_lin = jnp.einsum("td,fd->tf", mid_tree, up_weight, preferred_element_type=jnp.float32)
    hidden = gated_gelu(gate_lin, up_lin).astype(jnp.bfloat16)
    feedforward_pre = group_sums(jnp.dot(hidden, down_weight, preferred_element_type=jnp.float32))
    feedforward_branch = norm_rows(feedforward_pre, feedforward_post_gain)
    result = middle + feedforward_branch
    squares = jnp.stack(
        [
            jnp.sum(valid_rows[:, None] * summand * summand)
            for summand in (stream, attention_branch, feedforward_branch, result)
        ]
    )
    valid_total = jnp.sum(valid_rows) * model_width
    squares_all, valid_all = lax.psum((squares, valid_total), ("replica", "shard"))
    seed_grad = cotangent.astype(jnp.float32) * valid_rows[:, None]
    unused_four, pull_four = jax.vjp(norm_rows, feedforward_pre, feedforward_post_gain)
    ffpre_back, grad_four = pull_four(seed_grad)
    ffpre_low = ffpre_back.astype(jnp.bfloat16)
    ffpre_tree = group_rows(ffpre_low)
    hidden_back = jnp.einsum(
        "td,fd->tf", ffpre_tree, down_weight, preferred_element_type=jnp.float32
    ).astype(jnp.bfloat16)
    unused_glu, pull_glu = jax.vjp(gated_gelu, gate_lin, up_lin)
    gate_back, up_back = pull_glu(hidden_back.astype(jnp.float32))
    gate_back = gate_back.astype(jnp.bfloat16)
    up_back = up_back.astype(jnp.bfloat16)
    mid_terms = jnp.dot(gate_back, gate_weight, preferred_element_type=jnp.float32) + jnp.dot(
        up_back, up_weight, preferred_element_type=jnp.float32
    )
    mid_back = group_sums(mid_terms)
    gate_grad = jnp.einsum("tf,td->fd", gate_back, mid_tree, preferred_element_type=jnp.float32)
    up_grad = jnp.einsum("tf,td->fd", up_back, mid_tree, preferred_element_type=jnp.float32)
    down_grad = jnp.einsum("tf,td->fd", hidden, ffpre_tree, preferred_element_type=jnp.float32)
    unused_three, pull_three = jax.vjp(norm_rows, middle, feedforward_gain)
    middle_part, grad_three = pull_three(mid_back)
    middle_back = seed_grad + middle_part
    unused_two, pull_two = jax.vjp(norm_rows, attention_pre, attention_post_gain)
    attention_pre_back, grad_two = pull_two(middle_back)
    pre_low = attention_pre_back.astype(jnp.bfloat16)
    query_all, key_all, value_all, output_all = collect_attention(
        query_weight, key_weight, value_weight, output_weight
    )
    attended_back = jnp.einsum(
        "td,qd->tq", pre_low, output_all, preferred_element_type=jnp.float32
    ).astype(jnp.bfloat16)
    scores = jnp.einsum(
        "qgrd,kgd->grqk", query_groups, key_groups, preferred_element_type=jnp.float32
    )
    tanh_value = jnp.tanh(scores / score_cap)
    probs_back = jnp.where(
        mask_full,
        jnp.exp(jnp.where(mask_full, score_cap * tanh_value - log_total, -1000000000.0)),
        0.0,
    )
    back_groups = attended_back.reshape(row_count, KV_HEADS, group_size, HEAD)
    prob_grads = jnp.einsum(
        "qgrd,kgd->grqk", back_groups, value_groups, preferred_element_type=jnp.float32
    )
    inner_sum = jnp.sum(probs_back * prob_grads, axis=-1, keepdims=True)
    score_back = (probs_back * (prob_grads - inner_sum) * (1.0 - tanh_value * tanh_value)).astype(
        jnp.bfloat16
    )
    query_back = jnp.einsum(
        "grqk,kgd->qgrd", score_back, key_groups, preferred_element_type=jnp.float32
    ).reshape(row_count, HEADS, HEAD)
    key_back = jnp.einsum(
        "grqk,qgrd->kgd", score_back, query_groups, preferred_element_type=jnp.float32
    ).reshape(tree_size, KV_HEADS * HEAD)
    value_back = jnp.einsum(
        "grqk,qgrd->kgd",
        probs_back.astype(jnp.bfloat16),
        back_groups,
        preferred_element_type=jnp.float32,
    ).reshape(tree_size, KV_HEADS * HEAD)
    key_sum, value_sum = (
        lax.psum_scatter(key_back, "shard", scatter_dimension=0, tiled=True),
        lax.psum_scatter(value_back, "shard", scatter_dimension=0, tiled=True),
    )
    query_low = (
        rotate_back(query_back * query_scale, cos_table, sin_table)
        .astype(jnp.bfloat16)
        .reshape(row_count, HEADS * HEAD)
    )
    key_low = (
        rotate_back(key_sum.reshape(row_count, KV_HEADS, HEAD), cos_table, sin_table)
        .astype(jnp.bfloat16)
        .reshape(row_count, KV_HEADS * HEAD)
    )
    value_low = value_sum.astype(jnp.bfloat16)
    normed_back = (
        jnp.dot(query_low, query_all, preferred_element_type=jnp.float32)
        + jnp.dot(key_low, key_all, preferred_element_type=jnp.float32)
        + jnp.dot(value_low, value_all, preferred_element_type=jnp.float32)
    )
    output_local = jnp.einsum("tq,td->qd", attended, pre_low, preferred_element_type=jnp.float32)
    query_local = jnp.einsum("tq,td->qd", query_low, normed_in, preferred_element_type=jnp.float32)
    key_local = jnp.einsum("tq,td->qd", key_low, normed_in, preferred_element_type=jnp.float32)
    value_local = jnp.einsum("tq,td->qd", value_low, normed_in, preferred_element_type=jnp.float32)
    query_part, key_part, value_part, output_part = (
        lax.psum_scatter(query_local, "shard", scatter_dimension=0, tiled=True),
        lax.psum_scatter(key_local, "shard", scatter_dimension=0, tiled=True),
        lax.psum_scatter(value_local, "shard", scatter_dimension=0, tiled=True),
        lax.psum_scatter(output_local, "shard", scatter_dimension=0, tiled=True),
    )
    unused_one, pull_one = jax.vjp(norm_rows, stream, attention_gain)
    stream_part, grad_one = pull_one(normed_back)
    input_grad = middle_back + stream_part
    query_sum, key_total, value_total, output_sum, gate_sum, up_sum, down_sum = lax.psum(
        (query_part, key_part, value_part, output_part, gate_grad, up_grad, down_grad), "replica"
    )
    gain_one, gain_two, gain_three, gain_four = lax.psum(
        (grad_one, grad_two, grad_three, grad_four), ("replica", "shard")
    )
    stream_rms = jnp.sqrt(squares_all / valid_all)
    return (
        result.astype(jnp.bfloat16),
        input_grad,
        query_sum,
        key_total,
        value_total,
        output_sum,
        gate_sum,
        up_sum,
        down_sum,
        gain_one,
        gain_two,
        gain_three,
        gain_four,
        stream_rms,
    )


def norm_factor(stream):
    return lax.rsqrt(jnp.mean(stream * stream, axis=-1, keepdims=True) + norm_eps)


def norm_back(stream, norm_gain, gradient):
    factor = norm_factor(stream)
    weighted = gradient * (1.0 + norm_gain)
    inner = jnp.mean(weighted * stream, axis=-1, keepdims=True)
    back = factor * weighted - stream * (factor * factor * factor * inner)
    return back, gradient * stream * factor


def dot_nt(left, right):
    return lax.dot_general(
        left, right, (((1,), (1,)), ((), ())), preferred_element_type=jnp.float32
    )


def dot_nn(left, right):
    return lax.dot_general(
        left, right, (((1,), (0,)), ((), ())), preferred_element_type=jnp.float32
    )


def dot_tn(left, right):
    return lax.dot_general(
        left, right, (((0,), (0,)), ((), ())), preferred_element_type=jnp.float32
    )


def sum_low(values):
    return lax.psum_scatter(
        values.astype(jnp.bfloat16), "shard", scatter_dimension=0, tiled=True
    ).astype(jnp.float32)


def gelu_parts(gate_lin):
    root = math.sqrt(2.0 / math.pi)
    square = gate_lin * gate_lin
    tanh_value = jnp.tanh(root * gate_lin * (1.0 + 0.044715 * square))
    half_up = 0.5 * (1.0 + tanh_value)
    slope = half_up + 0.5 * gate_lin * (1.0 - tanh_value * tanh_value) * root * (
        1.0 + 3.0 * 0.044715 * square
    )
    return gate_lin * half_up, slope


MESH_ID = pl.DeviceIdType.MESH
VMEM_BYTES = 62 * 2**20
ROOT = math.sqrt(2.0 / math.pi)


class Plane:
    def __init__(self):
        self.me = lax.axis_index("shard")
        core = lax.rem(self.me, 2)
        x = lax.rem(lax.div(self.me, 2), 2)
        y = lax.div(self.me, 4)
        self.core = core
        self.own_chip = 2 * y + x
        self.x_chip = 2 * y + 1 - x
        self.y_chip = 2 * (1 - y) + x
        self.diag_chip = 2 * (1 - y) + 1 - x
        self.mate = self.me + 1 - 2 * core
        self.x_dev = 2 * self.x_chip + core
        self.y_dev = 2 * self.y_chip + core
        self.diag_dev = 2 * self.diag_chip + core

    def near(self):
        return [{"shard": dev} for dev in (self.mate, self.x_dev, self.y_dev)]


class Wires:
    def __init__(self, send_sem, recv_sem):
        self.send_sem, self.recv_sem = send_sem, recv_sem
        self.sent = []

    def send(self, source, target, device):
        at = len(self.sent)
        copy = pltpu.make_async_remote_copy(
            src_ref=source,
            dst_ref=target,
            send_sem=self.send_sem.at[at],
            recv_sem=self.recv_sem.at[at],
            device_id=device if isinstance(device, dict) else {"shard": device},
            device_id_type=MESH_ID,
        )
        copy.start()
        self.sent.append(copy)
        return copy

    def finish(self):
        for copy in self.sent:
            copy.wait_send()


def greet(devices):
    barrier = pltpu.get_barrier_semaphore()
    for device in devices:
        pl.semaphore_signal(barrier, inc=1, device_id=device, device_id_type=MESH_ID)
    pl.semaphore_wait(barrier, len(devices))


def block_rows(ref, start, size, step=16):
    return ref.at[pl.ds(pl.multiple_of(start, step), size)]


def add_row(sums, at, term):
    sums[at : at + 1, :] += jnp.sum(term, axis=0, keepdims=True)


def by_rows(count, body, size=32):
    def step(at, carry):
        body(pl.ds(pl.multiple_of(at * size, size), size))
        return carry

    lax.fori_loop(0, count // size, step, 0)


def column_tile(width):
    return max(t for t in range(128, 769, 128) if width % t == 0)


def by_columns(width, body):
    tile = column_tile(width)

    def step(at, carry):
        body(pl.ds(pl.multiple_of(at * tile, 128), tile))
        return carry

    lax.fori_loop(0, width // tile, step, 0)


def gather_tree(wires, plane, own, tree, rows, use):
    half = rows // 2

    def part(dev, start, size):
        return block_rows(tree, dev * rows + start, size)

    def own_part(start, size):
        return own.at[pl.ds(start, size)]

    me, mate = plane.me, plane.mate
    first_x = wires.send(own_part(0, half), part(me, 0, half), plane.x_dev)
    first_y = wires.send(own_part(half, half), part(me, half, half), plane.y_dev)
    to_mate = wires.send(own_part(0, rows), part(me, 0, rows), mate)
    rest_x = wires.send(own_part(half, half), part(me, half, half), plane.x_dev)
    rest_y = wires.send(own_part(0, half), part(me, 0, half), plane.y_dev)
    to_mate.wait_recv()
    use(plane.own_chip)
    first_x.wait_recv()
    turn_y = wires.send(part(plane.x_dev, 0, half), part(plane.x_dev, 0, half), plane.y_dev)
    first_y.wait_recv()
    turn_x = wires.send(part(plane.y_dev, half, half), part(plane.y_dev, half, half), plane.x_dev)
    rest_x.wait_recv()
    mate_x = wires.send(part(plane.x_dev, 0, rows), part(plane.x_dev, 0, rows), mate)
    rest_y.wait_recv()
    mate_y = wires.send(part(plane.y_dev, 0, rows), part(plane.y_dev, 0, rows), mate)
    mate_x.wait_recv()
    use(plane.x_chip)
    turn_y.wait_recv()
    turn_x.wait_recv()
    mate_diag = wires.send(part(plane.diag_dev, 0, rows), part(plane.diag_dev, 0, rows), mate)
    mate_y.wait_recv()
    use(plane.y_chip)
    mate_diag.wait_recv()
    use(plane.diag_chip)


GATHER_COPIES = 10
DIAG, SIDE_X, SIDE_Y, OWN = range(4)


def scatter_scratch(rows, width):
    half = rows // 2
    low = jnp.bfloat16
    return [
        pltpu.VMEM((3, rows, width), jnp.float32),
        pltpu.VMEM((2 * rows, column_tile(width)), jnp.float32),
        pltpu.VMEM((2, rows, width), low),
        pltpu.VMEM((4, rows, width), low),
        pltpu.VMEM((3, half, width), low),
        pltpu.VMEM((3, half, width), low),
        pltpu.VMEM((3, half, width), low),
        pltpu.VMEM((3, half, width), low),
    ]


class Scatter:
    def __init__(self, wires, plane, scratch, product, total, order, loads=()):
        self.loads = list(loads)
        self.wires, self.plane, self.product, self.total = wires, plane, product, total
        self.sums, self.piece, self.mate_out, self.mate_in = scratch[:4]
        self.x_out, self.x_in, self.y_out, self.y_in = scratch[4:]
        self.order = order
        self.slots = {place: (0, 1, 2, 0)[at] for at, place in enumerate(order)}
        if order[0] == OWN:
            self.slots[SIDE_Y] = self.slots[DIAG]
        self.rows, self.width = total.shape
        self.half = self.rows // 2
        self.to_mate = {}

    def produce(self, place):
        plane, rows = self.plane, self.rows
        chip = (plane.diag_chip, plane.x_chip, plane.y_chip, plane.own_chip)[place]
        slot, at = self.slots[place], self.order.index(place)
        out_slot = at % 2
        if at >= 2:
            self.to_mate[self.order[at - 2]].wait_send()
        while self.loads:
            self.loads.pop().wait()

        def tile(columns):
            self.piece[...] = self.product(chip, columns)
            self.sums[slot, :, columns] = self.piece[block_at(plane.core * rows, rows), :]
            self.mate_out[out_slot, :, columns] = self.piece[
                block_at((1 - plane.core) * rows, rows), :
            ].astype(jnp.bfloat16)

        by_columns(self.width, tile)
        self.to_mate[place] = self.wires.send(
            self.mate_out.at[out_slot], self.mate_in.at[place], plane.mate
        )

    def low_part(self, out, out_slot, place, start, more=None):
        def step(at):
            there = pl.ds(pl.multiple_of(start + at.start, 16), at.size)
            value = self.sums[self.slots[place], there, :] + self.mate_in[
                place, there, :
            ].astype(jnp.float32)
            if more is not None:
                value += more[0, at, :].astype(jnp.float32)
            out[out_slot, at, :] = value.astype(jnp.bfloat16)

        by_rows(self.half, step)

    def to_x(self, slot):
        return self.wires.send(self.x_out.at[slot], self.x_in.at[slot], self.plane.x_dev)

    def to_y(self, slot):
        return self.wires.send(self.y_out.at[slot], self.y_in.at[slot], self.plane.y_dev)

    def send_diag(self):
        self.to_mate[DIAG].wait_recv()
        self.low_part(self.x_out, 0, DIAG, 0)
        self.x_first = self.to_x(0)
        self.low_part(self.y_out, 0, DIAG, self.half)
        self.y_first = self.to_y(0)

    def send_x(self):
        self.to_mate[SIDE_X].wait_recv()
        self.low_part(self.x_out, 1, SIDE_X, 0)
        self.x_next = self.to_x(1)

    def send_y(self):
        self.to_mate[SIDE_Y].wait_recv()
        self.low_part(self.y_out, 1, SIDE_Y, self.half)
        self.y_next = self.to_y(1)

    def turn(self):
        self.y_first.wait_recv()
        self.low_part(self.x_out, 2, SIDE_X, self.half, self.y_in)
        self.x_last = self.to_x(2)
        self.x_first.wait_recv()
        self.low_part(self.y_out, 2, SIDE_Y, 0, self.x_in)
        self.y_last = self.to_y(2)

    def finish(self):
        self.to_mate[OWN].wait_recv()
        late = [self.x_next, self.y_next, self.x_last, self.y_last]
        for copy in late:
            copy.wait_recv()
        for start, x_slot, y_slot in ((0, 1, 2), (self.half, 2, 1)):

            def step(at, start=start, x_slot=x_slot, y_slot=y_slot):
                there = pl.ds(pl.multiple_of(start + at.start, 16), at.size)
                self.total[there, :] = (
                    self.sums[self.slots[OWN], there, :]
                    + self.mate_in[OWN, there, :].astype(jnp.float32)
                    + self.x_in[x_slot, at, :].astype(jnp.float32)
                    + self.y_in[y_slot, at, :].astype(jnp.float32)
                )

            by_rows(self.half, step)
        for copy in [self.x_first, self.y_first] + late:
            copy.wait_send()
        for place in self.order[2:]:
            self.to_mate[place].wait_send()


def scatter_sum(wires, plane, scratch, product, total, before=lambda chip: None, meanwhile=()):
    scatter = Scatter(wires, plane, scratch, product, total, (DIAG, SIDE_X, SIDE_Y, OWN))
    work = iter(tuple(meanwhile) + (lambda: None,) * 2)
    before(plane.diag_chip)
    scatter.produce(DIAG)
    before(plane.x_chip)
    scatter.produce(SIDE_X)
    scatter.send_diag()
    before(plane.y_chip)
    scatter.produce(SIDE_Y)
    scatter.send_x()
    before(plane.own_chip)
    scatter.produce(OWN)
    scatter.send_y()
    next(work)()
    scatter.turn()
    next(work)()
    scatter.finish()


def gather_and_scatter(wires, plane, own, tree, rows, use, scatter):
    half = rows // 2

    def part(dev, start, size):
        return block_rows(tree, dev * rows + start, size)

    def own_part(start, size):
        return own.at[pl.ds(start, size)]

    def onward(dev, start, size, device):
        return wires.send(part(dev, start, size), part(dev, start, size), device)

    me, mate, x_dev, y_dev = plane.me, plane.mate, plane.x_dev, plane.y_dev
    first_x = wires.send(own_part(0, half), part(me, 0, half), x_dev)
    first_y = wires.send(own_part(half, half), part(me, half, half), y_dev)
    to_mate = wires.send(own_part(0, rows), part(me, 0, rows), mate)
    to_mate.wait_recv()
    use(plane.own_chip)
    first_x.wait_recv()
    turn_y = onward(x_dev, 0, half, y_dev)
    first_y.wait_recv()
    turn_x = onward(y_dev, half, half, x_dev)
    rest_x = wires.send(own_part(half, half), part(me, half, half), x_dev)
    rest_y = wires.send(own_part(0, half), part(me, 0, half), y_dev)
    scatter.produce(OWN)
    turn_y.wait_recv()
    turn_x.wait_recv()
    mate_diag = onward(plane.diag_dev, 0, rows, mate)
    mate_diag.wait_recv()
    use(plane.diag_chip)
    rest_x.wait_recv()
    mate_x = onward(x_dev, 0, rows, mate)
    rest_y.wait_recv()
    mate_y = onward(y_dev, 0, rows, mate)
    scatter.produce(DIAG)
    mate_x.wait_recv()
    use(plane.x_chip)
    scatter.send_diag()
    scatter.produce(SIDE_X)
    mate_y.wait_recv()
    use(plane.y_chip)
    scatter.send_x()
    scatter.produce(SIDE_Y)
    copies = [first_x, first_y, to_mate, turn_y, turn_x, rest_x, rest_y, mate_diag, mate_x, mate_y]
    for copy in copies:
        copy.wait_send()
    scatter.send_y()
    scatter.turn()
    scatter.finish()


SCATTER_COPIES = 10


def block_at(start, size):
    return pl.ds(pl.multiple_of(start, 16), size)


def load(source, target, sem):
    copy = pltpu.make_async_copy(source, target, sem)
    copy.start()
    return copy


def replica_steps(replicas, near):
    return [step for step in range(1, replicas) if (min(step, replicas - step) == 1) == near]


def replica_device(replicas, step):
    return {"replica": lax.rem(lax.axis_index("replica") + step, replicas)}


def send_over(wires, source, target, replicas, steps):
    return [
        wires.send(
            source, target.at[steps.index(replicas - step)], replica_device(replicas, step)
        )
        for step in steps
    ]


def forward_kernel(
    replicas,
    own,
    middle,
    cotangent,
    valid,
    gain,
    gate_hbm,
    up_hbm,
    down_hbm,
    tree_out,
    hidden_out,
    mix_out,
    gelu_out,
    every_out,
    block_out,
    back_out,
    sums_out,
    total,
    tree,
    gate_w,
    up_w,
    down_w,
    hidden,
    mix,
    gelu,
    gate_lin,
    up_lin,
    send_sem,
    recv_sem,
    local_sem,
    *scratch,
):
    plane = Plane()
    rows = own.shape[0]
    wires = Wires(send_sem, recv_sem)
    loads = [
        load(gate_hbm, gate_w, local_sem.at[0]),
        load(up_hbm, up_w, local_sem.at[1]),
        load(down_hbm, down_w, local_sem.at[2]),
    ]
    steps = replica_steps(replicas, True)
    greet(plane.near() + [replica_device(replicas, step) for step in steps])
    tree[block_at(plane.me * rows, rows), :] = own[...]
    stores = []

    def use(chip):
        order = len(stores) // 3
        slot = order % 2
        if order == 0:
            loads[0].wait()
            loads[1].wait()
        if order >= 2:
            stores[3 * (order - 2) + 1].wait()
            stores[3 * (order - 2) + 2].wait()
        there = block_at(chip * 2 * rows, 2 * rows)
        gate_lin[...] = dot_nt(tree[there, :], gate_w[...])
        up_lin[...] = dot_nt(tree[there, :], up_w[...])

        def step(at):
            gelu_value, slope = gelu_parts(gate_lin[at, :])
            up_value = up_lin[at, :]
            mix[slot, at, :] = (up_value * slope).astype(jnp.bfloat16)
            gelu[slot, at, :] = gelu_value.astype(jnp.bfloat16)
            hidden[block_at(chip * 2 * rows + at.start, at.size), :] = (
                gelu_value * up_value
            ).astype(jnp.bfloat16)

        by_rows(2 * rows, step, 16)
        base = 3 + 3 * order
        stores.append(load(hidden.at[there], hidden_out.at[there], local_sem.at[base]))
        stores.append(load(mix.at[slot], mix_out.at[there], local_sem.at[base + 1]))
        stores.append(load(gelu.at[slot], gelu_out.at[there], local_sem.at[base + 2]))

    over = send_over(wires, own, every_out, replicas, steps)

    def product(chip, columns):
        return dot_nn(hidden[block_at(chip * 2 * rows, 2 * rows), :], down_w[:, columns])

    scatter = Scatter(
        wires, plane, scratch, product, total, (OWN, DIAG, SIDE_X, SIDE_Y), loads[2:]
    )
    gather_and_scatter(wires, plane, own, tree, rows, use, scatter)
    tree_store = load(tree, tree_out, local_sem.at[15])
    sums_out[...] = jnp.zeros_like(sums_out)

    def finish(at):
        value = total[at, :]
        gradient = cotangent[at, :].astype(jnp.float32) * valid[at, :]
        branch = norm_rows(value, gain[...])
        result = middle[at, :] + branch
        block_out[at, :] = result.astype(jnp.bfloat16)
        back, gain_terms = norm_back(value, gain[...], gradient)
        back_out[at, :] = back.astype(jnp.bfloat16)
        add_row(sums_out, 0, gain_terms)
        add_row(sums_out, 1, valid[at, :] * branch * branch)
        add_row(sums_out, 2, valid[at, :] * result * result)

    by_rows(rows, finish)
    for copy in over:
        copy.wait()
    for copy in stores[0:1] + stores[3:4] + stores[6:] + [tree_store]:
        copy.wait()


def any_specs(count):
    return [pl.BlockSpec(memory_space=pl.ANY)] * count


def vmem_specs(count):
    return [pl.BlockSpec(memory_space=pltpu.VMEM)] * count


def remote_params(identity):
    return pltpu.CompilerParams(
        collective_id=identity, has_side_effects=True, vmem_limit_bytes=VMEM_BYTES
    )


def feedforward_forward(
    own, middle, cotangent, valid, gain, gate_weight, up_weight, down_weight
):
    rows, width = own.shape
    units = gate_weight.shape[0]
    replicas, count = lax.axis_size("replica"), lax.axis_size("shard")
    tree_rows = count * rows
    low, full = jnp.bfloat16, jnp.float32
    copies = GATHER_COPIES + SCATTER_COPIES + replicas - 1
    return pl.pallas_call(
        functools.partial(forward_kernel, replicas),
        out_shape=(
            jax.ShapeDtypeStruct((tree_rows, width), low),
            jax.ShapeDtypeStruct((tree_rows, units), low),
            jax.ShapeDtypeStruct((tree_rows, units), low),
            jax.ShapeDtypeStruct((tree_rows, units), low),
            jax.ShapeDtypeStruct((len(replica_steps(replicas, True)), rows, width), low),
            jax.ShapeDtypeStruct((rows, width), low),
            jax.ShapeDtypeStruct((rows, width), low),
            jax.ShapeDtypeStruct((8, width), full),
        ),
        in_specs=vmem_specs(5) + any_specs(3),
        out_specs=tuple(any_specs(5) + vmem_specs(3)),
        scratch_shapes=[
            pltpu.VMEM((rows, width), full),
            pltpu.VMEM((tree_rows, width), low),
            pltpu.VMEM((units, width), low),
            pltpu.VMEM((units, width), low),
            pltpu.VMEM((units, width), low),
            pltpu.VMEM((tree_rows, units), low),
            pltpu.VMEM((2, 2 * rows, units), low),
            pltpu.VMEM((2, 2 * rows, units), low),
            pltpu.VMEM((2 * rows, units), full),
            pltpu.VMEM((2 * rows, units), full),
            pltpu.SemaphoreType.DMA((copies,)),
            pltpu.SemaphoreType.DMA((copies,)),
            pltpu.SemaphoreType.DMA((16,)),
        ]
        + scatter_scratch(rows, width),
        compiler_params=remote_params(1),
        cost_estimate=pl.CostEstimate(
            flops=6 * tree_rows * units * width, bytes_accessed=40 * 2**20, transcendentals=0
        ),
    )(own, middle, cotangent, valid, gain[None], gate_weight, up_weight, down_weight)


def backward_kernel(
    replicas,
    own,
    middle,
    attention_pre,
    cotangent,
    valid,
    gain,
    post_gain,
    mid_own,
    gate_hbm,
    up_hbm,
    down_hbm,
    mix_hbm,
    gelu_hbm,
    tree_out,
    gate_out,
    up_out,
    every_out,
    middle_out,
    back_out,
    sums_out,
    total,
    tree,
    gate_w,
    up_w,
    down_w,
    gate_back,
    up_back,
    mix,
    gelu,
    hidden_back,
    send_sem,
    recv_sem,
    local_sem,
    *scratch,
):
    plane = Plane()
    rows = own.shape[0]
    wires = Wires(send_sem, recv_sem)
    chips = [plane.own_chip, plane.diag_chip, plane.x_chip, plane.y_chip]

    def fetch(order):
        there = block_at(chips[order] * 2 * rows, 2 * rows)
        return [
            load(mix_hbm.at[there], mix.at[order % 2], local_sem.at[3 + 2 * order]),
            load(gelu_hbm.at[there], gelu.at[order % 2], local_sem.at[4 + 2 * order]),
        ]

    loads = [load(down_hbm, down_w, local_sem.at[2])]
    fetched = [fetch(0), fetch(1)]
    loads += [
        load(gate_hbm, gate_w, local_sem.at[0]),
        load(up_hbm, up_w, local_sem.at[1]),
    ]
    steps = replica_steps(replicas, False)
    greet(plane.near() + [replica_device(replicas, step) for step in steps])
    tree[block_at(plane.me * rows, rows), :] = own[...]
    stores = []

    def use(chip):
        order = len(stores) // 2
        slot = order % 2
        if order == 0:
            loads[0].wait()
        there = block_at(chip * 2 * rows, 2 * rows)
        hidden_back[...] = dot_nt(tree[there, :], down_w[...])
        for copy in fetched[order]:
            copy.wait()

        def step(at):
            value = hidden_back[at, :].astype(jnp.bfloat16).astype(jnp.float32)
            here = block_at(chip * 2 * rows + at.start, at.size)
            gate_back[here, :] = (value * mix[slot, at, :].astype(jnp.float32)).astype(jnp.bfloat16)
            up_back[here, :] = (value * gelu[slot, at, :].astype(jnp.float32)).astype(jnp.bfloat16)

        by_rows(2 * rows, step, 16)
        if order + 2 < 4:
            fetched.append(fetch(order + 2))
        base = 11 + 2 * order
        stores.append(load(gate_back.at[there], gate_out.at[there], local_sem.at[base]))
        stores.append(load(up_back.at[there], up_out.at[there], local_sem.at[base + 1]))

    over = send_over(wires, mid_own, every_out, replicas, steps)

    def product(chip, columns):
        there = block_at(chip * 2 * rows, 2 * rows)
        return dot_nn(gate_back[there, :], gate_w[:, columns]) + dot_nn(
            up_back[there, :], up_w[:, columns]
        )

    scatter = Scatter(
        wires, plane, scratch, product, total, (OWN, DIAG, SIDE_X, SIDE_Y), loads[1:]
    )
    gather_and_scatter(wires, plane, own, tree, rows, use, scatter)
    tree_store = load(tree, tree_out, local_sem.at[19])
    sums_out[...] = jnp.zeros_like(sums_out)

    def finish(at):
        back, gain_terms = norm_back(middle[at, :], gain[...], total[at, :])
        back += cotangent[at, :].astype(jnp.float32) * valid[at, :]
        middle_out[at, :] = back
        add_row(sums_out, 0, gain_terms)
        back, gain_terms = norm_back(attention_pre[at, :], post_gain[...], back)
        back_out[at, :] = back.astype(jnp.bfloat16)
        add_row(sums_out, 1, gain_terms)

    by_rows(rows, finish)
    for copy in over:
        copy.wait()
    for copy in stores + [tree_store]:
        copy.wait()


def feedforward_backward(
    own,
    middle,
    attention_pre,
    cotangent,
    valid,
    gain,
    post_gain,
    mid_own,
    gate_weight,
    up_weight,
    down_weight,
    mix,
    gelu,
):
    rows, width = own.shape
    units = gate_weight.shape[0]
    replicas, count = lax.axis_size("replica"), lax.axis_size("shard")
    tree_rows = count * rows
    low, full = jnp.bfloat16, jnp.float32
    copies = GATHER_COPIES + SCATTER_COPIES + replicas - 1
    return pl.pallas_call(
        functools.partial(backward_kernel, replicas),
        out_shape=(
            jax.ShapeDtypeStruct((tree_rows, width), low),
            jax.ShapeDtypeStruct((tree_rows, units), low),
            jax.ShapeDtypeStruct((tree_rows, units), low),
            jax.ShapeDtypeStruct((len(replica_steps(replicas, False)), rows, width), low),
            jax.ShapeDtypeStruct((rows, width), full),
            jax.ShapeDtypeStruct((rows, width), low),
            jax.ShapeDtypeStruct((8, width), full),
        ),
        in_specs=vmem_specs(7) + any_specs(6),
        out_specs=tuple(any_specs(4) + vmem_specs(3)),
        scratch_shapes=[
            pltpu.VMEM((rows, width), full),
            pltpu.VMEM((tree_rows, width), low),
            pltpu.VMEM((units, width), low),
            pltpu.VMEM((units, width), low),
            pltpu.VMEM((units, width), low),
            pltpu.VMEM((tree_rows, units), low),
            pltpu.VMEM((tree_rows, units), low),
            pltpu.VMEM((2, 2 * rows, units), low),
            pltpu.VMEM((2, 2 * rows, units), low),
            pltpu.VMEM((2 * rows, units), full),
            pltpu.SemaphoreType.DMA((copies,)),
            pltpu.SemaphoreType.DMA((copies,)),
            pltpu.SemaphoreType.DMA((20,)),
        ]
        + scatter_scratch(rows, width),
        compiler_params=remote_params(2),
        cost_estimate=pl.CostEstimate(
            flops=6 * tree_rows * units * width, bytes_accessed=40 * 2**20, transcendentals=0
        ),
    )(
        own,
        middle,
        attention_pre,
        cotangent,
        valid,
        gain[None],
        post_gain[None],
        mid_own,
        gate_weight,
        up_weight,
        down_weight,
        mix,
        gelu,
    )


class Copy:
    def __init__(self, build):
        self.build = build

    def start(self):
        self.build().start()

    def wait_recv(self):
        self.build().wait_recv()

    def wait_send(self):
        self.build().wait_send()


class PlaneGather:
    def __init__(self, plane, own, tree, rows, send_sem, recv_sem, local_sem, base):
        half = rows // 2
        me, mate, x_dev, y_dev = plane.me, plane.mate, plane.x_dev, plane.y_dev
        diag = plane.diag_dev
        self.started = []

        def part(dev, start, size):
            return block_rows(tree, dev * rows + start, size)

        def copy(source, target, device):
            at = base + len(self.started)

            def build():
                return pltpu.make_async_remote_copy(
                    src_ref=source(),
                    dst_ref=target(),
                    send_sem=send_sem.at[at],
                    recv_sem=recv_sem.at[at],
                    device_id={"shard": device},
                    device_id_type=MESH_ID,
                )

            self.started.append(Copy(build))
            return self.started[-1]

        def from_own(start, size, device):
            return copy(
                lambda: own().at[pl.ds(start, size)], lambda: part(me, start, size), device
            )

        def onward(dev, start, size, device):
            return copy(lambda: part(dev, start, size), lambda: part(dev, start, size), device)

        self.first_x = from_own(0, half, x_dev)
        self.first_y = from_own(half, half, y_dev)
        self.to_mate = from_own(0, rows, mate)
        self.rest_x = from_own(half, half, x_dev)
        self.rest_y = from_own(0, half, y_dev)
        self.turn_y = onward(x_dev, 0, half, y_dev)
        self.turn_x = onward(y_dev, half, half, x_dev)
        self.mate_x = onward(x_dev, 0, rows, mate)
        self.mate_y = onward(y_dev, 0, rows, mate)
        self.mate_diag = onward(diag, 0, rows, mate)
        self.local = lambda: pltpu.make_async_copy(own(), part(me, 0, rows), local_sem)

    def begin(self):
        for copy in (self.first_x, self.first_y, self.to_mate, self.rest_x, self.rest_y):
            copy.start()
        self.local().start()

    def forward(self):
        self.first_x.wait_recv()
        self.turn_y.start()
        self.first_y.wait_recv()
        self.turn_x.start()
        self.rest_x.wait_recv()
        self.mate_x.start()
        self.rest_y.wait_recv()
        self.mate_y.start()

    def near_rows(self):
        self.local().wait()
        self.to_mate.wait_recv()
        self.mate_x.wait_recv()

    def turned(self):
        self.turn_y.wait_recv()
        self.turn_x.wait_recv()
        self.mate_diag.start()

    def far_rows(self):
        self.mate_y.wait_recv()
        self.mate_diag.wait_recv()

    def finish(self):
        for copy in self.started:
            copy.wait_send()


def grads_kernel(
    replicas,
    mid_near,
    mid_far,
    back_every,
    mid_tree,
    back_tree,
    hidden_hbm,
    gate_back_hbm,
    up_back_hbm,
    gate_hbm,
    up_hbm,
    down_hbm,
    mid_begun,
    gate_out,
    up_out,
    down_out,
    mid_rows,
    back_rows,
    gate_sum,
    up_sum,
    down_sum,
    gate_w,
    up_w,
    down_w,
    mid,
    back,
    own_hidden,
    own_gate,
    own_up,
    hidden,
    gate_back,
    up_back,
    send_sem,
    recv_sem,
    local_sem,
    block_sem,
    weight_sem,
):
    plane = Plane()
    units, width = gate_w.shape
    size = mid.shape[1]
    rows = back_every.shape[1]
    tree_rows = mid_tree.shape[0]
    blocks = tree_rows // size
    half_blocks = blocks // 2
    low = jnp.bfloat16
    y = lax.div(plane.me, 4)
    others = replicas - 1
    last = (others + 1) * blocks - 1
    weights = [
        pltpu.make_async_copy(source, target, weight_sem.at[at])
        for at, (source, target) in enumerate(
            ((gate_hbm, gate_w), (up_hbm, up_w), (down_hbm, down_w))
        )
    ]
    gathers = []
    far = replica_steps(replicas, False)
    for step in range(others):
        pair = []
        if step + 1 in far:
            mid_own = mid_far.at[far.index(step + 1)]
        else:
            mid_own = mid_near.at[min(step, 1)]
        sources = ((mid_own, mid_rows), (back_every.at[step], back_rows))
        for at, (own, tree) in enumerate(sources):
            count = 2 * step + at
            pair.append(
                PlaneGather(
                    plane,
                    lambda own=own: own,
                    tree.at[step],
                    rows,
                    send_sem,
                    recv_sem,
                    local_sem.at[count],
                    GATHER_COPIES * count,
                )
            )
        gathers.append(pair)

    def own_loads(block, slot):
        there = block_at(block * size, size)
        return [
            pltpu.make_async_copy(source.at[there], target.at[slot], block_sem.at[slot, at])
            for at, (source, target) in enumerate(
                (
                    (mid_tree, mid),
                    (back_tree, back),
                    (hidden_hbm, own_hidden),
                    (gate_back_hbm, own_gate),
                    (up_back_hbm, own_up),
                )
            )
        ]

    def other_loads(block, slot):
        tree = lax.div(block, blocks) - 1
        within = lax.rem(block, blocks)
        part = lax.div(within, half_blocks)
        start = (y + part - 2 * y * part) * half_blocks * size
        there = block_at(start + lax.rem(within, half_blocks) * size, size)
        return [
            pltpu.make_async_copy(source.at[tree, there], target.at[slot], block_sem.at[slot, at])
            for at, (source, target) in enumerate(((mid_rows, mid), (back_rows, back)))
        ]

    def add(total, dot, lhs, rhs, slot):
        def tile(columns):
            total[:, columns] += dot(lhs, rhs[slot, :, columns])

        by_columns(width, tile)

    events = {}

    def event(block, *actions):
        events.setdefault(block, []).extend(actions)

    for copy in weights:
        copy.start()
    for copy in own_loads(0, 0):
        copy.start()
    for total in (down_sum, gate_sum, up_sum):
        by_rows(units, lambda at, total=total: total.__setitem__((at, slice(None)), jnp.zeros((at.size, width), jnp.float32)))
    greet(plane.near())
    gathers[0] = gathers[0][1:]
    gathers[0][0].begin()
    for step, pair in enumerate(gathers):
        base = step * blocks
        event(base + half_blocks - 2, pair[0].forward)
        event(base + half_blocks, *[gather.forward for gather in pair[1:]])
        if step + 1 < others:
            event(base + half_blocks, *[gather.begin for gather in gathers[step + 1]])
        event(base + blocks - 1, *[gather.near_rows for gather in pair])
        event(base + blocks, *[gather.turned for gather in pair])
        event(base + blocks + half_blocks - 1, *[gather.far_rows for gather in pair])

    def body(block, carry):
        slot = lax.rem(block, 2)
        is_own = block < blocks

        @pl.when(is_own)
        def _():
            for copy in own_loads(block, slot):
                copy.wait()

        @pl.when(block == blocks)
        def _():
            for copy in weights:
                copy.wait()

        @pl.when(block >= blocks)
        def _():
            for copy in other_loads(block, slot):
                copy.wait()
            tile = max(t for t in (384, 256, 128) if units % t == 0)
            for at in range(units // tile):
                there = pl.ds(at * tile, tile)
                gelu_value, slope = gelu_parts(dot_nt(gate_w[there, :], mid[slot]))
                up_lin = dot_nt(up_w[there, :], mid[slot])
                hidden_back = dot_nt(down_w[there, :], back[slot]).astype(low).astype(jnp.float32)
                hidden[there, :] = (gelu_value * up_lin).astype(low)
                gate_back[there, :] = (hidden_back * up_lin * slope).astype(low)
                up_back[there, :] = (hidden_back * gelu_value).astype(low)

        for when, actions in events.items():

            @pl.when(block == when)
            def _(actions=actions):
                for action in actions:
                    action()

        @pl.when(block + 1 < blocks)
        def _():
            for copy in own_loads(block + 1, 1 - slot):
                copy.start()

        @pl.when((block + 1 >= blocks) & (block < last))
        def _():
            for copy in other_loads(block + 1, 1 - slot):
                copy.start()

        @pl.when(is_own)
        def _():
            add(down_sum, dot_tn, own_hidden[slot], back, slot)
            add(gate_sum, dot_tn, own_gate[slot], mid, slot)
            add(up_sum, dot_tn, own_up[slot], mid, slot)

        @pl.when(block >= blocks)
        def _():
            stores = []
            for at, (total, lhs, rhs, out) in enumerate(
                (
                    (down_sum, hidden, back, down_out),
                    (gate_sum, gate_back, mid, gate_out),
                    (up_sum, up_back, mid, up_out),
                )
            ):
                add(total, dot_nn, lhs[...], rhs, slot)
                stores.append(pltpu.make_async_copy(total, out, weight_sem.at[3 + at]))
                pl.when(block == last)(stores[-1].start)

            @pl.when(block == last)
            def _():
                for copy in stores:
                    copy.wait()

        return carry

    lax.fori_loop(0, last + 1, body, 0)
    for pair in gathers:
        for gather in pair:
            gather.finish()


def feedforward_grads(
    mid_near,
    mid_far,
    back_every,
    mid_tree,
    back_tree,
    hidden,
    gate_back,
    up_back,
    gate_w,
    up_w,
    down_w,
    mid_begun,
):
    replicas = lax.axis_size("replica")
    width = mid_tree.shape[1]
    tree_rows = mid_tree.shape[0]
    units = gate_w.shape[0]
    size = tree_rows // 6
    low, full = jnp.bfloat16, jnp.float32
    copies = GATHER_COPIES * 2 * (replicas - 1)
    grad = jax.ShapeDtypeStruct((units, width), full)
    gathered = jax.ShapeDtypeStruct((replicas - 1, tree_rows, width), low)
    return pl.pallas_call(
        functools.partial(grads_kernel, replicas),
        out_shape=(grad, grad, grad, gathered, gathered),
        in_specs=any_specs(12),
        out_specs=tuple(any_specs(5)),
        input_output_aliases={11: 3},
        scratch_shapes=[pltpu.VMEM((units, width), full)] * 3
        + [pltpu.VMEM((units, width), low)] * 3
        + [pltpu.VMEM((2, size, width), low)] * 2
        + [pltpu.VMEM((2, size, units), low)] * 3
        + [pltpu.VMEM((units, size), low)] * 3
        + [
            pltpu.SemaphoreType.DMA((copies,)),
            pltpu.SemaphoreType.DMA((copies,)),
            pltpu.SemaphoreType.DMA((2 * (replicas - 1),)),
            pltpu.SemaphoreType.DMA((2, 5)),
            pltpu.SemaphoreType.DMA((6,)),
        ],
        compiler_params=remote_params(5),
        cost_estimate=pl.CostEstimate(
            flops=2 * (6 * replicas - 3) * tree_rows * units * width,
            bytes_accessed=200 * 2**20,
            transcendentals=0,
        ),
    )(
        mid_near,
        mid_far,
        back_every,
        mid_tree,
        back_tree,
        hidden,
        gate_back,
        up_back,
        gate_w,
        up_w,
        down_w,
        mid_begun,
    )[:3]


def turn(values, cos, sin):
    half = values.shape[-1] // 2
    first, second = values[:, :half], values[:, half:]
    return first * cos - second * sin, second * cos + first * sin


def turn_back(values, cos, sin):
    half = values.shape[-1] // 2
    first, second = values[:, :half], values[:, half:]
    return first * cos + second * sin, second * cos - first * sin


def allowed_block(query_bits, key_bits, query_start, key_start):
    shape = (query_bits.shape[0], key_bits.shape[1])
    query = query_start + lax.broadcasted_iota(jnp.int32, shape, 0)
    key = key_start + lax.broadcasted_iota(jnp.int32, shape, 1)
    return (((query_bits & key_bits) != 0) & (key < query)) | (key == query)


def attention_forward_kernel(
    stream,
    gain,
    cos_ref,
    sin_ref,
    query_bits,
    key_bits,
    query_w,
    key_own,
    value_own,
    output_w,
    post_gain,
    next_gain,
    valid,
    tree_out,
    query_out,
    key_out,
    value_out,
    attended_out,
    mass_out,
    total,
    middle_out,
    next_out,
    sums_out,
    own,
    tree,
    key_w,
    value_w,
    lin,
    send_sem,
    recv_sem,
    local_sem,
    *scratch,
):
    plane = Plane()
    rows, width = stream.shape
    head = query_w.shape[0]
    block = 2 * rows
    half = head // 2
    low, full = jnp.bfloat16, jnp.float32
    wires = Wires(send_sem, recv_sem)

    def normed(at):
        value = stream[at, :].astype(full)
        own[at, :] = norm_rows(value, gain[...]).astype(low)

    by_rows(rows, normed)
    greet(plane.near())
    mine = block_at(plane.core * half, half)
    key_w[mine, :] = key_own[...]
    value_w[mine, :] = value_own[...]
    tree[block_at(plane.me * rows, rows), :] = own[...]
    halves = [
        wires.send(key_own, key_w.at[mine], plane.mate),
        wires.send(value_own, value_w.at[mine], plane.mate),
    ]
    seen = []

    def use(chip):
        if not seen:
            for copy in halves:
                copy.wait_recv()
        seen.append(chip)
        there = block_at(chip * block, block)
        cos, sin = cos_ref[there, :], sin_ref[there, :]
        lin[...] = dot_nt(tree[there, :], query_w[...])
        first, second = turn(lin[...], cos, sin)
        query_out[there, :half] = (first * head**-0.5).astype(low)
        query_out[there, half:] = (second * head**-0.5).astype(low)
        lin[...] = dot_nt(tree[there, :], key_w[...])
        first, second = turn(lin[...], cos, sin)
        key_out[there, :half] = first.astype(low)
        key_out[there, half:] = second.astype(low)
        value_out[there, :] = dot_nt(tree[there, :], value_w[...]).astype(low)

    gather_tree(wires, plane, own, tree, rows, use)
    store = load(tree, tree_out, local_sem.at[0])
    gathered = list(wires.sent)

    def attend(chip):
        there = block_at(chip * block, block)
        bits = query_bits[there, :]

        def chunk(at, carry):
            result, mass = carry
            keys = block_at(at * block, block)
            scores = dot_nt(query_out[there, :], key_out[keys, :])
            allowed = allowed_block(
                bits, key_bits[:, pl.ds(pl.multiple_of(at * block, 128), block)], chip * block, at * block
            )
            raised = jnp.where(allowed, jnp.exp(score_cap * jnp.tanh(scores / score_cap)), 0.0)
            result += dot_nn(raised.astype(low), value_out[keys, :])
            return result, mass + jnp.sum(raised, axis=1, keepdims=True)

        result, mass = lax.fori_loop(
            0,
            chip + 1,
            chunk,
            (jnp.zeros((block, head), full), jnp.zeros((block, 1), full)),
        )
        scale = 1.0 / mass
        attended_out[there, :] = (result * scale).astype(low)
        mass_out[there, :] = jnp.broadcast_to(scale, (block, mass_out.shape[1]))

    def product(chip, columns):
        return dot_nn(attended_out[block_at(chip * block, block), :], output_w[:, columns])

    scatter_sum(wires, plane, scratch, product, total, attend)
    sums_out[...] = jnp.zeros_like(sums_out)

    def finish(at):
        value = stream[at, :].astype(full)
        branch = norm_rows(total[at, :], post_gain[...])
        middle = value + branch
        middle_out[at, :] = middle
        next_out[at, :] = norm_rows(middle, next_gain[...]).astype(low)
        add_row(sums_out, 0, valid[at, :] * value * value)
        add_row(sums_out, 1, valid[at, :] * branch * branch)

    by_rows(rows, finish)
    for copy in gathered:
        copy.wait_send()
    store.wait()


def attention_forward(
    stream,
    gain,
    cos,
    sin,
    query_bits,
    key_bits,
    query_weight,
    key_weight,
    value_weight,
    output_weight,
    post_gain,
    next_gain,
    valid,
):
    rows, width = stream.shape
    head = query_weight.shape[0]
    tree_rows = cos.shape[0]
    low, full = jnp.bfloat16, jnp.float32
    copies = GATHER_COPIES + SCATTER_COPIES + 2
    heads = jax.ShapeDtypeStruct((tree_rows, head), low)
    return pl.pallas_call(
        attention_forward_kernel,
        out_shape=(
            jax.ShapeDtypeStruct((tree_rows, width), low),
            heads,
            heads,
            heads,
            heads,
            jax.ShapeDtypeStruct((tree_rows, 128), full),
            jax.ShapeDtypeStruct((rows, width), full),
            jax.ShapeDtypeStruct((rows, width), full),
            jax.ShapeDtypeStruct((rows, width), low),
            jax.ShapeDtypeStruct((8, width), full),
        ),
        in_specs=vmem_specs(13),
        out_specs=tuple(any_specs(1) + vmem_specs(9)),
        scratch_shapes=[
            pltpu.VMEM((rows, width), low),
            pltpu.VMEM((tree_rows, width), low),
            pltpu.VMEM((head, width), low),
            pltpu.VMEM((head, width), low),
            pltpu.VMEM((2 * rows, head), full),
            pltpu.SemaphoreType.DMA((copies,)),
            pltpu.SemaphoreType.DMA((copies,)),
            pltpu.SemaphoreType.DMA((1,)),
        ]
        + scatter_scratch(rows, width),
        compiler_params=remote_params(3),
        cost_estimate=pl.CostEstimate(
            flops=10 * tree_rows * head * width, bytes_accessed=20 * 2**20, transcendentals=0
        ),
    )(
        stream,
        gain[None],
        cos,
        sin,
        query_bits,
        key_bits,
        query_weight,
        key_weight,
        value_weight,
        output_weight,
        post_gain[None],
        next_gain[None],
        valid,
    )


def attention_backward_kernel(
    replicas,
    own,
    cos_ref,
    sin_ref,
    query_bits,
    key_bits,
    weights,
    output_w,
    queries,
    keys_ref,
    values,
    attended,
    mass,
    stream,
    gain,
    middle_back,
    normed_hbm,
    mid_near,
    ffn_own,
    tree_out,
    mid_rows,
    every_out,
    back_out,
    grads_out,
    input_out,
    sums_out,
    total,
    tree,
    normed,
    attended_back,
    query_sum,
    key_sum,
    value_sum,
    mate_out,
    mate_in,
    send_sem,
    recv_sem,
    local_sem,
    mid_send_sem,
    mid_recv_sem,
    *scratch,
):
    plane = Plane()
    rows, width = own.shape
    head = output_w.shape[0]
    half = head // 2
    block = 2 * rows
    low, full = jnp.bfloat16, jnp.float32
    wires = Wires(send_sem, recv_sem)
    normed_load = load(normed_hbm, normed, local_sem.at[1])
    mid_gather = PlaneGather(
        plane,
        lambda: mid_near.at[0],
        mid_rows.at[0],
        rows,
        mid_send_sem,
        mid_recv_sem,
        local_sem.at[2],
        0,
    )
    steps = list(range(1, replicas))
    greet(plane.near() + [replica_device(replicas, step) for step in steps])
    over = send_over(wires, ffn_own, every_out, replicas, steps)
    tree[block_at(plane.me * rows, rows), :] = own[...]
    key_sum[...] = jnp.zeros_like(key_sum)
    value_sum[...] = jnp.zeros_like(value_sum)

    seen = []

    def use(chip):
        seen.append(chip)
        if len(seen) == 3:
            mid_gather.begin()
        there = block_at(chip * block, block)
        attended_back[there, :] = dot_nt(tree[there, :], output_w[...]).astype(low)
        inner = jnp.sum(
            attended_back[there, :].astype(full) * attended[there, :].astype(full),
            axis=1,
            keepdims=True,
        )
        bits = query_bits[there, :]
        scale = mass[there, :1]

        def chunk(at, result):
            here = block_at(at * block, block)
            tanh_value = jnp.tanh(dot_nt(queries[there, :], keys_ref[here, :]) / score_cap)
            allowed = allowed_block(
                bits, key_bits[:, pl.ds(pl.multiple_of(at * block, 128), block)], chip * block, at * block
            )
            probs = jnp.where(allowed, jnp.exp(score_cap * tanh_value) * scale, 0.0)
            prob_grads = dot_nt(attended_back[there, :], values[here, :])
            score_back = (probs * (prob_grads - inner) * (1.0 - tanh_value * tanh_value)).astype(low)
            value_sum[here, :] += dot_tn(probs.astype(low), attended_back[there, :])
            key_sum[here, :] += dot_tn(score_back, queries[there, :])
            return result + dot_nn(score_back, keys_ref[here, :])

        result = lax.fori_loop(0, chip + 1, chunk, jnp.zeros((block, head), full))
        first, second = turn_back(result * head**-0.5, cos_ref[there, :], sin_ref[there, :])
        query_sum[there, :half] = first.astype(low)
        query_sum[there, half:] = second.astype(low)

    gather_tree(wires, plane, own, tree, rows, use)
    store = load(tree, tree_out, local_sem.at[0])
    back_out[:, :head] = query_sum[...]
    first_core = plane.core == 0

    def exchange(at):
        first, second = turn_back(key_sum[at, :], cos_ref[at, :], sin_ref[at, :])
        key_sum[at, :half] = jnp.where(first_core, first, second)
        mate_out[at, :half] = jnp.where(first_core, second, first)
        first, second = value_sum[at, :half], value_sum[at, half:]
        value_sum[at, :half] = jnp.where(first_core, first, second)
        mate_out[at, half:] = jnp.where(first_core, second, first)

    by_rows(tree.shape[0], exchange)
    swap = wires.send(mate_out, mate_in, plane.mate)
    swap.wait_recv()

    def finish(at):
        back_out[at, head : head + half] = (key_sum[at, :half] + mate_in[at, :half]).astype(low)
        back_out[at, head + half :] = (value_sum[at, :half] + mate_in[at, half:]).astype(low)

    by_rows(tree.shape[0], finish)
    gathered = list(wires.sent)

    def product(chip, columns):
        return dot_nn(back_out[block_at(chip * block, block), :], weights[:, columns])

    def projection_grads():
        mid_gather.forward()
        normed_load.wait()

        def tile(columns):
            grads_out[: 2 * head, columns] = dot_tn(back_out[...], normed[:, columns]).astype(low)

        by_columns(width, tile)

    def output_grads():
        mid_gather.turned()

        def tile(columns):
            grads_out[2 * head :, columns] = dot_tn(attended[...], tree[:, columns]).astype(low)

        by_columns(width, tile)

    scatter_sum(
        wires, plane, scratch, product, total, meanwhile=(projection_grads, output_grads)
    )
    sums_out[...] = jnp.zeros_like(sums_out)

    def input_rows(at):
        back, gain_terms = norm_back(stream[at, :].astype(full), gain[...], total[at, :])
        input_out[at, :] = middle_back[at, :] + back
        add_row(sums_out, 0, gain_terms)

    by_rows(rows, input_rows)
    mid_gather.near_rows()
    mid_gather.far_rows()
    mid_gather.finish()
    for copy in over:
        copy.wait_recv()
    for copy in gathered:
        copy.wait_send()
    store.wait()


def attention_backward(
    own, cos, sin, query_bits, key_bits, weights, output_weight, queries, keys, values, attended, mass,
    stream, gain, middle_back, normed, mid_near, ffn_own,
):
    rows, width = own.shape
    head = output_weight.shape[0]
    tree_rows = cos.shape[0]
    replicas = lax.axis_size("replica")
    low, full = jnp.bfloat16, jnp.float32
    copies = GATHER_COPIES + SCATTER_COPIES + replicas
    return pl.pallas_call(
        functools.partial(attention_backward_kernel, replicas),
        out_shape=(
            jax.ShapeDtypeStruct((tree_rows, width), low),
            jax.ShapeDtypeStruct((replicas - 1, tree_rows, width), low),
            jax.ShapeDtypeStruct((replicas - 1, rows, width), low),
            jax.ShapeDtypeStruct((tree_rows, 2 * head), low),
            jax.ShapeDtypeStruct((3 * head, width), low),
            jax.ShapeDtypeStruct((rows, width), full),
            jax.ShapeDtypeStruct((8, width), full),
        ),
        in_specs=vmem_specs(15) + any_specs(3),
        out_specs=tuple(any_specs(3) + vmem_specs(4)),
        scratch_shapes=[
            pltpu.VMEM((rows, width), full),
            pltpu.VMEM((tree_rows, width), low),
            pltpu.VMEM((tree_rows, width), low),
            pltpu.VMEM((tree_rows, head), low),
            pltpu.VMEM((tree_rows, head), low),
            pltpu.VMEM((tree_rows, head), full),
            pltpu.VMEM((tree_rows, head), full),
            pltpu.VMEM((tree_rows, head), full),
            pltpu.VMEM((tree_rows, head), full),
            pltpu.SemaphoreType.DMA((copies,)),
            pltpu.SemaphoreType.DMA((copies,)),
            pltpu.SemaphoreType.DMA((3,)),
            pltpu.SemaphoreType.DMA((GATHER_COPIES,)),
            pltpu.SemaphoreType.DMA((GATHER_COPIES,)),
        ]
        + scatter_scratch(rows, width),
        compiler_params=remote_params(4),
        cost_estimate=pl.CostEstimate(
            flops=10 * tree_rows * head * width, bytes_accessed=20 * 2**20, transcendentals=0
        ),
    )(own, cos, sin, query_bits, key_bits, weights, output_weight, queries, keys, values, attended, mass, stream, gain[None], middle_back, normed, mid_near, ffn_own)


def shards_heads(
    hidden_in,
    cotangent,
    token_segment,
    token_valid,
    segment_parent,
    query_weight,
    key_weight,
    value_weight,
    output_weight,
    gate_weight,
    up_weight,
    down_weight,
    attention_gain,
    attention_post_gain,
    feedforward_gain,
    feedforward_post_gain,
):
    row_count, model_width = hidden_in.shape
    shard = lax.axis_index("shard")
    row_start = shard * row_count
    position, parent_tok, grand_tok = tree_tables(token_segment, token_valid, segment_parent[0])
    key_bits = jnp.where(token_valid == 1, 1 << token_segment, 0)[None]
    query_bits = ((1 << token_segment) | (1 << parent_tok) | (1 << grand_tok))[:, None]
    cos_table, sin_table = rope_tables(position, HEAD)
    cos_table, sin_table = cos_table[:, 0, : HEAD // 2], sin_table[:, 0, : HEAD // 2]
    valid_rows = lax.dynamic_slice_in_dim(token_valid, row_start, row_count)
    valid_rows = valid_rows.astype(jnp.float32)[:, None]
    (
        normed_in,
        queries,
        keys,
        values,
        attended,
        mass,
        attention_pre,
        middle,
        normed_mid,
        first_sums,
    ) = attention_forward(
        hidden_in,
        attention_gain,
        cos_table,
        sin_table,
        query_bits,
        key_bits,
        query_weight,
        key_weight,
        value_weight,
        output_weight,
        attention_post_gain,
        feedforward_gain,
        valid_rows,
    )
    mid_tree, hidden, mix, gelu_value, mid_near, block_out, ffpre_low, second_sums = (
        feedforward_forward(
            normed_mid,
            middle,
            cotangent,
            valid_rows,
            feedforward_post_gain,
            gate_weight,
            up_weight,
            down_weight,
        )
    )
    ffpre_tree, gate_back, up_back, mid_far, middle_back, pre_low, third_sums = (
        feedforward_backward(
            ffpre_low,
            middle,
            attention_pre,
            cotangent,
            valid_rows,
            feedforward_gain,
            attention_post_gain,
            normed_mid,
            gate_weight,
            up_weight,
            down_weight,
            mix,
            gelu_value,
        )
    )
    (
        pre_tree,
        mid_begun,
        ffpre_every,
        projection_back,
        attention_grads,
        input_grad,
        fourth_sums,
    ) = attention_backward(
        pre_low,
        cos_table,
        sin_table,
        query_bits,
        key_bits,
        jnp.concatenate([query_weight, key_weight, value_weight]),
        output_weight,
        queries,
        keys,
        values,
        attended,
        mass,
        hidden_in,
        attention_gain,
        middle_back,
        normed_in,
        mid_near,
        ffpre_low,
    )
    attention_grads = lax.psum(attention_grads, "replica").astype(jnp.float32)
    sizes = [query_weight.shape[0], key_weight.shape[0], value_weight.shape[0]]
    query_sum, key_sum, value_sum, output_sum = jnp.split(
        attention_grads, [sizes[0], sizes[0] + sizes[1], sum(sizes)]
    )
    gate_sum, up_sum, down_sum = feedforward_grads(
        mid_near,
        mid_far,
        ffpre_every,
        mid_tree,
        ffpre_tree,
        hidden,
        gate_back,
        up_back,
        gate_weight,
        up_weight,
        down_weight,
        mid_begun,
    )
    valid_total = jnp.full((1, model_width), jnp.sum(valid_rows))
    smalls = jnp.concatenate(
        [fourth_sums[:1], third_sums[:2], second_sums[:3], first_sums[:2], valid_total]
    )
    smalls = jnp.sum(lax.all_gather(smalls, ("replica", "shard")), axis=0)
    gain_one, gain_three, gain_two, gain_four = smalls[0], smalls[1], smalls[2], smalls[3]
    totals = jnp.sum(smalls[4:], axis=1)
    squares_all = jnp.stack([totals[2], totals[3], totals[0], totals[1]])
    valid_all = totals[4]
    stream_rms = jnp.sqrt(squares_all / valid_all)
    return (
        block_out,
        input_grad,
        query_sum,
        key_sum,
        value_sum,
        output_sum,
        gate_sum,
        up_sum,
        down_sum,
        gain_one,
        gain_two,
        gain_three,
        gain_four,
        stream_rms,
    )


def solution(mesh):
    heads_fit = mesh.shape["shard"] == HEADS and mesh.shape["replica"] > 2
    return jax.shard_map(
        shards_heads if heads_fit else shards_generic,
        mesh=mesh,
        in_specs=(
            P(("replica", "shard"), None),
            P(("replica", "shard"), None),
            P("replica"),
            P("replica"),
            P("replica", None),
            P("shard", None),
            P("shard", None),
            P("shard", None),
            P("shard", None),
            P("shard", None),
            P("shard", None),
            P("shard", None),
            P(),
            P(),
            P(),
            P(),
        ),
        out_specs=(
            P(("replica", "shard"), None),
            P(("replica", "shard"), None),
            P("shard", None),
            P("shard", None),
            P("shard", None),
            P("shard", None),
            P("shard", None),
            P("shard", None),
            P("shard", None),
            P(),
            P(),
            P(),
            P(),
            P(),
        ),
        check_vma=False,
    )
```

```python
import functools
import math

import jax
import jax.numpy as jnp
from jax import lax
from jax.experimental import pallas as pl
from jax.experimental.pallas import tpu as pltpu
from jax.sharding import PartitionSpec as P

HEADS = 8
KV_HEADS = 4
HEAD = 256


norm_eps = 1e-06
score_cap = 50.0


def norm_rows(stream, norm_gain):
    factor = lax.rsqrt(jnp.mean(stream * stream, axis=-1, keepdims=True) + norm_eps)
    return stream * factor * (1.0 + norm_gain)


def rotate(values, cos_table, sin_table):
    half_width = values.shape[-1] // 2
    turned = jnp.concatenate([-values[..., half_width:], values[..., :half_width]], axis=-1)
    return values * cos_table + turned * sin_table


def rotate_back(gradient, cos_table, sin_table):
    half_width = gradient.shape[-1] // 2
    shifted = gradient * sin_table
    unturned = jnp.concatenate([shifted[..., half_width:], -shifted[..., :half_width]], axis=-1)
    return gradient * cos_table + unturned


def rope_tables(position, head_size):
    half_width = head_size // 2
    frequency = jnp.power(10000.0, -jnp.arange(half_width, dtype=jnp.float32) * 2.0 / head_size)
    angles = position.astype(jnp.float32)[:, None] * frequency[None, :]
    angles = jnp.concatenate([angles, angles], axis=-1)[:, None, :]
    return (jnp.cos(angles), jnp.sin(angles))


def tree_tables(segment, valid_mask, parent):
    labels = jnp.arange(parent.shape[0], dtype=jnp.int32)
    member = (segment[:, None] == labels[None, :]).astype(jnp.int32)
    lengths = jnp.sum(member * valid_mask[:, None], axis=0)
    starts = jnp.sum((segment[:, None] < labels[None, :]).astype(jnp.int32), axis=0)
    parent_of = (parent[:, None] == labels[None, :]).astype(jnp.int32)
    grandparent = jnp.sum(parent_of * parent[None, :], axis=1)
    parent_len = jnp.sum(parent_of * lengths[None, :], axis=1)
    grand_of = (grandparent[:, None] == labels[None, :]).astype(jnp.int32)
    grand_len = jnp.sum(grand_of * lengths[None, :], axis=1)
    offsets = jnp.where(parent != labels, parent_len, 0) + jnp.where(
        grandparent != parent, grand_len, 0
    )
    token_index = jnp.arange(segment.shape[0], dtype=jnp.int32)
    position = jnp.sum(member * (offsets - starts)[None, :], axis=1) + token_index
    parent_tok = jnp.sum(member * parent[None, :], axis=1)
    grand_tok = jnp.sum(member * grandparent[None, :], axis=1)
    return (position, parent_tok, grand_tok)


def allowed_mask(query_index, query_seg, query_parent, query_grand, key_index, key_seg, key_valid):
    lineage = (
        (key_seg[None, :] == query_seg[:, None])
        | (key_seg[None, :] == query_parent[:, None])
        | (key_seg[None, :] == query_grand[:, None])
    )
    earlier = (key_seg[None, :] != query_seg[:, None]) | (key_index[None, :] < query_index[:, None])
    itself = key_index[None, :] == query_index[:, None]
    return itself | (key_valid[None, :] == 1) & lineage & earlier


def softmax_parts(scores, allowed):
    capped = score_cap * jnp.tanh(scores / score_cap)
    held = jnp.where(allowed, capped, -1000000000.0)
    largest = jnp.max(held, axis=-1, keepdims=True)
    raised = jnp.where(allowed, jnp.exp(held - largest), 0.0)
    total_mass = jnp.sum(raised, axis=-1, keepdims=True)
    return (raised / total_mass, largest + jnp.log(total_mass))


def gated_gelu(gate_lin, up_lin):
    return jax.nn.gelu(gate_lin, approximate=True) * up_lin


def collect_attention(query_weight, key_weight, value_weight, output_weight):
    return (
        lax.all_gather(query_weight, "shard", axis=0, tiled=True),
        lax.all_gather(key_weight, "shard", axis=0, tiled=True),
        lax.all_gather(value_weight, "shard", axis=0, tiled=True),
        lax.all_gather(output_weight, "shard", axis=0, tiled=True),
    )


def group_rows(values):
    return lax.all_gather(values, "shard", axis=0, tiled=True)


def group_sums(values):
    return lax.psum_scatter(values, "shard", scatter_dimension=0, tiled=True)


def shards_generic(
    hidden_in,
    cotangent,
    token_segment,
    token_valid,
    segment_parent,
    query_weight,
    key_weight,
    value_weight,
    output_weight,
    gate_weight,
    up_weight,
    down_weight,
    attention_gain,
    attention_post_gain,
    feedforward_gain,
    feedforward_post_gain,
):
    row_count, model_width = hidden_in.shape
    group_size = HEADS // KV_HEADS
    row_start = lax.axis_index("shard") * row_count
    tree_size = token_segment.shape[0]
    position, parent_tok, grand_tok = tree_tables(token_segment, token_valid, segment_parent[0])
    key_index = jnp.arange(tree_size, dtype=jnp.int32)

    def own_rows(table):
        return lax.dynamic_slice_in_dim(table, row_start, row_count)

    allowed = allowed_mask(
        own_rows(key_index),
        own_rows(token_segment),
        own_rows(parent_tok),
        own_rows(grand_tok),
        key_index,
        token_segment,
        token_valid,
    )
    mask_full = allowed[None, None]
    cos_table, sin_table = rope_tables(own_rows(position), HEAD)
    query_scale = HEAD ** (-0.5)
    valid_rows = own_rows(token_valid).astype(jnp.float32)
    stream = hidden_in.astype(jnp.float32)
    query_all, key_all, value_all, output_all = collect_attention(
        query_weight, key_weight, value_weight, output_weight
    )
    normed_in = norm_rows(stream, attention_gain).astype(jnp.bfloat16)
    query_lin = jnp.einsum("td,qd->tq", normed_in, query_all, preferred_element_type=jnp.float32)
    key_lin = jnp.einsum("td,qd->tq", normed_in, key_all, preferred_element_type=jnp.float32)
    value_lin = jnp.einsum("td,qd->tq", normed_in, value_all, preferred_element_type=jnp.float32)
    queries = (
        rotate(query_lin.reshape(row_count, HEADS, HEAD), cos_table, sin_table) * query_scale
    ).astype(jnp.bfloat16)
    keys_own = (
        rotate(key_lin.reshape(row_count, KV_HEADS, HEAD), cos_table, sin_table)
        .astype(jnp.bfloat16)
        .reshape(row_count, KV_HEADS * HEAD)
    )
    values_own = value_lin.astype(jnp.bfloat16)
    key_tree, value_tree = (
        lax.all_gather(keys_own, "shard", axis=0, tiled=True),
        lax.all_gather(values_own, "shard", axis=0, tiled=True),
    )
    query_groups = queries.reshape(row_count, KV_HEADS, group_size, HEAD)
    key_groups = key_tree.reshape(tree_size, KV_HEADS, HEAD)
    value_groups = value_tree.reshape(tree_size, KV_HEADS, HEAD)
    scores = jnp.einsum(
        "qgrd,kgd->grqk", query_groups, key_groups, preferred_element_type=jnp.float32
    )
    probs, log_total = softmax_parts(scores, mask_full)
    attended = jnp.einsum(
        "grqk,kgd->qgrd",
        probs.astype(jnp.bfloat16),
        value_groups,
        preferred_element_type=jnp.float32,
    )
    attended = attended.astype(jnp.bfloat16).reshape(row_count, HEADS * HEAD)
    attention_pre = jnp.dot(attended, output_all, preferred_element_type=jnp.float32)
    attention_branch = norm_rows(attention_pre, attention_post_gain)
    middle = stream + attention_branch
    normed_mid = norm_rows(middle, feedforward_gain).astype(jnp.bfloat16)
    mid_tree = group_rows(normed_mid)
    gate_lin = jnp.einsum("td,fd->tf", mid_tree, gate_weight, preferred_element_type=jnp.float32)
    up_lin = jnp.einsum("td,fd->tf", mid_tree, up_weight, preferred_element_type=jnp.float32)
    hidden = gated_gelu(gate_lin, up_lin).astype(jnp.bfloat16)
    feedforward_pre = group_sums(jnp.dot(hidden, down_weight, preferred_element_type=jnp.float32))
    feedforward_branch = norm_rows(feedforward_pre, feedforward_post_gain)
    result = middle + feedforward_branch
    squares = jnp.stack(
        [
            jnp.sum(valid_rows[:, None] * summand * summand)
            for summand in (stream, attention_branch, feedforward_branch, result)
        ]
    )
    valid_total = jnp.sum(valid_rows) * model_width
    squares_all, valid_all = lax.psum((squares, valid_total), ("replica", "shard"))
    seed_grad = cotangent.astype(jnp.float32) * valid_rows[:, None]
    unused_four, pull_four = jax.vjp(norm_rows, feedforward_pre, feedforward_post_gain)
    ffpre_back, grad_four = pull_four(seed_grad)
    ffpre_low = ffpre_back.astype(jnp.bfloat16)
    ffpre_tree = group_rows(ffpre_low)
    hidden_back = jnp.einsum(
        "td,fd->tf", ffpre_tree, down_weight, preferred_element_type=jnp.float32
    ).astype(jnp.bfloat16)
    unused_glu, pull_glu = jax.vjp(gated_gelu, gate_lin, up_lin)
    gate_back, up_back = pull_glu(hidden_back.astype(jnp.float32))
    gate_back = gate_back.astype(jnp.bfloat16)
    up_back = up_back.astype(jnp.bfloat16)
    mid_terms = jnp.dot(gate_back, gate_weight, preferred_element_type=jnp.float32) + jnp.dot(
        up_back, up_weight, preferred_element_type=jnp.float32
    )
    mid_back = group_sums(mid_terms)
    gate_grad = jnp.einsum("tf,td->fd", gate_back, mid_tree, preferred_element_type=jnp.float32)
    up_grad = jnp.einsum("tf,td->fd", up_back, mid_tree, preferred_element_type=jnp.float32)
    down_grad = jnp.einsum("tf,td->fd", hidden, ffpre_tree, preferred_element_type=jnp.float32)
    unused_three, pull_three = jax.vjp(norm_rows, middle, feedforward_gain)
    middle_part, grad_three = pull_three(mid_back)
    middle_back = seed_grad + middle_part
    unused_two, pull_two = jax.vjp(norm_rows, attention_pre, attention_post_gain)
    attention_pre_back, grad_two = pull_two(middle_back)
    pre_low = attention_pre_back.astype(jnp.bfloat16)
    query_all, key_all, value_all, output_all = collect_attention(
        query_weight, key_weight, value_weight, output_weight
    )
    attended_back = jnp.einsum(
        "td,qd->tq", pre_low, output_all, preferred_element_type=jnp.float32
    ).astype(jnp.bfloat16)
    scores = jnp.einsum(
        "qgrd,kgd->grqk", query_groups, key_groups, preferred_element_type=jnp.float32
    )
    tanh_value = jnp.tanh(scores / score_cap)
    probs_back = jnp.where(
        mask_full,
        jnp.exp(jnp.where(mask_full, score_cap * tanh_value - log_total, -1000000000.0)),
        0.0,
    )
    back_groups = attended_back.reshape(row_count, KV_HEADS, group_size, HEAD)
    prob_grads = jnp.einsum(
        "qgrd,kgd->grqk", back_groups, value_groups, preferred_element_type=jnp.float32
    )
    inner_sum = jnp.sum(probs_back * prob_grads, axis=-1, keepdims=True)
    score_back = (probs_back * (prob_grads - inner_sum) * (1.0 - tanh_value * tanh_value)).astype(
        jnp.bfloat16
    )
    query_back = jnp.einsum(
        "grqk,kgd->qgrd", score_back, key_groups, preferred_element_type=jnp.float32
    ).reshape(row_count, HEADS, HEAD)
    key_back = jnp.einsum(
        "grqk,qgrd->kgd", score_back, query_groups, preferred_element_type=jnp.float32
    ).reshape(tree_size, KV_HEADS * HEAD)
    value_back = jnp.einsum(
        "grqk,qgrd->kgd",
        probs_back.astype(jnp.bfloat16),
        back_groups,
        preferred_element_type=jnp.float32,
    ).reshape(tree_size, KV_HEADS * HEAD)
    key_sum, value_sum = (
        lax.psum_scatter(key_back, "shard", scatter_dimension=0, tiled=True),
        lax.psum_scatter(value_back, "shard", scatter_dimension=0, tiled=True),
    )
    query_low = (
        rotate_back(query_back * query_scale, cos_table, sin_table)
        .astype(jnp.bfloat16)
        .reshape(row_count, HEADS * HEAD)
    )
    key_low = (
        rotate_back(key_sum.reshape(row_count, KV_HEADS, HEAD), cos_table, sin_table)
        .astype(jnp.bfloat16)
        .reshape(row_count, KV_HEADS * HEAD)
    )
    value_low = value_sum.astype(jnp.bfloat16)
    normed_back = (
        jnp.dot(query_low, query_all, preferred_element_type=jnp.float32)
        + jnp.dot(key_low, key_all, preferred_element_type=jnp.float32)
        + jnp.dot(value_low, value_all, preferred_element_type=jnp.float32)
    )
    output_local = jnp.einsum("tq,td->qd", attended, pre_low, preferred_element_type=jnp.float32)
    query_local = jnp.einsum("tq,td->qd", query_low, normed_in, preferred_element_type=jnp.float32)
    key_local = jnp.einsum("tq,td->qd", key_low, normed_in, preferred_element_type=jnp.float32)
    value_local = jnp.einsum("tq,td->qd", value_low, normed_in, preferred_element_type=jnp.float32)
    query_part, key_part, value_part, output_part = (
        lax.psum_scatter(query_local, "shard", scatter_dimension=0, tiled=True),
        lax.psum_scatter(key_local, "shard", scatter_dimension=0, tiled=True),
        lax.psum_scatter(value_local, "shard", scatter_dimension=0, tiled=True),
        lax.psum_scatter(output_local, "shard", scatter_dimension=0, tiled=True),
    )
    unused_one, pull_one = jax.vjp(norm_rows, stream, attention_gain)
    stream_part, grad_one = pull_one(normed_back)
    input_grad = middle_back + stream_part
    query_sum, key_total, value_total, output_sum, gate_sum, up_sum, down_sum = lax.psum(
        (query_part, key_part, value_part, output_part, gate_grad, up_grad, down_grad), "replica"
    )
    gain_one, gain_two, gain_three, gain_four = lax.psum(
        (grad_one, grad_two, grad_three, grad_four), ("replica", "shard")
    )
    stream_rms = jnp.sqrt(squares_all / valid_all)
    return (
        result.astype(jnp.bfloat16),
        input_grad,
        query_sum,
        key_total,
        value_total,
        output_sum,
        gate_sum,
        up_sum,
        down_sum,
        gain_one,
        gain_two,
        gain_three,
        gain_four,
        stream_rms,
    )


def norm_factor(stream):
    return lax.rsqrt(jnp.mean(stream * stream, axis=-1, keepdims=True) + norm_eps)


def norm_back(stream, norm_gain, gradient):
    factor = norm_factor(stream)
    weighted = gradient * (1.0 + norm_gain)
    inner = jnp.mean(weighted * stream, axis=-1, keepdims=True)
    back = factor * weighted - stream * (factor * factor * factor * inner)
    return back, gradient * stream * factor


def dot_nt(left, right):
    return lax.dot_general(
        left, right, (((1,), (1,)), ((), ())), preferred_element_type=jnp.float32
    )


def dot_nn(left, right):
    return lax.dot_general(
        left, right, (((1,), (0,)), ((), ())), preferred_element_type=jnp.float32
    )


def dot_tn(left, right):
    return lax.dot_general(
        left, right, (((0,), (0,)), ((), ())), preferred_element_type=jnp.float32
    )


def sum_low(values):
    return lax.psum_scatter(
        values.astype(jnp.bfloat16), "shard", scatter_dimension=0, tiled=True
    ).astype(jnp.float32)


def gelu_parts(gate_lin):
    root = math.sqrt(2.0 / math.pi)
    square = gate_lin * gate_lin
    tanh_value = jnp.tanh(root * gate_lin * (1.0 + 0.044715 * square))
    half_up = 0.5 * (1.0 + tanh_value)
    slope = half_up + 0.5 * gate_lin * (1.0 - tanh_value * tanh_value) * root * (
        1.0 + 3.0 * 0.044715 * square
    )
    return gate_lin * half_up, slope


MESH_ID = pl.DeviceIdType.MESH
VMEM_BYTES = 62 * 2**20
ROOT = math.sqrt(2.0 / math.pi)


class Plane:
    def __init__(self):
        self.me = lax.axis_index("shard")
        core = lax.rem(self.me, 2)
        x = lax.rem(lax.div(self.me, 2), 2)
        y = lax.div(self.me, 4)
        self.core = core
        self.own_chip = 2 * y + x
        self.x_chip = 2 * y + 1 - x
        self.y_chip = 2 * (1 - y) + x
        self.diag_chip = 2 * (1 - y) + 1 - x
        self.mate = self.me + 1 - 2 * core
        self.x_dev = 2 * self.x_chip + core
        self.y_dev = 2 * self.y_chip + core
        self.diag_dev = 2 * self.diag_chip + core

    def near(self):
        return [{"shard": dev} for dev in (self.mate, self.x_dev, self.y_dev)]


class Wires:
    def __init__(self, send_sem, recv_sem):
        self.send_sem, self.recv_sem = send_sem, recv_sem
        self.sent = []

    def send(self, source, target, device):
        at = len(self.sent)
        copy = pltpu.make_async_remote_copy(
            src_ref=source,
            dst_ref=target,
            send_sem=self.send_sem.at[at],
            recv_sem=self.recv_sem.at[at],
            device_id=device if isinstance(device, dict) else {"shard": device},
            device_id_type=MESH_ID,
        )
        copy.start()
        self.sent.append(copy)
        return copy

    def finish(self):
        for copy in self.sent:
            copy.wait_send()


def greet(devices):
    barrier = pltpu.get_barrier_semaphore()
    for device in devices:
        pl.semaphore_signal(barrier, inc=1, device_id=device, device_id_type=MESH_ID)
    pl.semaphore_wait(barrier, len(devices))


def block_rows(ref, start, size, step=16):
    return ref.at[pl.ds(pl.multiple_of(start, step), size)]


def add_row(sums, at, term):
    sums[at : at + 1, :] += jnp.sum(term, axis=0, keepdims=True)


def by_rows(count, body, size=32):
    def step(at, carry):
        body(pl.ds(pl.multiple_of(at * size, size), size))
        return carry

    lax.fori_loop(0, count // size, step, 0)


def column_tile(width):
    return max(t for t in range(128, 769, 128) if width % t == 0)


def by_columns(width, body):
    tile = column_tile(width)

    def step(at, carry):
        body(pl.ds(pl.multiple_of(at * tile, 128), tile))
        return carry

    lax.fori_loop(0, width // tile, step, 0)


def gather_tree(wires, plane, own, tree, rows, use):
    half = rows // 2

    def part(dev, start, size):
        return block_rows(tree, dev * rows + start, size)

    def own_part(start, size):
        return own.at[pl.ds(start, size)]

    me, mate = plane.me, plane.mate
    first_x = wires.send(own_part(0, half), part(me, 0, half), plane.x_dev)
    first_y = wires.send(own_part(half, half), part(me, half, half), plane.y_dev)
    to_mate = wires.send(own_part(0, rows), part(me, 0, rows), mate)
    rest_x = wires.send(own_part(half, half), part(me, half, half), plane.x_dev)
    rest_y = wires.send(own_part(0, half), part(me, 0, half), plane.y_dev)
    to_mate.wait_recv()
    use(plane.own_chip)
    first_x.wait_recv()
    turn_y = wires.send(part(plane.x_dev, 0, half), part(plane.x_dev, 0, half), plane.y_dev)
    first_y.wait_recv()
    turn_x = wires.send(part(plane.y_dev, half, half), part(plane.y_dev, half, half), plane.x_dev)
    rest_x.wait_recv()
    mate_x = wires.send(part(plane.x_dev, 0, rows), part(plane.x_dev, 0, rows), mate)
    rest_y.wait_recv()
    mate_y = wires.send(part(plane.y_dev, 0, rows), part(plane.y_dev, 0, rows), mate)
    mate_x.wait_recv()
    use(plane.x_chip)
    turn_y.wait_recv()
    turn_x.wait_recv()
    mate_diag = wires.send(part(plane.diag_dev, 0, rows), part(plane.diag_dev, 0, rows), mate)
    mate_y.wait_recv()
    use(plane.y_chip)
    mate_diag.wait_recv()
    use(plane.diag_chip)


GATHER_COPIES = 10
DIAG, SIDE_X, SIDE_Y, OWN = range(4)


def scatter_scratch(rows, width):
    half = rows // 2
    low = jnp.bfloat16
    return [
        pltpu.VMEM((3, rows, width), jnp.float32),
        pltpu.VMEM((2 * rows, column_tile(width)), jnp.float32),
        pltpu.VMEM((2, rows, width), low),
        pltpu.VMEM((4, rows, width), low),
        pltpu.VMEM((3, half, width), low),
        pltpu.VMEM((3, half, width), low),
        pltpu.VMEM((3, half, width), low),
        pltpu.VMEM((3, half, width), low),
    ]


class Scatter:
    def __init__(self, wires, plane, scratch, product, total, order, loads=()):
        self.loads = list(loads)
        self.wires, self.plane, self.product, self.total = wires, plane, product, total
        self.sums, self.piece, self.mate_out, self.mate_in = scratch[:4]
        self.x_out, self.x_in, self.y_out, self.y_in = scratch[4:]
        self.order = order
        self.slots = {place: (0, 1, 2, 0)[at] for at, place in enumerate(order)}
        if order[0] == OWN:
            self.slots[SIDE_Y] = self.slots[DIAG]
        self.rows, self.width = total.shape
        self.half = self.rows // 2
        self.to_mate = {}

    def produce(self, place):
        plane, rows = self.plane, self.rows
        chip = (plane.diag_chip, plane.x_chip, plane.y_chip, plane.own_chip)[place]
        slot, at = self.slots[place], self.order.index(place)
        out_slot = at % 2
        if at >= 2:
            self.to_mate[self.order[at - 2]].wait_send()
        while self.loads:
            self.loads.pop().wait()

        def tile(columns):
            self.piece[...] = self.product(chip, columns)
            self.sums[slot, :, columns] = self.piece[block_at(plane.core * rows, rows), :]
            self.mate_out[out_slot, :, columns] = self.piece[
                block_at((1 - plane.core) * rows, rows), :
            ].astype(jnp.bfloat16)

        by_columns(self.width, tile)
        self.to_mate[place] = self.wires.send(
            self.mate_out.at[out_slot], self.mate_in.at[place], plane.mate
        )

    def low_part(self, out, out_slot, place, start, more=None):
        def step(at):
            there = pl.ds(pl.multiple_of(start + at.start, 16), at.size)
            value = self.sums[self.slots[place], there, :] + self.mate_in[
                place, there, :
            ].astype(jnp.float32)
            if more is not None:
                value += more[0, at, :].astype(jnp.float32)
            out[out_slot, at, :] = value.astype(jnp.bfloat16)

        by_rows(self.half, step)

    def to_x(self, slot):
        return self.wires.send(self.x_out.at[slot], self.x_in.at[slot], self.plane.x_dev)

    def to_y(self, slot):
        return self.wires.send(self.y_out.at[slot], self.y_in.at[slot], self.plane.y_dev)

    def send_diag(self):
        self.to_mate[DIAG].wait_recv()
        self.low_part(self.x_out, 0, DIAG, 0)
        self.x_first = self.to_x(0)
        self.low_part(self.y_out, 0, DIAG, self.half)
        self.y_first = self.to_y(0)

    def send_x(self):
        self.to_mate[SIDE_X].wait_recv()
        self.low_part(self.x_out, 1, SIDE_X, 0)
        self.x_next = self.to_x(1)

    def send_y(self):
        self.to_mate[SIDE_Y].wait_recv()
        self.low_part(self.y_out, 1, SIDE_Y, self.half)
        self.y_next = self.to_y(1)

    def turn(self):
        self.y_first.wait_recv()
        self.low_part(self.x_out, 2, SIDE_X, self.half, self.y_in)
        self.x_last = self.to_x(2)
        self.x_first.wait_recv()
        self.low_part(self.y_out, 2, SIDE_Y, 0, self.x_in)
        self.y_last = self.to_y(2)

    def finish(self):
        self.to_mate[OWN].wait_recv()
        late = [self.x_next, self.y_next, self.x_last, self.y_last]
        for copy in late:
            copy.wait_recv()
        for start, x_slot, y_slot in ((0, 1, 2), (self.half, 2, 1)):

            def step(at, start=start, x_slot=x_slot, y_slot=y_slot):
                there = pl.ds(pl.multiple_of(start + at.start, 16), at.size)
                self.total[there, :] = (
                    self.sums[self.slots[OWN], there, :]
                    + self.mate_in[OWN, there, :].astype(jnp.float32)
                    + self.x_in[x_slot, at, :].astype(jnp.float32)
                    + self.y_in[y_slot, at, :].astype(jnp.float32)
                )

            by_rows(self.half, step)
        for copy in [self.x_first, self.y_first] + late:
            copy.wait_send()
        for place in self.order[2:]:
            self.to_mate[place].wait_send()


def scatter_sum(wires, plane, scratch, product, total, before=lambda chip: None, meanwhile=()):
    scatter = Scatter(wires, plane, scratch, product, total, (DIAG, SIDE_X, SIDE_Y, OWN))
    work = iter(tuple(meanwhile) + (lambda: None,) * 2)
    before(plane.diag_chip)
    scatter.produce(DIAG)
    before(plane.x_chip)
    scatter.produce(SIDE_X)
    scatter.send_diag()
    before(plane.y_chip)
    scatter.produce(SIDE_Y)
    scatter.send_x()
    before(plane.own_chip)
    scatter.produce(OWN)
    scatter.send_y()
    next(work)()
    scatter.turn()
    next(work)()
    scatter.finish()


def gather_and_scatter(wires, plane, own, tree, rows, use, scatter):
    half = rows // 2

    def part(dev, start, size):
        return block_rows(tree, dev * rows + start, size)

    def own_part(start, size):
        return own.at[pl.ds(start, size)]

    def onward(dev, start, size, device):
        return wires.send(part(dev, start, size), part(dev, start, size), device)

    me, mate, x_dev, y_dev = plane.me, plane.mate, plane.x_dev, plane.y_dev
    first_x = wires.send(own_part(0, half), part(me, 0, half), x_dev)
    first_y = wires.send(own_part(half, half), part(me, half, half), y_dev)
    to_mate = wires.send(own_part(0, rows), part(me, 0, rows), mate)
    to_mate.wait_recv()
    use(plane.own_chip)
    first_x.wait_recv()
    turn_y = onward(x_dev, 0, half, y_dev)
    first_y.wait_recv()
    turn_x = onward(y_dev, half, half, x_dev)
    rest_x = wires.send(own_part(half, half), part(me, half, half), x_dev)
    rest_y = wires.send(own_part(0, half), part(me, 0, half), y_dev)
    scatter.produce(OWN)
    turn_y.wait_recv()
    turn_x.wait_recv()
    mate_diag = onward(plane.diag_dev, 0, rows, mate)
    mate_diag.wait_recv()
    use(plane.diag_chip)
    rest_x.wait_recv()
    mate_x = onward(x_dev, 0, rows, mate)
    rest_y.wait_recv()
    mate_y = onward(y_dev, 0, rows, mate)
    scatter.produce(DIAG)
    mate_x.wait_recv()
    use(plane.x_chip)
    scatter.send_diag()
    scatter.produce(SIDE_X)
    mate_y.wait_recv()
    use(plane.y_chip)
    scatter.send_x()
    scatter.produce(SIDE_Y)
    copies = [first_x, first_y, to_mate, turn_y, turn_x, rest_x, rest_y, mate_diag, mate_x, mate_y]
    for copy in copies:
        copy.wait_send()
    scatter.send_y()
    scatter.turn()
    scatter.finish()


SCATTER_COPIES = 10


def block_at(start, size):
    return pl.ds(pl.multiple_of(start, 16), size)


def load(source, target, sem):
    copy = pltpu.make_async_copy(source, target, sem)
    copy.start()
    return copy


def replica_steps(replicas, near):
    return [step for step in range(1, replicas) if (min(step, replicas - step) == 1) == near]


def replica_device(replicas, step):
    return {"replica": lax.rem(lax.axis_index("replica") + step, replicas)}


def send_over(wires, source, target, replicas, steps):
    return [
        wires.send(
            source, target.at[steps.index(replicas - step)], replica_device(replicas, step)
        )
        for step in steps
    ]


def forward_kernel(
    replicas,
    own,
    middle,
    cotangent,
    valid,
    gain,
    gate_hbm,
    up_hbm,
    down_hbm,
    tree_out,
    hidden_out,
    mix_out,
    gelu_out,
    every_out,
    block_out,
    back_out,
    sums_out,
    total,
    tree,
    gate_w,
    up_w,
    down_w,
    hidden,
    mix,
    gelu,
    gate_lin,
    up_lin,
    send_sem,
    recv_sem,
    local_sem,
    *scratch,
):
    plane = Plane()
    rows = own.shape[0]
    wires = Wires(send_sem, recv_sem)
    loads = [
        load(gate_hbm, gate_w, local_sem.at[0]),
        load(up_hbm, up_w, local_sem.at[1]),
        load(down_hbm, down_w, local_sem.at[2]),
    ]
    steps = replica_steps(replicas, True)
    greet(plane.near() + [replica_device(replicas, step) for step in steps])
    tree[block_at(plane.me * rows, rows), :] = own[...]
    stores = []

    def use(chip):
        order = len(stores) // 3
        slot = order % 2
        if order == 0:
            loads[0].wait()
            loads[1].wait()
        if order >= 2:
            stores[3 * (order - 2) + 1].wait()
            stores[3 * (order - 2) + 2].wait()
        there = block_at(chip * 2 * rows, 2 * rows)
        gate_lin[...] = dot_nt(tree[there, :], gate_w[...])
        up_lin[...] = dot_nt(tree[there, :], up_w[...])

        def step(at):
            gelu_value, slope = gelu_parts(gate_lin[at, :])
            up_value = up_lin[at, :]
            mix[slot, at, :] = (up_value * slope).astype(jnp.bfloat16)
            gelu[slot, at, :] = gelu_value.astype(jnp.bfloat16)
            hidden[block_at(chip * 2 * rows + at.start, at.size), :] = (
                gelu_value * up_value
            ).astype(jnp.bfloat16)

        by_rows(2 * rows, step, 16)
        base = 3 + 3 * order
        stores.append(load(hidden.at[there], hidden_out.at[there], local_sem.at[base]))
        stores.append(load(mix.at[slot], mix_out.at[there], local_sem.at[base + 1]))
        stores.append(load(gelu.at[slot], gelu_out.at[there], local_sem.at[base + 2]))

    over = send_over(wires, own, every_out, replicas, steps)

    def product(chip, columns):
        return dot_nn(hidden[block_at(chip * 2 * rows, 2 * rows), :], down_w[:, columns])

    scatter = Scatter(
        wires, plane, scratch, product, total, (OWN, DIAG, SIDE_X, SIDE_Y), loads[2:]
    )
    gather_and_scatter(wires, plane, own, tree, rows, use, scatter)
    tree_store = load(tree, tree_out, local_sem.at[15])
    sums_out[...] = jnp.zeros_like(sums_out)

    def finish(at):
        value = total[at, :]
        gradient = cotangent[at, :].astype(jnp.float32) * valid[at, :]
        branch = norm_rows(value, gain[...])
        result = middle[at, :] + branch
        block_out[at, :] = result.astype(jnp.bfloat16)
        back, gain_terms = norm_back(value, gain[...], gradient)
        back_out[at, :] = back.astype(jnp.bfloat16)
        add_row(sums_out, 0, gain_terms)
        add_row(sums_out, 1, valid[at, :] * branch * branch)
        add_row(sums_out, 2, valid[at, :] * result * result)

    by_rows(rows, finish)
    for copy in over:
        copy.wait()
    for copy in stores[0:1] + stores[3:4] + stores[6:] + [tree_store]:
        copy.wait()


def any_specs(count):
    return [pl.BlockSpec(memory_space=pl.ANY)] * count


def vmem_specs(count):
    return [pl.BlockSpec(memory_space=pltpu.VMEM)] * count


def remote_params(identity):
    return pltpu.CompilerParams(
        collective_id=identity, has_side_effects=True, vmem_limit_bytes=VMEM_BYTES
    )


def feedforward_forward(
    own, middle, cotangent, valid, gain, gate_weight, up_weight, down_weight
):
    rows, width = own.shape
    units = gate_weight.shape[0]
    replicas, count = lax.axis_size("replica"), lax.axis_size("shard")
    tree_rows = count * rows
    low, full = jnp.bfloat16, jnp.float32
    copies = GATHER_COPIES + SCATTER_COPIES + replicas - 1
    return pl.pallas_call(
        functools.partial(forward_kernel, replicas),
        out_shape=(
            jax.ShapeDtypeStruct((tree_rows, width), low),
            jax.ShapeDtypeStruct((tree_rows, units), low),
            jax.ShapeDtypeStruct((tree_rows, units), low),
            jax.ShapeDtypeStruct((tree_rows, units), low),
            jax.ShapeDtypeStruct((len(replica_steps(replicas, True)), rows, width), low),
            jax.ShapeDtypeStruct((rows, width), low),
            jax.ShapeDtypeStruct((rows, width), low),
            jax.ShapeDtypeStruct((8, width), full),
        ),
        in_specs=vmem_specs(5) + any_specs(3),
        out_specs=tuple(any_specs(5) + vmem_specs(3)),
        scratch_shapes=[
            pltpu.VMEM((rows, width), full),
            pltpu.VMEM((tree_rows, width), low),
            pltpu.VMEM((units, width), low),
            pltpu.VMEM((units, width), low),
            pltpu.VMEM((units, width), low),
            pltpu.VMEM((tree_rows, units), low),
            pltpu.VMEM((2, 2 * rows, units), low),
            pltpu.VMEM((2, 2 * rows, units), low),
            pltpu.VMEM((2 * rows, units), full),
            pltpu.VMEM((2 * rows, units), full),
            pltpu.SemaphoreType.DMA((copies,)),
            pltpu.SemaphoreType.DMA((copies,)),
            pltpu.SemaphoreType.DMA((16,)),
        ]
        + scatter_scratch(rows, width),
        compiler_params=remote_params(1),
        cost_estimate=pl.CostEstimate(
            flops=6 * tree_rows * units * width, bytes_accessed=40 * 2**20, transcendentals=0
        ),
    )(own, middle, cotangent, valid, gain[None], gate_weight, up_weight, down_weight)


def backward_kernel(
    replicas,
    own,
    middle,
    attention_pre,
    cotangent,
    valid,
    gain,
    post_gain,
    mid_own,
    gate_hbm,
    up_hbm,
    down_hbm,
    mix_hbm,
    gelu_hbm,
    tree_out,
    gate_out,
    up_out,
    every_out,
    middle_out,
    back_out,
    sums_out,
    total,
    tree,
    gate_w,
    up_w,
    down_w,
    gate_back,
    up_back,
    mix,
    gelu,
    hidden_back,
    send_sem,
    recv_sem,
    local_sem,
    *scratch,
):
    plane = Plane()
    rows = own.shape[0]
    wires = Wires(send_sem, recv_sem)
    chips = [plane.own_chip, plane.diag_chip, plane.x_chip, plane.y_chip]

    def fetch(order):
        there = block_at(chips[order] * 2 * rows, 2 * rows)
        return [
            load(mix_hbm.at[there], mix.at[order % 2], local_sem.at[3 + 2 * order]),
            load(gelu_hbm.at[there], gelu.at[order % 2], local_sem.at[4 + 2 * order]),
        ]

    loads = [load(down_hbm, down_w, local_sem.at[2])]
    fetched = [fetch(0), fetch(1)]
    loads += [
        load(gate_hbm, gate_w, local_sem.at[0]),
        load(up_hbm, up_w, local_sem.at[1]),
    ]
    steps = replica_steps(replicas, False)
    greet(plane.near() + [replica_device(replicas, step) for step in steps])
    tree[block_at(plane.me * rows, rows), :] = own[...]
    stores = []

    def use(chip):
        order = len(stores) // 2
        slot = order % 2
        if order == 0:
            loads[0].wait()
        there = block_at(chip * 2 * rows, 2 * rows)
        hidden_back[...] = dot_nt(tree[there, :], down_w[...])
        for copy in fetched[order]:
            copy.wait()

        def step(at):
            value = hidden_back[at, :].astype(jnp.bfloat16).astype(jnp.float32)
            here = block_at(chip * 2 * rows + at.start, at.size)
            gate_back[here, :] = (value * mix[slot, at, :].astype(jnp.float32)).astype(jnp.bfloat16)
            up_back[here, :] = (value * gelu[slot, at, :].astype(jnp.float32)).astype(jnp.bfloat16)

        by_rows(2 * rows, step, 16)
        if order + 2 < 4:
            fetched.append(fetch(order + 2))
        base = 11 + 2 * order
        stores.append(load(gate_back.at[there], gate_out.at[there], local_sem.at[base]))
        stores.append(load(up_back.at[there], up_out.at[there], local_sem.at[base + 1]))

    over = send_over(wires, mid_own, every_out, replicas, steps)

    def product(chip, columns):
        there = block_at(chip * 2 * rows, 2 * rows)
        return dot_nn(gate_back[there, :], gate_w[:, columns]) + dot_nn(
            up_back[there, :], up_w[:, columns]
        )

    scatter = Scatter(
        wires, plane, scratch, product, total, (OWN, DIAG, SIDE_X, SIDE_Y), loads[1:]
    )
    gather_and_scatter(wires, plane, own, tree, rows, use, scatter)
    tree_store = load(tree, tree_out, local_sem.at[19])
    sums_out[...] = jnp.zeros_like(sums_out)

    def finish(at):
        back, gain_terms = norm_back(middle[at, :], gain[...], total[at, :])
        back += cotangent[at, :].astype(jnp.float32) * valid[at, :]
        middle_out[at, :] = back
        add_row(sums_out, 0, gain_terms)
        back, gain_terms = norm_back(attention_pre[at, :], post_gain[...], back)
        back_out[at, :] = back.astype(jnp.bfloat16)
        add_row(sums_out, 1, gain_terms)

    by_rows(rows, finish)
    for copy in over:
        copy.wait()
    for copy in stores + [tree_store]:
        copy.wait()


def feedforward_backward(
    own,
    middle,
    attention_pre,
    cotangent,
    valid,
    gain,
    post_gain,
    mid_own,
    gate_weight,
    up_weight,
    down_weight,
    mix,
    gelu,
):
    rows, width = own.shape
    units = gate_weight.shape[0]
    replicas, count = lax.axis_size("replica"), lax.axis_size("shard")
    tree_rows = count * rows
    low, full = jnp.bfloat16, jnp.float32
    copies = GATHER_COPIES + SCATTER_COPIES + replicas - 1
    return pl.pallas_call(
        functools.partial(backward_kernel, replicas),
        out_shape=(
            jax.ShapeDtypeStruct((tree_rows, width), low),
            jax.ShapeDtypeStruct((tree_rows, units), low),
            jax.ShapeDtypeStruct((tree_rows, units), low),
            jax.ShapeDtypeStruct((len(replica_steps(replicas, False)), rows, width), low),
            jax.ShapeDtypeStruct((rows, width), full),
            jax.ShapeDtypeStruct((rows, width), low),
            jax.ShapeDtypeStruct((8, width), full),
        ),
        in_specs=vmem_specs(7) + any_specs(6),
        out_specs=tuple(any_specs(4) + vmem_specs(3)),
        scratch_shapes=[
            pltpu.VMEM((rows, width), full),
            pltpu.VMEM((tree_rows, width), low),
            pltpu.VMEM((units, width), low),
            pltpu.VMEM((units, width), low),
            pltpu.VMEM((units, width), low),
            pltpu.VMEM((tree_rows, units), low),
            pltpu.VMEM((tree_rows, units), low),
            pltpu.VMEM((2, 2 * rows, units), low),
            pltpu.VMEM((2, 2 * rows, units), low),
            pltpu.VMEM((2 * rows, units), full),
            pltpu.SemaphoreType.DMA((copies,)),
            pltpu.SemaphoreType.DMA((copies,)),
            pltpu.SemaphoreType.DMA((20,)),
        ]
        + scatter_scratch(rows, width),
        compiler_params=remote_params(2),
        cost_estimate=pl.CostEstimate(
            flops=6 * tree_rows * units * width, bytes_accessed=40 * 2**20, transcendentals=0
        ),
    )(
        own,
        middle,
        attention_pre,
        cotangent,
        valid,
        gain[None],
        post_gain[None],
        mid_own,
        gate_weight,
        up_weight,
        down_weight,
        mix,
        gelu,
    )


class Copy:
    def __init__(self, build):
        self.build = build

    def start(self):
        self.build().start()

    def wait_recv(self):
        self.build().wait_recv()

    def wait_send(self):
        self.build().wait_send()


class PlaneGather:
    def __init__(self, plane, own, tree, rows, send_sem, recv_sem, local_sem, base):
        half = rows // 2
        me, mate, x_dev, y_dev = plane.me, plane.mate, plane.x_dev, plane.y_dev
        diag = plane.diag_dev
        self.started = []

        def part(dev, start, size):
            return block_rows(tree, dev * rows + start, size)

        def copy(source, target, device):
            at = base + len(self.started)

            def build():
                return pltpu.make_async_remote_copy(
                    src_ref=source(),
                    dst_ref=target(),
                    send_sem=send_sem.at[at],
                    recv_sem=recv_sem.at[at],
                    device_id={"shard": device},
                    device_id_type=MESH_ID,
                )

            self.started.append(Copy(build))
            return self.started[-1]

        def from_own(start, size, device):
            return copy(
                lambda: own().at[pl.ds(start, size)], lambda: part(me, start, size), device
            )

        def onward(dev, start, size, device):
            return copy(lambda: part(dev, start, size), lambda: part(dev, start, size), device)

        self.first_x = from_own(0, half, x_dev)
        self.first_y = from_own(half, half, y_dev)
        self.to_mate = from_own(0, rows, mate)
        self.rest_x = from_own(half, half, x_dev)
        self.rest_y = from_own(0, half, y_dev)
        self.turn_y = onward(x_dev, 0, half, y_dev)
        self.turn_x = onward(y_dev, half, half, x_dev)
        self.mate_x = onward(x_dev, 0, rows, mate)
        self.mate_y = onward(y_dev, 0, rows, mate)
        self.mate_diag = onward(diag, 0, rows, mate)
        self.local = lambda: pltpu.make_async_copy(own(), part(me, 0, rows), local_sem)

    def begin(self):
        for copy in (self.first_x, self.first_y, self.to_mate, self.rest_x, self.rest_y):
            copy.start()
        self.local().start()

    def turn(self):
        self.first_x.wait_recv()
        self.turn_y.start()
        self.first_y.wait_recv()
        self.turn_x.start()

    def to_mates(self):
        self.rest_x.wait_recv()
        self.mate_x.start()
        self.rest_y.wait_recv()
        self.mate_y.start()

    def near_rows(self):
        self.local().wait()
        self.to_mate.wait_recv()
        self.mate_x.wait_recv()

    def turned(self):
        self.turn_y.wait_recv()
        self.turn_x.wait_recv()
        self.mate_diag.start()

    def far_rows(self):
        self.mate_y.wait_recv()
        self.mate_diag.wait_recv()

    def finish(self):
        for copy in self.started:
            copy.wait_send()


def grads_kernel(
    replicas,
    mid_near,
    mid_far,
    back_every,
    mid_tree,
    back_tree,
    hidden_hbm,
    gate_back_hbm,
    up_back_hbm,
    gate_hbm,
    up_hbm,
    down_hbm,
    mid_begun,
    gate_out,
    up_out,
    down_out,
    mid_rows,
    back_rows,
    gate_sum,
    up_sum,
    down_sum,
    gate_w,
    up_w,
    down_w,
    mid,
    back,
    own_hidden,
    own_gate,
    own_up,
    hidden,
    gate_back,
    up_back,
    send_sem,
    recv_sem,
    local_sem,
    block_sem,
    weight_sem,
):
    plane = Plane()
    units, width = gate_w.shape
    size = mid.shape[1]
    rows = back_every.shape[1]
    tree_rows = mid_tree.shape[0]
    blocks = tree_rows // size
    half_blocks = blocks // 2
    low = jnp.bfloat16
    y = lax.div(plane.me, 4)
    others = replicas - 1
    last = others * blocks + half_blocks - 1
    weights = [
        pltpu.make_async_copy(source, target, weight_sem.at[at])
        for at, (source, target) in enumerate(
            ((gate_hbm, gate_w), (up_hbm, up_w), (down_hbm, down_w))
        )
    ]
    gathers = []
    far = replica_steps(replicas, False)
    for step in range(others):
        pair = []
        if step + 1 in far:
            mid_own = mid_far.at[far.index(step + 1)]
        else:
            mid_own = mid_near.at[min(step, 1)]
        sources = ((mid_own, mid_rows), (back_every.at[step], back_rows))
        for at, (own, tree) in enumerate(sources):
            count = 2 * step + at
            pair.append(
                PlaneGather(
                    plane,
                    lambda own=own: own,
                    tree.at[step],
                    rows,
                    send_sem,
                    recv_sem,
                    local_sem.at[count],
                    GATHER_COPIES * count,
                )
            )
        gathers.append(pair)

    def own_loads(block, slot):
        there = block_at(block * size, size)
        return [
            pltpu.make_async_copy(source.at[there], target.at[slot], block_sem.at[slot, at])
            for at, (source, target) in enumerate(
                (
                    (mid_tree, mid),
                    (back_tree, back),
                    (hidden_hbm, own_hidden),
                    (gate_back_hbm, own_gate),
                    (up_back_hbm, own_up),
                )
            )
        ]

    def other_loads(block, slot):
        tree = lax.div(block, blocks) - 1
        within = lax.rem(block, blocks)
        part = lax.div(within, half_blocks)
        start = (y + part - 2 * y * part) * half_blocks * size
        there = block_at(start + lax.rem(within, half_blocks) * size, size)
        return [
            pltpu.make_async_copy(source.at[tree, there], target.at[slot], block_sem.at[slot, at])
            for at, (source, target) in enumerate(((mid_rows, mid), (back_rows, back)))
        ]

    def add(total, dot, lhs, rhs, slot, first=False):
        def part(at):
            left = lhs[:, at] if dot is dot_tn else lhs[at, :]
            if first:
                total[at, :] = dot(left, rhs[slot])
            else:
                total[at, :] += dot(left, rhs[slot])

        by_rows(units, part, 384)

    events = {}

    def event(block, *actions):
        events.setdefault(block, []).extend(actions)

    for copy in weights:
        copy.start()
    for copy in own_loads(0, 0):
        copy.start()
    greet(plane.near())
    gathers[0] = gathers[0][1:]
    gathers[0][0].begin()
    for step, pair in enumerate(gathers):
        base = step * blocks
        if len(pair) == 1:
            event(base + 2, pair[0].turn)
            event(base + 4, pair[0].to_mates)
        else:
            event(base + 1, pair[0].turn)
            event(base + 2, pair[0].to_mates)
            event(base + 3, pair[1].turn)
            event(base + 4, pair[1].to_mates)
        if step + 1 < others:
            event(base + 4, *[gather.begin for gather in gathers[step + 1]])
        event(base + 5, *[gather.near_rows for gather in pair])
        event(base + 6 + (len(pair) > 1), *[gather.turned for gather in pair])
        event(base + 8, *[gather.far_rows for gather in pair])

    def body(block, carry):
        slot = lax.rem(block, 2)
        is_own = block < blocks

        @pl.when(is_own)
        def _():
            for copy in own_loads(block, slot):
                copy.wait()

        @pl.when(block == blocks)
        def _():
            for copy in weights:
                copy.wait()

        @pl.when(block >= blocks)
        def _():
            for copy in other_loads(block, slot):
                copy.wait()
            tile = units // 2
            for at in range(2):
                there = pl.ds(at * tile, tile)
                gelu_value, slope = gelu_parts(dot_nt(gate_w[there, :], mid[slot]))
                up_lin = dot_nt(up_w[there, :], mid[slot])
                hidden_back = dot_nt(down_w[there, :], back[slot]).astype(low).astype(jnp.float32)
                hidden[there, :] = (gelu_value * up_lin).astype(low)
                gate_back[there, :] = (hidden_back * up_lin * slope).astype(low)
                up_back[there, :] = (hidden_back * gelu_value).astype(low)

        for when, actions in events.items():

            @pl.when(block == when)
            def _(actions=actions):
                for action in actions:
                    action()

        @pl.when(block + 1 < blocks)
        def _():
            for copy in own_loads(block + 1, 1 - slot):
                copy.start()

        @pl.when((block + 1 >= blocks) & (block < last))
        def _():
            for copy in other_loads(block + 1, 1 - slot):
                copy.start()

        for first in (True, False):

            @pl.when(block == 0 if first else (block > 0) & is_own)
            def _(first=first):
                add(down_sum, dot_tn, own_hidden.at[slot], back, slot, first)
                add(gate_sum, dot_tn, own_gate.at[slot], mid, slot, first)
                add(up_sum, dot_tn, own_up.at[slot], mid, slot, first)

        @pl.when(block >= blocks)
        def _():
            stores = []
            for at, (total, lhs, rhs, out) in enumerate(
                (
                    (down_sum, hidden, back, down_out),
                    (gate_sum, gate_back, mid, gate_out),
                    (up_sum, up_back, mid, up_out),
                )
            ):
                add(total, dot_nn, lhs, rhs, slot)
                stores.append(pltpu.make_async_copy(total, out, weight_sem.at[3 + at]))
                pl.when(block == last)(stores[-1].start)

            @pl.when(block == last)
            def _():
                for copy in stores:
                    copy.wait()

        return carry

    lax.fori_loop(0, last + 1, body, 0)
    for pair in gathers:
        for gather in pair:
            gather.finish()


def feedforward_grads(
    mid_near,
    mid_far,
    back_every,
    mid_tree,
    back_tree,
    hidden,
    gate_back,
    up_back,
    gate_w,
    up_w,
    down_w,
    mid_begun,
):
    replicas = lax.axis_size("replica")
    width = mid_tree.shape[1]
    tree_rows = mid_tree.shape[0]
    units = gate_w.shape[0]
    size = tree_rows // 6
    low, full = jnp.bfloat16, jnp.float32
    copies = GATHER_COPIES * 2 * (replicas - 1)
    grad = jax.ShapeDtypeStruct((units, width), full)
    gathered = jax.ShapeDtypeStruct((replicas - 1, tree_rows, width), low)
    return pl.pallas_call(
        functools.partial(grads_kernel, replicas),
        out_shape=(grad, grad, grad, gathered, gathered),
        in_specs=any_specs(12),
        out_specs=tuple(any_specs(5)),
        input_output_aliases={11: 3},
        scratch_shapes=[pltpu.VMEM((units, width), full)] * 3
        + [pltpu.VMEM((units, width), low)] * 3
        + [pltpu.VMEM((2, size, width), low)] * 2
        + [pltpu.VMEM((2, size, units), low)] * 3
        + [pltpu.VMEM((units, size), low)] * 3
        + [
            pltpu.SemaphoreType.DMA((copies,)),
            pltpu.SemaphoreType.DMA((copies,)),
            pltpu.SemaphoreType.DMA((2 * (replicas - 1),)),
            pltpu.SemaphoreType.DMA((2, 5)),
            pltpu.SemaphoreType.DMA((6,)),
        ],
        compiler_params=remote_params(5),
        cost_estimate=pl.CostEstimate(
            flops=2 * (6 * replicas - 3) * tree_rows * units * width,
            bytes_accessed=200 * 2**20,
            transcendentals=0,
        ),
    )(
        mid_near,
        mid_far,
        back_every,
        mid_tree,
        back_tree,
        hidden,
        gate_back,
        up_back,
        gate_w,
        up_w,
        down_w,
        mid_begun,
    )


def last_kernel(
    start_ref,
    mid_ref,
    back_ref,
    gate_hbm,
    up_hbm,
    down_hbm,
    gate_so_far,
    up_so_far,
    down_so_far,
    gate_out,
    up_out,
    down_out,
    gate_sum,
    up_sum,
    down_sum,
    gate_w,
    up_w,
    down_w,
    hidden,
    gate_back,
    up_back,
    sems,
):
    step = pl.program_id(0)
    final = step == pl.num_programs(0) - 1
    units = gate_w.shape[0]
    low = jnp.bfloat16
    weights = [
        pltpu.make_async_copy(source, target, sems.at[at])
        for at, (source, target) in enumerate(
            ((gate_hbm, gate_w), (up_hbm, up_w), (down_hbm, down_w))
        )
    ]
    sums = [
        pltpu.make_async_copy(source, target, sems.at[3 + at])
        for at, (source, target) in enumerate(
            ((down_so_far, down_sum), (gate_so_far, gate_sum), (up_so_far, up_sum))
        )
    ]

    @pl.when(step == 0)
    def _():
        for copy in weights:
            copy.start()
        for copy in weights:
            copy.wait()
        for copy in sums:
            copy.start()

    tile = units // 2
    for at in range(2):
        there = pl.ds(at * tile, tile)
        gelu_value, slope = gelu_parts(dot_nt(gate_w[there, :], mid_ref[...]))
        up_lin = dot_nt(up_w[there, :], mid_ref[...])
        hidden_back = dot_nt(down_w[there, :], back_ref[...]).astype(low).astype(jnp.float32)
        hidden[there, :] = (gelu_value * up_lin).astype(low)
        gate_back[there, :] = (hidden_back * up_lin * slope).astype(low)
        up_back[there, :] = (hidden_back * gelu_value).astype(low)
    stores = []
    for at, (total, lhs, rhs, out) in enumerate(
        (
            (down_sum, hidden, back_ref, down_out),
            (gate_sum, gate_back, mid_ref, gate_out),
            (up_sum, up_back, mid_ref, up_out),
        )
    ):
        pl.when(step == 0)(sums[at].wait)

        def part(at, total=total, lhs=lhs, rhs=rhs):
            total[at, :] += dot_nn(lhs[at, :], rhs[...])

        by_rows(units, part, 384)
        stores.append(pltpu.make_async_copy(total, out, sems.at[6 + at]))
        pl.when(final)(stores[-1].start)

    @pl.when(final)
    def _():
        for copy in stores:
            copy.wait()


def last_grads(gate_sum, up_sum, down_sum, mid_rows, back_rows, gate_w, up_w, down_w):
    trees, tree_rows, width = mid_rows.shape
    units = gate_w.shape[0]
    size = tree_rows // 6
    low, full = jnp.bfloat16, jnp.float32
    start = (3 * (1 - lax.axis_index("shard") // 4)).reshape(1)

    def block(step, start_ref):
        return trees - 1, start_ref[0] + step, 0

    grad = jax.ShapeDtypeStruct((units, width), full)
    return pl.pallas_call(
        last_kernel,
        grid_spec=pltpu.PrefetchScalarGridSpec(
            num_scalar_prefetch=1,
            grid=(3,),
            in_specs=[pl.BlockSpec((None, size, width), block)] * 2 + any_specs(6),
            out_specs=tuple(any_specs(3)),
            scratch_shapes=[pltpu.VMEM((units, width), full)] * 3
            + [pltpu.VMEM((units, width), low)] * 3
            + [pltpu.VMEM((units, size), low)] * 3
            + [pltpu.SemaphoreType.DMA((9,))],
        ),
        out_shape=(grad, grad, grad),
        compiler_params=pltpu.CompilerParams(vmem_limit_bytes=VMEM_BYTES),
        cost_estimate=pl.CostEstimate(
            flops=6 * tree_rows * units * width, bytes_accessed=90 * 2**20, transcendentals=0
        ),
    )(start, mid_rows, back_rows, gate_w, up_w, down_w, gate_sum, up_sum, down_sum)


def turn(values, cos, sin):
    half = values.shape[-1] // 2
    first, second = values[:, :half], values[:, half:]
    return first * cos - second * sin, second * cos + first * sin


def turn_back(values, cos, sin):
    half = values.shape[-1] // 2
    first, second = values[:, :half], values[:, half:]
    return first * cos + second * sin, second * cos - first * sin


def allowed_block(query_bits, key_bits, query_start, key_start):
    shape = (query_bits.shape[0], key_bits.shape[1])
    query = query_start + lax.broadcasted_iota(jnp.int32, shape, 0)
    key = key_start + lax.broadcasted_iota(jnp.int32, shape, 1)
    return (((query_bits & key_bits) != 0) & (key < query)) | (key == query)


def attention_forward_kernel(
    stream,
    gain,
    cos_ref,
    sin_ref,
    query_bits,
    key_bits,
    query_w,
    key_own,
    value_own,
    output_w,
    post_gain,
    next_gain,
    valid,
    tree_out,
    query_out,
    key_out,
    value_out,
    attended_out,
    mass_out,
    total,
    middle_out,
    next_out,
    sums_out,
    own,
    tree,
    key_w,
    value_w,
    lin,
    send_sem,
    recv_sem,
    local_sem,
    *scratch,
):
    plane = Plane()
    rows, width = stream.shape
    head = query_w.shape[0]
    block = 2 * rows
    half = head // 2
    low, full = jnp.bfloat16, jnp.float32
    wires = Wires(send_sem, recv_sem)

    def normed(at):
        value = stream[at, :].astype(full)
        own[at, :] = norm_rows(value, gain[...]).astype(low)

    by_rows(rows, normed)
    greet(plane.near())
    mine = block_at(plane.core * half, half)
    key_w[mine, :] = key_own[...]
    value_w[mine, :] = value_own[...]
    tree[block_at(plane.me * rows, rows), :] = own[...]
    halves = [
        wires.send(key_own, key_w.at[mine], plane.mate),
        wires.send(value_own, value_w.at[mine], plane.mate),
    ]
    seen = []

    def use(chip):
        if not seen:
            for copy in halves:
                copy.wait_recv()
        seen.append(chip)
        there = block_at(chip * block, block)
        cos, sin = cos_ref[there, :], sin_ref[there, :]
        lin[...] = dot_nt(tree[there, :], query_w[...])
        first, second = turn(lin[...], cos, sin)
        query_out[there, :half] = (first * head**-0.5).astype(low)
        query_out[there, half:] = (second * head**-0.5).astype(low)
        lin[...] = dot_nt(tree[there, :], key_w[...])
        first, second = turn(lin[...], cos, sin)
        key_out[there, :half] = first.astype(low)
        key_out[there, half:] = second.astype(low)
        value_out[there, :] = dot_nt(tree[there, :], value_w[...]).astype(low)

    gather_tree(wires, plane, own, tree, rows, use)
    store = load(tree, tree_out, local_sem.at[0])
    gathered = list(wires.sent)

    def attend(chip):
        there = block_at(chip * block, block)
        bits = query_bits[there, :]

        def chunk(at, carry):
            result, mass = carry
            keys = block_at(at * block, block)
            scores = dot_nt(query_out[there, :], key_out[keys, :])
            allowed = allowed_block(
                bits, key_bits[:, pl.ds(pl.multiple_of(at * block, 128), block)], chip * block, at * block
            )
            raised = jnp.where(allowed, jnp.exp(score_cap * jnp.tanh(scores / score_cap)), 0.0)
            result += dot_nn(raised.astype(low), value_out[keys, :])
            return result, mass + jnp.sum(raised, axis=1, keepdims=True)

        result, mass = lax.fori_loop(
            0,
            chip + 1,
            chunk,
            (jnp.zeros((block, head), full), jnp.zeros((block, 1), full)),
        )
        scale = 1.0 / mass
        attended_out[there, :] = (result * scale).astype(low)
        mass_out[there, :] = jnp.broadcast_to(scale, (block, mass_out.shape[1]))

    def product(chip, columns):
        return dot_nn(attended_out[block_at(chip * block, block), :], output_w[:, columns])

    scatter_sum(wires, plane, scratch, product, total, attend)
    sums_out[...] = jnp.zeros_like(sums_out)

    def finish(at):
        value = stream[at, :].astype(full)
        branch = norm_rows(total[at, :], post_gain[...])
        middle = value + branch
        middle_out[at, :] = middle
        next_out[at, :] = norm_rows(middle, next_gain[...]).astype(low)
        add_row(sums_out, 0, valid[at, :] * value * value)
        add_row(sums_out, 1, valid[at, :] * branch * branch)

    by_rows(rows, finish)
    for copy in gathered:
        copy.wait_send()
    store.wait()


def attention_forward(
    stream,
    gain,
    cos,
    sin,
    query_bits,
    key_bits,
    query_weight,
    key_weight,
    value_weight,
    output_weight,
    post_gain,
    next_gain,
    valid,
):
    rows, width = stream.shape
    head = query_weight.shape[0]
    tree_rows = cos.shape[0]
    low, full = jnp.bfloat16, jnp.float32
    copies = GATHER_COPIES + SCATTER_COPIES + 2
    heads = jax.ShapeDtypeStruct((tree_rows, head), low)
    return pl.pallas_call(
        attention_forward_kernel,
        out_shape=(
            jax.ShapeDtypeStruct((tree_rows, width), low),
            heads,
            heads,
            heads,
            heads,
            jax.ShapeDtypeStruct((tree_rows, 128), full),
            jax.ShapeDtypeStruct((rows, width), full),
            jax.ShapeDtypeStruct((rows, width), full),
            jax.ShapeDtypeStruct((rows, width), low),
            jax.ShapeDtypeStruct((8, width), full),
        ),
        in_specs=vmem_specs(13),
        out_specs=tuple(any_specs(1) + vmem_specs(9)),
        scratch_shapes=[
            pltpu.VMEM((rows, width), low),
            pltpu.VMEM((tree_rows, width), low),
            pltpu.VMEM((head, width), low),
            pltpu.VMEM((head, width), low),
            pltpu.VMEM((2 * rows, head), full),
            pltpu.SemaphoreType.DMA((copies,)),
            pltpu.SemaphoreType.DMA((copies,)),
            pltpu.SemaphoreType.DMA((1,)),
        ]
        + scatter_scratch(rows, width),
        compiler_params=remote_params(3),
        cost_estimate=pl.CostEstimate(
            flops=10 * tree_rows * head * width, bytes_accessed=20 * 2**20, transcendentals=0
        ),
    )(
        stream,
        gain[None],
        cos,
        sin,
        query_bits,
        key_bits,
        query_weight,
        key_weight,
        value_weight,
        output_weight,
        post_gain[None],
        next_gain[None],
        valid,
    )


def attention_backward_kernel(
    replicas,
    own,
    cos_ref,
    sin_ref,
    query_bits,
    key_bits,
    weights,
    output_w,
    queries,
    keys_ref,
    values,
    attended,
    mass,
    gain,
    valid,
    first_sums,
    second_sums,
    third_sums,
    stream_hbm,
    middle_back_hbm,
    normed_hbm,
    mid_near,
    ffn_own,
    tree_out,
    mid_rows,
    every_out,
    back_out,
    grads_out,
    input_out,
    sums_out,
    total,
    tree,
    normed,
    attended_back,
    query_sum,
    key_sum,
    value_sum,
    mate_out,
    mate_in,
    send_sem,
    recv_sem,
    local_sem,
    mid_send_sem,
    mid_recv_sem,
    *scratch,
):
    plane = Plane()
    rows, width = own.shape
    head = output_w.shape[0]
    half = head // 2
    block = 2 * rows
    low, full = jnp.bfloat16, jnp.float32
    wires = Wires(send_sem, recv_sem)
    normed_load = load(normed_hbm, normed, local_sem.at[1])
    mid_gather = PlaneGather(
        plane,
        lambda: mid_near.at[0],
        mid_rows.at[0],
        rows,
        mid_send_sem,
        mid_recv_sem,
        local_sem.at[2],
        0,
    )
    steps = list(range(1, replicas))
    greet(plane.near() + [replica_device(replicas, step) for step in steps])
    over = send_over(wires, ffn_own, every_out, replicas, steps)
    tree[block_at(plane.me * rows, rows), :] = own[...]
    key_sum[...] = jnp.zeros_like(key_sum)
    value_sum[...] = jnp.zeros_like(value_sum)

    seen = []

    def use(chip):
        seen.append(chip)
        if len(seen) == 3:
            mid_gather.begin()
        there = block_at(chip * block, block)
        attended_back[there, :] = dot_nt(tree[there, :], output_w[...]).astype(low)
        inner = jnp.sum(
            attended_back[there, :].astype(full) * attended[there, :].astype(full),
            axis=1,
            keepdims=True,
        )
        bits = query_bits[there, :]
        scale = mass[there, :1]

        def chunk(at, result):
            here = block_at(at * block, block)
            tanh_value = jnp.tanh(dot_nt(queries[there, :], keys_ref[here, :]) / score_cap)
            allowed = allowed_block(
                bits, key_bits[:, pl.ds(pl.multiple_of(at * block, 128), block)], chip * block, at * block
            )
            probs = jnp.where(allowed, jnp.exp(score_cap * tanh_value) * scale, 0.0)
            prob_grads = dot_nt(attended_back[there, :], values[here, :])
            score_back = (probs * (prob_grads - inner) * (1.0 - tanh_value * tanh_value)).astype(low)
            value_sum[here, :] += dot_tn(probs.astype(low), attended_back[there, :])
            key_sum[here, :] += dot_tn(score_back, queries[there, :])
            return result + dot_nn(score_back, keys_ref[here, :])

        result = lax.fori_loop(0, chip + 1, chunk, jnp.zeros((block, head), full))
        first, second = turn_back(result * head**-0.5, cos_ref[there, :], sin_ref[there, :])
        query_sum[there, :half] = first.astype(low)
        query_sum[there, half:] = second.astype(low)

    gather_tree(wires, plane, own, tree, rows, use)
    store = load(tree, tree_out, local_sem.at[0])
    back_out[:, :head] = query_sum[...]
    first_core = plane.core == 0

    def exchange(at):
        first, second = turn_back(key_sum[at, :], cos_ref[at, :], sin_ref[at, :])
        key_sum[at, :half] = jnp.where(first_core, first, second)
        mate_out[at, :half] = jnp.where(first_core, second, first)
        first, second = value_sum[at, :half], value_sum[at, half:]
        value_sum[at, :half] = jnp.where(first_core, first, second)
        mate_out[at, half:] = jnp.where(first_core, second, first)

    by_rows(tree.shape[0], exchange)
    swap = wires.send(mate_out, mate_in, plane.mate)
    swap.wait_recv()

    def finish(at):
        back_out[at, head : head + half] = (key_sum[at, :half] + mate_in[at, :half]).astype(low)
        back_out[at, head + half :] = (value_sum[at, :half] + mate_in[at, half:]).astype(low)

    by_rows(tree.shape[0], finish)
    gathered = list(wires.sent)

    def product(chip, columns):
        return dot_nn(back_out[block_at(chip * block, block), :], weights[:, columns])

    def projection_grads():
        mid_gather.turn()
        mid_gather.to_mates()
        normed_load.wait()

        def tile(columns):
            grads_out[: 2 * head, columns] = dot_tn(back_out[...], normed[:, columns]).astype(low)

        by_columns(width, tile)

    def output_grads():
        mid_gather.turned()

        def tile(columns):
            grads_out[2 * head :, columns] = dot_tn(attended[...], tree[:, columns]).astype(low)

        by_columns(width, tile)

    scatter_sum(
        wires, plane, scratch, product, total, meanwhile=(projection_grads, output_grads)
    )
    sums_out[...] = jnp.zeros_like(sums_out)

    stream, middle_back = scratch[2].at[0], scratch[0].at[1]
    late = [
        load(stream_hbm, stream, local_sem.at[3]),
        load(middle_back_hbm, middle_back, local_sem.at[4]),
    ]
    for copy in late:
        copy.wait()

    def input_rows(at):
        back, gain_terms = norm_back(stream[at, :].astype(full), gain[...], total[at, :])
        input_out[at, :] = middle_back[at, :] + back
        add_row(sums_out, 0, gain_terms)

    by_rows(rows, input_rows)
    sums_out[1:3, :] = third_sums[0:2, :]
    sums_out[3:6, :] = second_sums[0:3, :]
    sums_out[6:8, :] = first_sums[0:2, :]
    sums_out[8:9, :] = jnp.broadcast_to(jnp.sum(valid[...], axis=0, keepdims=True), (1, width))
    mid_gather.near_rows()
    mid_gather.far_rows()
    mid_gather.finish()
    for copy in over:
        copy.wait_recv()
    for copy in gathered:
        copy.wait_send()
    store.wait()


def attention_backward(
    own, cos, sin, query_bits, key_bits, weights, output_weight, queries, keys, values, attended, mass,
    stream, gain, middle_back, valid, sums, normed, mid_near, ffn_own,
):
    rows, width = own.shape
    head = output_weight.shape[0]
    tree_rows = cos.shape[0]
    replicas = lax.axis_size("replica")
    low, full = jnp.bfloat16, jnp.float32
    copies = GATHER_COPIES + SCATTER_COPIES + replicas
    return pl.pallas_call(
        functools.partial(attention_backward_kernel, replicas),
        out_shape=(
            jax.ShapeDtypeStruct((tree_rows, width), low),
            jax.ShapeDtypeStruct((replicas - 1, tree_rows, width), low),
            jax.ShapeDtypeStruct((replicas - 1, rows, width), low),
            jax.ShapeDtypeStruct((tree_rows, 2 * head), low),
            jax.ShapeDtypeStruct((3 * head, width), low),
            jax.ShapeDtypeStruct((rows, width), full),
            jax.ShapeDtypeStruct((16, width), full),
        ),
        in_specs=vmem_specs(17) + any_specs(5),
        out_specs=tuple(any_specs(3) + vmem_specs(4)),
        scratch_shapes=[
            pltpu.VMEM((rows, width), full),
            pltpu.VMEM((tree_rows, width), low),
            pltpu.VMEM((tree_rows, width), low),
            pltpu.VMEM((tree_rows, head), low),
            pltpu.VMEM((tree_rows, head), low),
            pltpu.VMEM((tree_rows, head), full),
            pltpu.VMEM((tree_rows, head), full),
            pltpu.VMEM((tree_rows, head), full),
            pltpu.VMEM((tree_rows, head), full),
            pltpu.SemaphoreType.DMA((copies,)),
            pltpu.SemaphoreType.DMA((copies,)),
            pltpu.SemaphoreType.DMA((5,)),
            pltpu.SemaphoreType.DMA((GATHER_COPIES,)),
            pltpu.SemaphoreType.DMA((GATHER_COPIES,)),
        ]
        + scatter_scratch(rows, width),
        compiler_params=remote_params(4),
        cost_estimate=pl.CostEstimate(
            flops=10 * tree_rows * head * width, bytes_accessed=20 * 2**20, transcendentals=0
        ),
    )(own, cos, sin, query_bits, key_bits, weights, output_weight, queries, keys, values, attended, mass, gain[None], valid, *sums, stream, middle_back, normed, mid_near, ffn_own)


def shards_heads(
    hidden_in,
    cotangent,
    token_segment,
    token_valid,
    segment_parent,
    query_weight,
    key_weight,
    value_weight,
    output_weight,
    gate_weight,
    up_weight,
    down_weight,
    attention_gain,
    attention_post_gain,
    feedforward_gain,
    feedforward_post_gain,
):
    row_count, model_width = hidden_in.shape
    shard = lax.axis_index("shard")
    row_start = shard * row_count
    position, parent_tok, grand_tok = tree_tables(token_segment, token_valid, segment_parent[0])
    key_bits = jnp.where(token_valid == 1, 1 << token_segment, 0)[None]
    query_bits = ((1 << token_segment) | (1 << parent_tok) | (1 << grand_tok))[:, None]
    cos_table, sin_table = rope_tables(position, HEAD)
    cos_table, sin_table = cos_table[:, 0, : HEAD // 2], sin_table[:, 0, : HEAD // 2]
    valid_rows = lax.dynamic_slice_in_dim(token_valid, row_start, row_count)
    valid_rows = valid_rows.astype(jnp.float32)[:, None]
    (
        normed_in,
        queries,
        keys,
        values,
        attended,
        mass,
        attention_pre,
        middle,
        normed_mid,
        first_sums,
    ) = attention_forward(
        hidden_in,
        attention_gain,
        cos_table,
        sin_table,
        query_bits,
        key_bits,
        query_weight,
        key_weight,
        value_weight,
        output_weight,
        attention_post_gain,
        feedforward_gain,
        valid_rows,
    )
    mid_tree, hidden, mix, gelu_value, mid_near, block_out, ffpre_low, second_sums = (
        feedforward_forward(
            normed_mid,
            middle,
            cotangent,
            valid_rows,
            feedforward_post_gain,
            gate_weight,
            up_weight,
            down_weight,
        )
    )
    ffpre_tree, gate_back, up_back, mid_far, middle_back, pre_low, third_sums = (
        feedforward_backward(
            ffpre_low,
            middle,
            attention_pre,
            cotangent,
            valid_rows,
            feedforward_gain,
            attention_post_gain,
            normed_mid,
            gate_weight,
            up_weight,
            down_weight,
            mix,
            gelu_value,
        )
    )
    (
        pre_tree,
        mid_begun,
        ffpre_every,
        projection_back,
        attention_grads,
        input_grad,
        sums,
    ) = attention_backward(
        pre_low,
        cos_table,
        sin_table,
        query_bits,
        key_bits,
        jnp.concatenate([query_weight, key_weight, value_weight]),
        output_weight,
        queries,
        keys,
        values,
        attended,
        mass,
        hidden_in,
        attention_gain,
        middle_back,
        valid_rows,
        (first_sums, second_sums, third_sums),
        normed_in,
        mid_near,
        ffpre_low,
    )
    attention_grads = lax.psum(attention_grads, "replica").astype(jnp.float32)
    sizes = [query_weight.shape[0], key_weight.shape[0], value_weight.shape[0]]
    query_sum, key_sum, value_sum, output_sum = jnp.split(
        attention_grads, [sizes[0], sizes[0] + sizes[1], sum(sizes)]
    )
    gate_sum, up_sum, down_sum, mid_rows, back_rows = feedforward_grads(
        mid_near,
        mid_far,
        ffpre_every,
        mid_tree,
        ffpre_tree,
        hidden,
        gate_back,
        up_back,
        gate_weight,
        up_weight,
        down_weight,
        mid_begun,
    )
    gate_sum, up_sum, down_sum = last_grads(
        gate_sum, up_sum, down_sum, mid_rows, back_rows, gate_weight, up_weight, down_weight
    )
    smalls = jnp.sum(lax.all_gather(sums, ("replica", "shard")), axis=0)
    gain_one, gain_three, gain_two, gain_four = smalls[0], smalls[1], smalls[2], smalls[3]
    totals = jnp.sum(smalls[4:], axis=1)
    squares_all = jnp.stack([totals[2], totals[3], totals[0], totals[1]])
    valid_all = totals[4]
    stream_rms = jnp.sqrt(squares_all / valid_all)
    return (
        block_out,
        input_grad,
        query_sum,
        key_sum,
        value_sum,
        output_sum,
        gate_sum,
        up_sum,
        down_sum,
        gain_one,
        gain_two,
        gain_three,
        gain_four,
        stream_rms,
    )


def solution(mesh):
    heads_fit = mesh.shape["shard"] == HEADS and mesh.shape["replica"] > 2
    return jax.shard_map(
        shards_heads if heads_fit else shards_generic,
        mesh=mesh,
        in_specs=(
            P(("replica", "shard"), None),
            P(("replica", "shard"), None),
            P("replica"),
            P("replica"),
            P("replica", None),
            P("shard", None),
            P("shard", None),
            P("shard", None),
            P("shard", None),
            P("shard", None),
            P("shard", None),
            P("shard", None),
            P(),
            P(),
            P(),
            P(),
        ),
        out_specs=(
            P(("replica", "shard"), None),
            P(("replica", "shard"), None),
            P("shard", None),
            P("shard", None),
            P("shard", None),
            P("shard", None),
            P("shard", None),
            P("shard", None),
            P("shard", None),
            P(),
            P(),
            P(),
            P(),
            P(),
        ),
        check_vma=False,
    )
```

```python
import functools
import math

import jax
import jax.numpy as jnp
from jax import lax
from jax.experimental import pallas as pl
from jax.experimental.pallas import tpu as pltpu
from jax.sharding import PartitionSpec as P

HEADS = 8
KV_HEADS = 4
HEAD = 256


norm_eps = 1e-06
score_cap = 50.0


def norm_rows(stream, norm_gain):
    factor = lax.rsqrt(jnp.mean(stream * stream, axis=-1, keepdims=True) + norm_eps)
    return stream * factor * (1.0 + norm_gain)


def rotate(values, cos_table, sin_table):
    half_width = values.shape[-1] // 2
    turned = jnp.concatenate([-values[..., half_width:], values[..., :half_width]], axis=-1)
    return values * cos_table + turned * sin_table


def rotate_back(gradient, cos_table, sin_table):
    half_width = gradient.shape[-1] // 2
    shifted = gradient * sin_table
    unturned = jnp.concatenate([shifted[..., half_width:], -shifted[..., :half_width]], axis=-1)
    return gradient * cos_table + unturned


def rope_tables(position, head_size):
    half_width = head_size // 2
    frequency = jnp.power(10000.0, -jnp.arange(half_width, dtype=jnp.float32) * 2.0 / head_size)
    angles = position.astype(jnp.float32)[:, None] * frequency[None, :]
    angles = jnp.concatenate([angles, angles], axis=-1)[:, None, :]
    return (jnp.cos(angles), jnp.sin(angles))


def tree_tables(segment, valid_mask, parent):
    labels = jnp.arange(parent.shape[0], dtype=jnp.int32)
    member = (segment[:, None] == labels[None, :]).astype(jnp.int32)
    lengths = jnp.sum(member * valid_mask[:, None], axis=0)
    starts = jnp.sum((segment[:, None] < labels[None, :]).astype(jnp.int32), axis=0)
    parent_of = (parent[:, None] == labels[None, :]).astype(jnp.int32)
    grandparent = jnp.sum(parent_of * parent[None, :], axis=1)
    parent_len = jnp.sum(parent_of * lengths[None, :], axis=1)
    grand_of = (grandparent[:, None] == labels[None, :]).astype(jnp.int32)
    grand_len = jnp.sum(grand_of * lengths[None, :], axis=1)
    offsets = jnp.where(parent != labels, parent_len, 0) + jnp.where(
        grandparent != parent, grand_len, 0
    )
    token_index = jnp.arange(segment.shape[0], dtype=jnp.int32)
    position = jnp.sum(member * (offsets - starts)[None, :], axis=1) + token_index
    parent_tok = jnp.sum(member * parent[None, :], axis=1)
    grand_tok = jnp.sum(member * grandparent[None, :], axis=1)
    return (position, parent_tok, grand_tok)


def allowed_mask(query_index, query_seg, query_parent, query_grand, key_index, key_seg, key_valid):
    lineage = (
        (key_seg[None, :] == query_seg[:, None])
        | (key_seg[None, :] == query_parent[:, None])
        | (key_seg[None, :] == query_grand[:, None])
    )
    earlier = (key_seg[None, :] != query_seg[:, None]) | (key_index[None, :] < query_index[:, None])
    itself = key_index[None, :] == query_index[:, None]
    return itself | (key_valid[None, :] == 1) & lineage & earlier


def softmax_parts(scores, allowed):
    capped = score_cap * jnp.tanh(scores / score_cap)
    held = jnp.where(allowed, capped, -1000000000.0)
    largest = jnp.max(held, axis=-1, keepdims=True)
    raised = jnp.where(allowed, jnp.exp(held - largest), 0.0)
    total_mass = jnp.sum(raised, axis=-1, keepdims=True)
    return (raised / total_mass, largest + jnp.log(total_mass))


def gated_gelu(gate_lin, up_lin):
    return jax.nn.gelu(gate_lin, approximate=True) * up_lin


def collect_attention(query_weight, key_weight, value_weight, output_weight):
    return (
        lax.all_gather(query_weight, "shard", axis=0, tiled=True),
        lax.all_gather(key_weight, "shard", axis=0, tiled=True),
        lax.all_gather(value_weight, "shard", axis=0, tiled=True),
        lax.all_gather(output_weight, "shard", axis=0, tiled=True),
    )


def group_rows(values):
    return lax.all_gather(values, "shard", axis=0, tiled=True)


def group_sums(values):
    return lax.psum_scatter(values, "shard", scatter_dimension=0, tiled=True)


def shards_generic(
    hidden_in,
    cotangent,
    token_segment,
    token_valid,
    segment_parent,
    query_weight,
    key_weight,
    value_weight,
    output_weight,
    gate_weight,
    up_weight,
    down_weight,
    attention_gain,
    attention_post_gain,
    feedforward_gain,
    feedforward_post_gain,
):
    row_count, model_width = hidden_in.shape
    group_size = HEADS // KV_HEADS
    row_start = lax.axis_index("shard") * row_count
    tree_size = token_segment.shape[0]
    position, parent_tok, grand_tok = tree_tables(token_segment, token_valid, segment_parent[0])
    key_index = jnp.arange(tree_size, dtype=jnp.int32)

    def own_rows(table):
        return lax.dynamic_slice_in_dim(table, row_start, row_count)

    allowed = allowed_mask(
        own_rows(key_index),
        own_rows(token_segment),
        own_rows(parent_tok),
        own_rows(grand_tok),
        key_index,
        token_segment,
        token_valid,
    )
    mask_full = allowed[None, None]
    cos_table, sin_table = rope_tables(own_rows(position), HEAD)
    query_scale = HEAD ** (-0.5)
    valid_rows = own_rows(token_valid).astype(jnp.float32)
    stream = hidden_in.astype(jnp.float32)
    query_all, key_all, value_all, output_all = collect_attention(
        query_weight, key_weight, value_weight, output_weight
    )
    normed_in = norm_rows(stream, attention_gain).astype(jnp.bfloat16)
    query_lin = jnp.einsum("td,qd->tq", normed_in, query_all, preferred_element_type=jnp.float32)
    key_lin = jnp.einsum("td,qd->tq", normed_in, key_all, preferred_element_type=jnp.float32)
    value_lin = jnp.einsum("td,qd->tq", normed_in, value_all, preferred_element_type=jnp.float32)
    queries = (
        rotate(query_lin.reshape(row_count, HEADS, HEAD), cos_table, sin_table) * query_scale
    ).astype(jnp.bfloat16)
    keys_own = (
        rotate(key_lin.reshape(row_count, KV_HEADS, HEAD), cos_table, sin_table)
        .astype(jnp.bfloat16)
        .reshape(row_count, KV_HEADS * HEAD)
    )
    values_own = value_lin.astype(jnp.bfloat16)
    key_tree, value_tree = (
        lax.all_gather(keys_own, "shard", axis=0, tiled=True),
        lax.all_gather(values_own, "shard", axis=0, tiled=True),
    )
    query_groups = queries.reshape(row_count, KV_HEADS, group_size, HEAD)
    key_groups = key_tree.reshape(tree_size, KV_HEADS, HEAD)
    value_groups = value_tree.reshape(tree_size, KV_HEADS, HEAD)
    scores = jnp.einsum(
        "qgrd,kgd->grqk", query_groups, key_groups, preferred_element_type=jnp.float32
    )
    probs, log_total = softmax_parts(scores, mask_full)
    attended = jnp.einsum(
        "grqk,kgd->qgrd",
        probs.astype(jnp.bfloat16),
        value_groups,
        preferred_element_type=jnp.float32,
    )
    attended = attended.astype(jnp.bfloat16).reshape(row_count, HEADS * HEAD)
    attention_pre = jnp.dot(attended, output_all, preferred_element_type=jnp.float32)
    attention_branch = norm_rows(attention_pre, attention_post_gain)
    middle = stream + attention_branch
    normed_mid = norm_rows(middle, feedforward_gain).astype(jnp.bfloat16)
    mid_tree = group_rows(normed_mid)
    gate_lin = jnp.einsum("td,fd->tf", mid_tree, gate_weight, preferred_element_type=jnp.float32)
    up_lin = jnp.einsum("td,fd->tf", mid_tree, up_weight, preferred_element_type=jnp.float32)
    hidden = gated_gelu(gate_lin, up_lin).astype(jnp.bfloat16)
    feedforward_pre = group_sums(jnp.dot(hidden, down_weight, preferred_element_type=jnp.float32))
    feedforward_branch = norm_rows(feedforward_pre, feedforward_post_gain)
    result = middle + feedforward_branch
    squares = jnp.stack(
        [
            jnp.sum(valid_rows[:, None] * summand * summand)
            for summand in (stream, attention_branch, feedforward_branch, result)
        ]
    )
    valid_total = jnp.sum(valid_rows) * model_width
    squares_all, valid_all = lax.psum((squares, valid_total), ("replica", "shard"))
    seed_grad = cotangent.astype(jnp.float32) * valid_rows[:, None]
    unused_four, pull_four = jax.vjp(norm_rows, feedforward_pre, feedforward_post_gain)
    ffpre_back, grad_four = pull_four(seed_grad)
    ffpre_low = ffpre_back.astype(jnp.bfloat16)
    ffpre_tree = group_rows(ffpre_low)
    hidden_back = jnp.einsum(
        "td,fd->tf", ffpre_tree, down_weight, preferred_element_type=jnp.float32
    ).astype(jnp.bfloat16)
    unused_glu, pull_glu = jax.vjp(gated_gelu, gate_lin, up_lin)
    gate_back, up_back = pull_glu(hidden_back.astype(jnp.float32))
    gate_back = gate_back.astype(jnp.bfloat16)
    up_back = up_back.astype(jnp.bfloat16)
    mid_terms = jnp.dot(gate_back, gate_weight, preferred_element_type=jnp.float32) + jnp.dot(
        up_back, up_weight, preferred_element_type=jnp.float32
    )
    mid_back = group_sums(mid_terms)
    gate_grad = jnp.einsum("tf,td->fd", gate_back, mid_tree, preferred_element_type=jnp.float32)
    up_grad = jnp.einsum("tf,td->fd", up_back, mid_tree, preferred_element_type=jnp.float32)
    down_grad = jnp.einsum("tf,td->fd", hidden, ffpre_tree, preferred_element_type=jnp.float32)
    unused_three, pull_three = jax.vjp(norm_rows, middle, feedforward_gain)
    middle_part, grad_three = pull_three(mid_back)
    middle_back = seed_grad + middle_part
    unused_two, pull_two = jax.vjp(norm_rows, attention_pre, attention_post_gain)
    attention_pre_back, grad_two = pull_two(middle_back)
    pre_low = attention_pre_back.astype(jnp.bfloat16)
    query_all, key_all, value_all, output_all = collect_attention(
        query_weight, key_weight, value_weight, output_weight
    )
    attended_back = jnp.einsum(
        "td,qd->tq", pre_low, output_all, preferred_element_type=jnp.float32
    ).astype(jnp.bfloat16)
    scores = jnp.einsum(
        "qgrd,kgd->grqk", query_groups, key_groups, preferred_element_type=jnp.float32
    )
    tanh_value = jnp.tanh(scores / score_cap)
    probs_back = jnp.where(
        mask_full,
        jnp.exp(jnp.where(mask_full, score_cap * tanh_value - log_total, -1000000000.0)),
        0.0,
    )
    back_groups = attended_back.reshape(row_count, KV_HEADS, group_size, HEAD)
    prob_grads = jnp.einsum(
        "qgrd,kgd->grqk", back_groups, value_groups, preferred_element_type=jnp.float32
    )
    inner_sum = jnp.sum(probs_back * prob_grads, axis=-1, keepdims=True)
    score_back = (probs_back * (prob_grads - inner_sum) * (1.0 - tanh_value * tanh_value)).astype(
        jnp.bfloat16
    )
    query_back = jnp.einsum(
        "grqk,kgd->qgrd", score_back, key_groups, preferred_element_type=jnp.float32
    ).reshape(row_count, HEADS, HEAD)
    key_back = jnp.einsum(
        "grqk,qgrd->kgd", score_back, query_groups, preferred_element_type=jnp.float32
    ).reshape(tree_size, KV_HEADS * HEAD)
    value_back = jnp.einsum(
        "grqk,qgrd->kgd",
        probs_back.astype(jnp.bfloat16),
        back_groups,
        preferred_element_type=jnp.float32,
    ).reshape(tree_size, KV_HEADS * HEAD)
    key_sum, value_sum = (
        lax.psum_scatter(key_back, "shard", scatter_dimension=0, tiled=True),
        lax.psum_scatter(value_back, "shard", scatter_dimension=0, tiled=True),
    )
    query_low = (
        rotate_back(query_back * query_scale, cos_table, sin_table)
        .astype(jnp.bfloat16)
        .reshape(row_count, HEADS * HEAD)
    )
    key_low = (
        rotate_back(key_sum.reshape(row_count, KV_HEADS, HEAD), cos_table, sin_table)
        .astype(jnp.bfloat16)
        .reshape(row_count, KV_HEADS * HEAD)
    )
    value_low = value_sum.astype(jnp.bfloat16)
    normed_back = (
        jnp.dot(query_low, query_all, preferred_element_type=jnp.float32)
        + jnp.dot(key_low, key_all, preferred_element_type=jnp.float32)
        + jnp.dot(value_low, value_all, preferred_element_type=jnp.float32)
    )
    output_local = jnp.einsum("tq,td->qd", attended, pre_low, preferred_element_type=jnp.float32)
    query_local = jnp.einsum("tq,td->qd", query_low, normed_in, preferred_element_type=jnp.float32)
    key_local = jnp.einsum("tq,td->qd", key_low, normed_in, preferred_element_type=jnp.float32)
    value_local = jnp.einsum("tq,td->qd", value_low, normed_in, preferred_element_type=jnp.float32)
    query_part, key_part, value_part, output_part = (
        lax.psum_scatter(query_local, "shard", scatter_dimension=0, tiled=True),
        lax.psum_scatter(key_local, "shard", scatter_dimension=0, tiled=True),
        lax.psum_scatter(value_local, "shard", scatter_dimension=0, tiled=True),
        lax.psum_scatter(output_local, "shard", scatter_dimension=0, tiled=True),
    )
    unused_one, pull_one = jax.vjp(norm_rows, stream, attention_gain)
    stream_part, grad_one = pull_one(normed_back)
    input_grad = middle_back + stream_part
    query_sum, key_total, value_total, output_sum, gate_sum, up_sum, down_sum = lax.psum(
        (query_part, key_part, value_part, output_part, gate_grad, up_grad, down_grad), "replica"
    )
    gain_one, gain_two, gain_three, gain_four = lax.psum(
        (grad_one, grad_two, grad_three, grad_four), ("replica", "shard")
    )
    stream_rms = jnp.sqrt(squares_all / valid_all)
    return (
        result.astype(jnp.bfloat16),
        input_grad,
        query_sum,
        key_total,
        value_total,
        output_sum,
        gate_sum,
        up_sum,
        down_sum,
        gain_one,
        gain_two,
        gain_three,
        gain_four,
        stream_rms,
    )


def norm_factor(stream):
    return lax.rsqrt(jnp.mean(stream * stream, axis=-1, keepdims=True) + norm_eps)


def norm_back(stream, norm_gain, gradient):
    factor = norm_factor(stream)
    weighted = gradient * (1.0 + norm_gain)
    inner = jnp.mean(weighted * stream, axis=-1, keepdims=True)
    back = factor * weighted - stream * (factor * factor * factor * inner)
    return back, gradient * stream * factor


def dot_nt(left, right):
    return lax.dot_general(
        left, right, (((1,), (1,)), ((), ())), preferred_element_type=jnp.float32
    )


def dot_nn(left, right):
    return lax.dot_general(
        left, right, (((1,), (0,)), ((), ())), preferred_element_type=jnp.float32
    )


def dot_tn(left, right):
    return lax.dot_general(
        left, right, (((0,), (0,)), ((), ())), preferred_element_type=jnp.float32
    )


def sum_low(values):
    return lax.psum_scatter(
        values.astype(jnp.bfloat16), "shard", scatter_dimension=0, tiled=True
    ).astype(jnp.float32)


def gelu_parts(gate_lin):
    root = math.sqrt(2.0 / math.pi)
    square = gate_lin * gate_lin
    tanh_value = jnp.tanh(root * gate_lin * (1.0 + 0.044715 * square))
    half_up = 0.5 * (1.0 + tanh_value)
    slope = half_up + 0.5 * gate_lin * (1.0 - tanh_value * tanh_value) * root * (
        1.0 + 3.0 * 0.044715 * square
    )
    return gate_lin * half_up, slope


MESH_ID = pl.DeviceIdType.MESH
VMEM_BYTES = 62 * 2**20
ROOT = math.sqrt(2.0 / math.pi)


class Plane:
    def __init__(self):
        self.me = lax.axis_index("shard")
        core = lax.rem(self.me, 2)
        x = lax.rem(lax.div(self.me, 2), 2)
        y = lax.div(self.me, 4)
        self.core = core
        self.own_chip = 2 * y + x
        self.x_chip = 2 * y + 1 - x
        self.y_chip = 2 * (1 - y) + x
        self.diag_chip = 2 * (1 - y) + 1 - x
        self.mate = self.me + 1 - 2 * core
        self.x_dev = 2 * self.x_chip + core
        self.y_dev = 2 * self.y_chip + core
        self.diag_dev = 2 * self.diag_chip + core

    def near(self):
        return [{"shard": dev} for dev in (self.mate, self.x_dev, self.y_dev)]


class Wires:
    def __init__(self, send_sem, recv_sem):
        self.send_sem, self.recv_sem = send_sem, recv_sem
        self.sent = []

    def send(self, source, target, device):
        at = len(self.sent)
        copy = pltpu.make_async_remote_copy(
            src_ref=source,
            dst_ref=target,
            send_sem=self.send_sem.at[at],
            recv_sem=self.recv_sem.at[at],
            device_id=device if isinstance(device, dict) else {"shard": device},
            device_id_type=MESH_ID,
        )
        copy.start()
        self.sent.append(copy)
        return copy

    def finish(self):
        for copy in self.sent:
            copy.wait_send()


def greet(devices):
    barrier = pltpu.get_barrier_semaphore()
    for device in devices:
        pl.semaphore_signal(barrier, inc=1, device_id=device, device_id_type=MESH_ID)
    pl.semaphore_wait(barrier, len(devices))


def block_rows(ref, start, size, step=16):
    return ref.at[pl.ds(pl.multiple_of(start, step), size)]


def add_row(sums, at, term):
    sums[at : at + 1, :] += jnp.sum(term, axis=0, keepdims=True)


def by_rows(count, body, size=32):
    def step(at, carry):
        body(pl.ds(pl.multiple_of(at * size, size), size))
        return carry

    lax.fori_loop(0, count // size, step, 0)


def column_tile(width):
    return max(t for t in range(128, 769, 128) if width % t == 0)


def by_columns(width, body):
    tile = column_tile(width)

    def step(at, carry):
        body(pl.ds(pl.multiple_of(at * tile, 128), tile))
        return carry

    lax.fori_loop(0, width // tile, step, 0)


def gather_tree(wires, plane, own, tree, rows, use):
    half = rows // 2

    def part(dev, start, size):
        return block_rows(tree, dev * rows + start, size)

    def own_part(start, size):
        return own.at[pl.ds(start, size)]

    me, mate = plane.me, plane.mate
    first_x = wires.send(own_part(0, half), part(me, 0, half), plane.x_dev)
    first_y = wires.send(own_part(half, half), part(me, half, half), plane.y_dev)
    to_mate = wires.send(own_part(0, rows), part(me, 0, rows), mate)
    rest_x = wires.send(own_part(half, half), part(me, half, half), plane.x_dev)
    rest_y = wires.send(own_part(0, half), part(me, 0, half), plane.y_dev)
    to_mate.wait_recv()
    use(plane.own_chip)
    first_x.wait_recv()
    turn_y = wires.send(part(plane.x_dev, 0, half), part(plane.x_dev, 0, half), plane.y_dev)
    first_y.wait_recv()
    turn_x = wires.send(part(plane.y_dev, half, half), part(plane.y_dev, half, half), plane.x_dev)
    rest_x.wait_recv()
    mate_x = wires.send(part(plane.x_dev, 0, rows), part(plane.x_dev, 0, rows), mate)
    rest_y.wait_recv()
    mate_y = wires.send(part(plane.y_dev, 0, rows), part(plane.y_dev, 0, rows), mate)
    mate_x.wait_recv()
    use(plane.x_chip)
    turn_y.wait_recv()
    turn_x.wait_recv()
    mate_diag = wires.send(part(plane.diag_dev, 0, rows), part(plane.diag_dev, 0, rows), mate)
    mate_y.wait_recv()
    use(plane.y_chip)
    mate_diag.wait_recv()
    use(plane.diag_chip)


GATHER_COPIES = 10
DIAG, SIDE_X, SIDE_Y, OWN = range(4)


def scatter_scratch(rows, width):
    half = rows // 2
    low = jnp.bfloat16
    return [
        pltpu.VMEM((3, rows, width), jnp.float32),
        pltpu.VMEM((2 * rows, column_tile(width)), jnp.float32),
        pltpu.VMEM((2, rows, width), low),
        pltpu.VMEM((4, rows, width), low),
        pltpu.VMEM((3, half, width), low),
        pltpu.VMEM((3, half, width), low),
        pltpu.VMEM((3, half, width), low),
        pltpu.VMEM((3, half, width), low),
    ]


class Scatter:
    def __init__(self, wires, plane, scratch, product, total, order, loads=()):
        self.loads = list(loads)
        self.wires, self.plane, self.product, self.total = wires, plane, product, total
        self.sums, self.piece, self.mate_out, self.mate_in = scratch[:4]
        self.x_out, self.x_in, self.y_out, self.y_in = scratch[4:]
        self.order = order
        self.slots = {place: (0, 1, 2, 0)[at] for at, place in enumerate(order)}
        if order[0] == OWN:
            self.slots[SIDE_Y] = self.slots[DIAG]
        self.rows, self.width = total.shape
        self.half = self.rows // 2
        self.to_mate = {}

    def produce(self, place):
        plane, rows = self.plane, self.rows
        chip = (plane.diag_chip, plane.x_chip, plane.y_chip, plane.own_chip)[place]
        slot, at = self.slots[place], self.order.index(place)
        out_slot = at % 2
        if at >= 2:
            self.to_mate[self.order[at - 2]].wait_send()
        while self.loads:
            self.loads.pop().wait()

        def tile(columns):
            self.piece[...] = self.product(chip, columns)
            self.sums[slot, :, columns] = self.piece[block_at(plane.core * rows, rows), :]
            self.mate_out[out_slot, :, columns] = self.piece[
                block_at((1 - plane.core) * rows, rows), :
            ].astype(jnp.bfloat16)

        by_columns(self.width, tile)
        self.to_mate[place] = self.wires.send(
            self.mate_out.at[out_slot], self.mate_in.at[place], plane.mate
        )

    def low_part(self, out, out_slot, place, start, more=None):
        def step(at):
            there = pl.ds(pl.multiple_of(start + at.start, 16), at.size)
            value = self.sums[self.slots[place], there, :] + self.mate_in[
                place, there, :
            ].astype(jnp.float32)
            if more is not None:
                value += more[0, at, :].astype(jnp.float32)
            out[out_slot, at, :] = value.astype(jnp.bfloat16)

        by_rows(self.half, step)

    def to_x(self, slot):
        return self.wires.send(self.x_out.at[slot], self.x_in.at[slot], self.plane.x_dev)

    def to_y(self, slot):
        return self.wires.send(self.y_out.at[slot], self.y_in.at[slot], self.plane.y_dev)

    def send_diag(self):
        self.to_mate[DIAG].wait_recv()
        self.low_part(self.x_out, 0, DIAG, 0)
        self.x_first = self.to_x(0)
        self.low_part(self.y_out, 0, DIAG, self.half)
        self.y_first = self.to_y(0)

    def send_x(self):
        self.to_mate[SIDE_X].wait_recv()
        self.low_part(self.x_out, 1, SIDE_X, 0)
        self.x_next = self.to_x(1)

    def send_y(self):
        self.to_mate[SIDE_Y].wait_recv()
        self.low_part(self.y_out, 1, SIDE_Y, self.half)
        self.y_next = self.to_y(1)

    def turn(self):
        self.y_first.wait_recv()
        self.low_part(self.x_out, 2, SIDE_X, self.half, self.y_in)
        self.x_last = self.to_x(2)
        self.x_first.wait_recv()
        self.low_part(self.y_out, 2, SIDE_Y, 0, self.x_in)
        self.y_last = self.to_y(2)

    def finish(self):
        self.to_mate[OWN].wait_recv()
        late = [self.x_next, self.y_next, self.x_last, self.y_last]
        for copy in late:
            copy.wait_recv()
        for start, x_slot, y_slot in ((0, 1, 2), (self.half, 2, 1)):

            def step(at, start=start, x_slot=x_slot, y_slot=y_slot):
                there = pl.ds(pl.multiple_of(start + at.start, 16), at.size)
                self.total[there, :] = (
                    self.sums[self.slots[OWN], there, :]
                    + self.mate_in[OWN, there, :].astype(jnp.float32)
                    + self.x_in[x_slot, at, :].astype(jnp.float32)
                    + self.y_in[y_slot, at, :].astype(jnp.float32)
                )

            by_rows(self.half, step)
        for copy in [self.x_first, self.y_first] + late:
            copy.wait_send()
        for place in self.order[2:]:
            self.to_mate[place].wait_send()


def scatter_sum(wires, plane, scratch, product, total, before=lambda chip: None, meanwhile=()):
    scatter = Scatter(wires, plane, scratch, product, total, (DIAG, SIDE_X, SIDE_Y, OWN))
    work = iter(tuple(meanwhile) + (lambda: None,) * 2)
    before(plane.diag_chip)
    scatter.produce(DIAG)
    before(plane.x_chip)
    scatter.produce(SIDE_X)
    scatter.send_diag()
    before(plane.y_chip)
    scatter.produce(SIDE_Y)
    scatter.send_x()
    before(plane.own_chip)
    scatter.produce(OWN)
    scatter.send_y()
    next(work)()
    scatter.turn()
    next(work)()
    scatter.finish()


def gather_and_scatter(wires, plane, own, tree, rows, use, scatter):
    half = rows // 2

    def part(dev, start, size):
        return block_rows(tree, dev * rows + start, size)

    def own_part(start, size):
        return own.at[pl.ds(start, size)]

    def onward(dev, start, size, device):
        return wires.send(part(dev, start, size), part(dev, start, size), device)

    me, mate, x_dev, y_dev = plane.me, plane.mate, plane.x_dev, plane.y_dev
    first_x = wires.send(own_part(0, half), part(me, 0, half), x_dev)
    first_y = wires.send(own_part(half, half), part(me, half, half), y_dev)
    to_mate = wires.send(own_part(0, rows), part(me, 0, rows), mate)
    to_mate.wait_recv()
    use(plane.own_chip)
    first_x.wait_recv()
    turn_y = onward(x_dev, 0, half, y_dev)
    first_y.wait_recv()
    turn_x = onward(y_dev, half, half, x_dev)
    rest_x = wires.send(own_part(half, half), part(me, half, half), x_dev)
    rest_y = wires.send(own_part(0, half), part(me, 0, half), y_dev)
    scatter.produce(OWN)
    turn_y.wait_recv()
    turn_x.wait_recv()
    mate_diag = onward(plane.diag_dev, 0, rows, mate)
    mate_diag.wait_recv()
    use(plane.diag_chip)
    rest_x.wait_recv()
    mate_x = onward(x_dev, 0, rows, mate)
    rest_y.wait_recv()
    mate_y = onward(y_dev, 0, rows, mate)
    scatter.produce(DIAG)
    mate_x.wait_recv()
    use(plane.x_chip)
    scatter.send_diag()
    scatter.produce(SIDE_X)
    mate_y.wait_recv()
    use(plane.y_chip)
    scatter.send_x()
    scatter.produce(SIDE_Y)
    copies = [first_x, first_y, to_mate, turn_y, turn_x, rest_x, rest_y, mate_diag, mate_x, mate_y]
    for copy in copies:
        copy.wait_send()
    scatter.send_y()
    scatter.turn()
    scatter.finish()


SCATTER_COPIES = 10


def block_at(start, size):
    return pl.ds(pl.multiple_of(start, 16), size)


def load(source, target, sem):
    copy = pltpu.make_async_copy(source, target, sem)
    copy.start()
    return copy


def replica_steps(replicas, near):
    return [step for step in range(1, replicas) if (min(step, replicas - step) == 1) == near]


def replica_device(replicas, step):
    return {"replica": lax.rem(lax.axis_index("replica") + step, replicas)}


def send_over(wires, source, target, replicas, steps):
    return [
        wires.send(
            source, target.at[steps.index(replicas - step)], replica_device(replicas, step)
        )
        for step in steps
    ]


def forward_kernel(
    replicas,
    own,
    middle,
    cotangent,
    valid,
    gain,
    gate_hbm,
    up_hbm,
    down_hbm,
    tree_out,
    hidden_out,
    mix_out,
    gelu_out,
    every_out,
    block_out,
    back_out,
    sums_out,
    total,
    tree,
    gate_w,
    up_w,
    down_w,
    hidden,
    mix,
    gelu,
    gate_lin,
    up_lin,
    send_sem,
    recv_sem,
    local_sem,
    *scratch,
):
    plane = Plane()
    rows = own.shape[0]
    wires = Wires(send_sem, recv_sem)
    loads = [
        load(gate_hbm, gate_w, local_sem.at[0]),
        load(up_hbm, up_w, local_sem.at[1]),
        load(down_hbm, down_w, local_sem.at[2]),
    ]
    steps = replica_steps(replicas, True)
    greet(plane.near() + [replica_device(replicas, step) for step in steps])
    tree[block_at(plane.me * rows, rows), :] = own[...]
    stores = []

    def use(chip):
        order = len(stores) // 3
        slot = order % 2
        if order == 0:
            loads[0].wait()
            loads[1].wait()
        if order >= 2:
            stores[3 * (order - 2) + 1].wait()
            stores[3 * (order - 2) + 2].wait()
        there = block_at(chip * 2 * rows, 2 * rows)
        gate_lin[...] = dot_nt(tree[there, :], gate_w[...])
        up_lin[...] = dot_nt(tree[there, :], up_w[...])

        def step(at):
            gelu_value, slope = gelu_parts(gate_lin[at, :])
            up_value = up_lin[at, :]
            mix[slot, at, :] = (up_value * slope).astype(jnp.bfloat16)
            gelu[slot, at, :] = gelu_value.astype(jnp.bfloat16)
            hidden[block_at(chip * 2 * rows + at.start, at.size), :] = (
                gelu_value * up_value
            ).astype(jnp.bfloat16)

        by_rows(2 * rows, step, 16)
        base = 3 + 3 * order
        stores.append(load(hidden.at[there], hidden_out.at[there], local_sem.at[base]))
        stores.append(load(mix.at[slot], mix_out.at[there], local_sem.at[base + 1]))
        stores.append(load(gelu.at[slot], gelu_out.at[there], local_sem.at[base + 2]))

    over = send_over(wires, own, every_out, replicas, steps)

    def product(chip, columns):
        return dot_nn(hidden[block_at(chip * 2 * rows, 2 * rows), :], down_w[:, columns])

    scatter = Scatter(
        wires, plane, scratch, product, total, (OWN, DIAG, SIDE_X, SIDE_Y), loads[2:]
    )
    gather_and_scatter(wires, plane, own, tree, rows, use, scatter)
    tree_store = load(tree, tree_out, local_sem.at[15])
    sums_out[...] = jnp.zeros_like(sums_out)

    def finish(at):
        value = total[at, :]
        gradient = cotangent[at, :].astype(jnp.float32) * valid[at, :]
        branch = norm_rows(value, gain[...])
        result = middle[at, :] + branch
        block_out[at, :] = result.astype(jnp.bfloat16)
        back, gain_terms = norm_back(value, gain[...], gradient)
        back_out[at, :] = back.astype(jnp.bfloat16)
        add_row(sums_out, 0, gain_terms)
        add_row(sums_out, 1, valid[at, :] * branch * branch)
        add_row(sums_out, 2, valid[at, :] * result * result)

    by_rows(rows, finish)
    for copy in over:
        copy.wait()
    for copy in stores[0:1] + stores[3:4] + stores[6:] + [tree_store]:
        copy.wait()


def any_specs(count):
    return [pl.BlockSpec(memory_space=pl.ANY)] * count


def vmem_specs(count):
    return [pl.BlockSpec(memory_space=pltpu.VMEM)] * count


def remote_params(identity):
    return pltpu.CompilerParams(
        collective_id=identity, has_side_effects=True, vmem_limit_bytes=VMEM_BYTES
    )


def feedforward_forward(
    own, middle, cotangent, valid, gain, gate_weight, up_weight, down_weight
):
    rows, width = own.shape
    units = gate_weight.shape[0]
    replicas, count = lax.axis_size("replica"), lax.axis_size("shard")
    tree_rows = count * rows
    low, full = jnp.bfloat16, jnp.float32
    copies = GATHER_COPIES + SCATTER_COPIES + replicas - 1
    return pl.pallas_call(
        functools.partial(forward_kernel, replicas),
        out_shape=(
            jax.ShapeDtypeStruct((tree_rows, width), low),
            jax.ShapeDtypeStruct((tree_rows, units), low),
            jax.ShapeDtypeStruct((tree_rows, units), low),
            jax.ShapeDtypeStruct((tree_rows, units), low),
            jax.ShapeDtypeStruct((len(replica_steps(replicas, True)), rows, width), low),
            jax.ShapeDtypeStruct((rows, width), low),
            jax.ShapeDtypeStruct((rows, width), low),
            jax.ShapeDtypeStruct((8, width), full),
        ),
        in_specs=vmem_specs(5) + any_specs(3),
        out_specs=tuple(any_specs(5) + vmem_specs(3)),
        scratch_shapes=[
            pltpu.VMEM((rows, width), full),
            pltpu.VMEM((tree_rows, width), low),
            pltpu.VMEM((units, width), low),
            pltpu.VMEM((units, width), low),
            pltpu.VMEM((units, width), low),
            pltpu.VMEM((tree_rows, units), low),
            pltpu.VMEM((2, 2 * rows, units), low),
            pltpu.VMEM((2, 2 * rows, units), low),
            pltpu.VMEM((2 * rows, units), full),
            pltpu.VMEM((2 * rows, units), full),
            pltpu.SemaphoreType.DMA((copies,)),
            pltpu.SemaphoreType.DMA((copies,)),
            pltpu.SemaphoreType.DMA((16,)),
        ]
        + scatter_scratch(rows, width),
        compiler_params=remote_params(1),
        cost_estimate=pl.CostEstimate(
            flops=6 * tree_rows * units * width, bytes_accessed=40 * 2**20, transcendentals=0
        ),
    )(own, middle, cotangent, valid, gain[None], gate_weight, up_weight, down_weight)


def backward_kernel(
    replicas,
    own,
    middle,
    attention_pre,
    cotangent,
    valid,
    gain,
    post_gain,
    mid_own,
    gate_hbm,
    up_hbm,
    down_hbm,
    mix_hbm,
    gelu_hbm,
    tree_out,
    gate_out,
    up_out,
    every_out,
    middle_out,
    back_out,
    sums_out,
    total,
    tree,
    gate_w,
    up_w,
    down_w,
    gate_back,
    up_back,
    mix,
    gelu,
    hidden_back,
    send_sem,
    recv_sem,
    local_sem,
    *scratch,
):
    plane = Plane()
    rows = own.shape[0]
    wires = Wires(send_sem, recv_sem)
    chips = [plane.own_chip, plane.diag_chip, plane.x_chip, plane.y_chip]

    def fetch(order):
        there = block_at(chips[order] * 2 * rows, 2 * rows)
        return [
            load(mix_hbm.at[there], mix.at[order % 2], local_sem.at[3 + 2 * order]),
            load(gelu_hbm.at[there], gelu.at[order % 2], local_sem.at[4 + 2 * order]),
        ]

    loads = [load(down_hbm, down_w, local_sem.at[2])]
    fetched = [fetch(0), fetch(1)]
    loads += [
        load(gate_hbm, gate_w, local_sem.at[0]),
        load(up_hbm, up_w, local_sem.at[1]),
    ]
    steps = replica_steps(replicas, False)
    greet(plane.near() + [replica_device(replicas, step) for step in steps])
    tree[block_at(plane.me * rows, rows), :] = own[...]
    stores = []

    def use(chip):
        order = len(stores) // 2
        slot = order % 2
        if order == 0:
            loads[0].wait()
        there = block_at(chip * 2 * rows, 2 * rows)
        hidden_back[...] = dot_nt(tree[there, :], down_w[...])
        for copy in fetched[order]:
            copy.wait()

        def step(at):
            value = hidden_back[at, :].astype(jnp.bfloat16).astype(jnp.float32)
            here = block_at(chip * 2 * rows + at.start, at.size)
            gate_back[here, :] = (value * mix[slot, at, :].astype(jnp.float32)).astype(jnp.bfloat16)
            up_back[here, :] = (value * gelu[slot, at, :].astype(jnp.float32)).astype(jnp.bfloat16)

        by_rows(2 * rows, step, 16)
        if order + 2 < 4:
            fetched.append(fetch(order + 2))
        base = 11 + 2 * order
        stores.append(load(gate_back.at[there], gate_out.at[there], local_sem.at[base]))
        stores.append(load(up_back.at[there], up_out.at[there], local_sem.at[base + 1]))

    over = send_over(wires, mid_own, every_out, replicas, steps)

    def product(chip, columns):
        there = block_at(chip * 2 * rows, 2 * rows)
        return dot_nn(gate_back[there, :], gate_w[:, columns]) + dot_nn(
            up_back[there, :], up_w[:, columns]
        )

    scatter = Scatter(
        wires, plane, scratch, product, total, (OWN, DIAG, SIDE_X, SIDE_Y), loads[1:]
    )
    gather_and_scatter(wires, plane, own, tree, rows, use, scatter)
    tree_store = load(tree, tree_out, local_sem.at[19])
    sums_out[...] = jnp.zeros_like(sums_out)

    def finish(at):
        back, gain_terms = norm_back(middle[at, :], gain[...], total[at, :])
        back += cotangent[at, :].astype(jnp.float32) * valid[at, :]
        middle_out[at, :] = back
        add_row(sums_out, 0, gain_terms)
        back, gain_terms = norm_back(attention_pre[at, :], post_gain[...], back)
        back_out[at, :] = back.astype(jnp.bfloat16)
        add_row(sums_out, 1, gain_terms)

    by_rows(rows, finish)
    for copy in over:
        copy.wait()
    for copy in stores + [tree_store]:
        copy.wait()


def feedforward_backward(
    own,
    middle,
    attention_pre,
    cotangent,
    valid,
    gain,
    post_gain,
    mid_own,
    gate_weight,
    up_weight,
    down_weight,
    mix,
    gelu,
):
    rows, width = own.shape
    units = gate_weight.shape[0]
    replicas, count = lax.axis_size("replica"), lax.axis_size("shard")
    tree_rows = count * rows
    low, full = jnp.bfloat16, jnp.float32
    copies = GATHER_COPIES + SCATTER_COPIES + replicas - 1
    return pl.pallas_call(
        functools.partial(backward_kernel, replicas),
        out_shape=(
            jax.ShapeDtypeStruct((tree_rows, width), low),
            jax.ShapeDtypeStruct((tree_rows, units), low),
            jax.ShapeDtypeStruct((tree_rows, units), low),
            jax.ShapeDtypeStruct((len(replica_steps(replicas, False)), rows, width), low),
            jax.ShapeDtypeStruct((rows, width), full),
            jax.ShapeDtypeStruct((rows, width), low),
            jax.ShapeDtypeStruct((8, width), full),
        ),
        in_specs=vmem_specs(7) + any_specs(6),
        out_specs=tuple(any_specs(4) + vmem_specs(3)),
        scratch_shapes=[
            pltpu.VMEM((rows, width), full),
            pltpu.VMEM((tree_rows, width), low),
            pltpu.VMEM((units, width), low),
            pltpu.VMEM((units, width), low),
            pltpu.VMEM((units, width), low),
            pltpu.VMEM((tree_rows, units), low),
            pltpu.VMEM((tree_rows, units), low),
            pltpu.VMEM((2, 2 * rows, units), low),
            pltpu.VMEM((2, 2 * rows, units), low),
            pltpu.VMEM((2 * rows, units), full),
            pltpu.SemaphoreType.DMA((copies,)),
            pltpu.SemaphoreType.DMA((copies,)),
            pltpu.SemaphoreType.DMA((20,)),
        ]
        + scatter_scratch(rows, width),
        compiler_params=remote_params(2),
        cost_estimate=pl.CostEstimate(
            flops=6 * tree_rows * units * width, bytes_accessed=40 * 2**20, transcendentals=0
        ),
    )(
        own,
        middle,
        attention_pre,
        cotangent,
        valid,
        gain[None],
        post_gain[None],
        mid_own,
        gate_weight,
        up_weight,
        down_weight,
        mix,
        gelu,
    )


class Copy:
    def __init__(self, build):
        self.build = build

    def start(self):
        self.build().start()

    def wait_recv(self):
        self.build().wait_recv()

    def wait_send(self):
        self.build().wait_send()


class PlaneGather:
    def __init__(self, plane, own, tree, rows, send_sem, recv_sem, local_sem, base):
        half = rows // 2
        me, mate, x_dev, y_dev = plane.me, plane.mate, plane.x_dev, plane.y_dev
        diag = plane.diag_dev
        self.started = []

        def part(dev, start, size):
            return block_rows(tree, dev * rows + start, size)

        def copy(source, target, device):
            at = base + len(self.started)

            def build():
                return pltpu.make_async_remote_copy(
                    src_ref=source(),
                    dst_ref=target(),
                    send_sem=send_sem.at[at],
                    recv_sem=recv_sem.at[at],
                    device_id={"shard": device},
                    device_id_type=MESH_ID,
                )

            self.started.append(Copy(build))
            return self.started[-1]

        def from_own(start, size, device):
            return copy(
                lambda: own().at[pl.ds(start, size)], lambda: part(me, start, size), device
            )

        def onward(dev, start, size, device):
            return copy(lambda: part(dev, start, size), lambda: part(dev, start, size), device)

        self.first_x = from_own(0, half, x_dev)
        self.first_y = from_own(half, half, y_dev)
        self.to_mate = from_own(0, rows, mate)
        self.rest_x = from_own(half, half, x_dev)
        self.rest_y = from_own(0, half, y_dev)
        self.turn_y = onward(x_dev, 0, half, y_dev)
        self.turn_x = onward(y_dev, half, half, x_dev)
        self.mate_x = onward(x_dev, 0, rows, mate)
        self.mate_y = onward(y_dev, 0, rows, mate)
        self.mate_diag = onward(diag, 0, rows, mate)
        self.local = lambda: pltpu.make_async_copy(own(), part(me, 0, rows), local_sem)

    def begin(self):
        for copy in (self.first_x, self.first_y, self.to_mate, self.rest_x, self.rest_y):
            copy.start()
        self.local().start()

    def turn(self):
        self.first_x.wait_recv()
        self.turn_y.start()
        self.first_y.wait_recv()
        self.turn_x.start()

    def to_mates(self):
        self.rest_x.wait_recv()
        self.mate_x.start()
        self.rest_y.wait_recv()
        self.mate_y.start()

    def near_rows(self):
        self.local().wait()
        self.to_mate.wait_recv()
        self.mate_x.wait_recv()

    def turned(self):
        self.turn_y.wait_recv()
        self.turn_x.wait_recv()
        self.mate_diag.start()

    def far_rows(self):
        self.mate_y.wait_recv()
        self.mate_diag.wait_recv()

    def finish(self):
        for copy in self.started:
            copy.wait_send()


def grads_kernel(
    replicas,
    mid_near,
    mid_far,
    back_every,
    mid_tree,
    back_tree,
    hidden_hbm,
    gate_back_hbm,
    up_back_hbm,
    gate_hbm,
    up_hbm,
    down_hbm,
    mid_begun,
    gate_out,
    up_out,
    down_out,
    mid_rows,
    back_rows,
    gate_sum,
    up_sum,
    down_sum,
    gate_w,
    up_w,
    down_w,
    mid,
    back,
    own_hidden,
    own_gate,
    own_up,
    hidden,
    gate_back,
    up_back,
    send_sem,
    recv_sem,
    local_sem,
    block_sem,
    weight_sem,
):
    plane = Plane()
    units, width = gate_w.shape
    size = mid.shape[1]
    rows = back_every.shape[1]
    tree_rows = mid_tree.shape[0]
    blocks = tree_rows // size
    half_blocks = blocks // 2
    low = jnp.bfloat16
    y = lax.div(plane.me, 4)
    others = replicas - 1
    last = others * blocks + half_blocks - 1
    weights = [
        pltpu.make_async_copy(source, target, weight_sem.at[at])
        for at, (source, target) in enumerate(
            ((gate_hbm, gate_w), (up_hbm, up_w), (down_hbm, down_w))
        )
    ]
    gathers = []
    far = replica_steps(replicas, False)
    for step in range(others):
        pair = []
        if step + 1 in far:
            mid_own = mid_far.at[far.index(step + 1)]
        else:
            mid_own = mid_near.at[min(step, 1)]
        sources = ((mid_own, mid_rows), (back_every.at[step], back_rows))
        for at, (own, tree) in enumerate(sources):
            count = 2 * step + at
            pair.append(
                PlaneGather(
                    plane,
                    lambda own=own: own,
                    tree.at[step],
                    rows,
                    send_sem,
                    recv_sem,
                    local_sem.at[count],
                    GATHER_COPIES * count,
                )
            )
        gathers.append(pair)

    def own_loads(block, slot):
        there = block_at(block * size, size)
        return [
            pltpu.make_async_copy(source.at[there], target.at[slot], block_sem.at[slot, at])
            for at, (source, target) in enumerate(
                (
                    (mid_tree, mid),
                    (back_tree, back),
                    (hidden_hbm, own_hidden),
                    (gate_back_hbm, own_gate),
                    (up_back_hbm, own_up),
                )
            )
        ]

    def other_loads(block, slot):
        tree = lax.div(block, blocks) - 1
        within = lax.rem(block, blocks)
        part = lax.div(within, half_blocks)
        start = (y + part - 2 * y * part) * half_blocks * size
        there = block_at(start + lax.rem(within, half_blocks) * size, size)
        return [
            pltpu.make_async_copy(source.at[tree, there], target.at[slot], block_sem.at[slot, at])
            for at, (source, target) in enumerate(((mid_rows, mid), (back_rows, back)))
        ]

    def add(total, dot, lhs, rhs, slot, first=False):
        def part(at):
            left = lhs[:, at] if dot is dot_tn else lhs[at, :]
            if first:
                total[at, :] = dot(left, rhs[slot])
            else:
                total[at, :] += dot(left, rhs[slot])

        by_rows(units, part, 384 if dot is dot_tn else units // 2)

    events = {}

    def event(block, *actions):
        events.setdefault(block, []).extend(actions)

    for copy in weights:
        copy.start()
    for copy in own_loads(0, 0):
        copy.start()
    greet(plane.near())
    gathers[0] = gathers[0][1:]
    gathers[0][0].begin()
    for step, pair in enumerate(gathers):
        base = step * blocks
        if len(pair) == 1:
            event(base + 2, pair[0].turn)
            event(base + 4, pair[0].to_mates)
        else:
            event(base + 1, pair[0].turn)
            event(base + 2, pair[0].to_mates)
            event(base + 3, pair[1].turn)
            event(base + 4, pair[1].to_mates)
        if step + 1 < others:
            event(base + 4, *[gather.begin for gather in gathers[step + 1]])
        event(base + 5, *[gather.near_rows for gather in pair])
        event(base + 6 + (len(pair) > 1), *[gather.turned for gather in pair])
        event(base + 8, *[gather.far_rows for gather in pair])

    def body(block, carry):
        slot = lax.rem(block, 2)
        is_own = block < blocks

        @pl.when(is_own)
        def _():
            for copy in own_loads(block, slot):
                copy.wait()

        @pl.when(block == blocks)
        def _():
            for copy in weights:
                copy.wait()

        @pl.when(block >= blocks)
        def _():
            for copy in other_loads(block, slot):
                copy.wait()
            tile = units // 2
            for at in range(2):
                there = pl.ds(at * tile, tile)
                gelu_value, slope = gelu_parts(dot_nt(gate_w[there, :], mid[slot]))
                up_lin = dot_nt(up_w[there, :], mid[slot])
                hidden_back = dot_nt(down_w[there, :], back[slot]).astype(low).astype(jnp.float32)
                hidden[there, :] = (gelu_value * up_lin).astype(low)
                gate_back[there, :] = (hidden_back * up_lin * slope).astype(low)
                up_back[there, :] = (hidden_back * gelu_value).astype(low)

        for when, actions in events.items():

            @pl.when(block == when)
            def _(actions=actions):
                for action in actions:
                    action()

        @pl.when(block + 1 < blocks)
        def _():
            for copy in own_loads(block + 1, 1 - slot):
                copy.start()

        @pl.when((block + 1 >= blocks) & (block < last))
        def _():
            for copy in other_loads(block + 1, 1 - slot):
                copy.start()

        for first in (True, False):

            @pl.when(block == 0 if first else (block > 0) & is_own)
            def _(first=first):
                add(down_sum, dot_tn, own_hidden.at[slot], back, slot, first)
                add(gate_sum, dot_tn, own_gate.at[slot], mid, slot, first)
                add(up_sum, dot_tn, own_up.at[slot], mid, slot, first)

        @pl.when(block >= blocks)
        def _():
            stores = []
            for at, (total, lhs, rhs, out) in enumerate(
                (
                    (down_sum, hidden, back, down_out),
                    (gate_sum, gate_back, mid, gate_out),
                    (up_sum, up_back, mid, up_out),
                )
            ):
                add(total, dot_nn, lhs, rhs, slot)
                stores.append(pltpu.make_async_copy(total, out, weight_sem.at[3 + at]))
                pl.when(block == last)(stores[-1].start)

            @pl.when(block == last)
            def _():
                for copy in stores:
                    copy.wait()

        return carry

    lax.fori_loop(0, last + 1, body, 0)
    for pair in gathers:
        for gather in pair:
            gather.finish()


def feedforward_grads(
    mid_near,
    mid_far,
    back_every,
    mid_tree,
    back_tree,
    hidden,
    gate_back,
    up_back,
    gate_w,
    up_w,
    down_w,
    mid_begun,
):
    replicas = lax.axis_size("replica")
    width = mid_tree.shape[1]
    tree_rows = mid_tree.shape[0]
    units = gate_w.shape[0]
    size = tree_rows // 6
    low, full = jnp.bfloat16, jnp.float32
    copies = GATHER_COPIES * 2 * (replicas - 1)
    grad = jax.ShapeDtypeStruct((units, width), full)
    gathered = jax.ShapeDtypeStruct((replicas - 1, tree_rows, width), low)
    return pl.pallas_call(
        functools.partial(grads_kernel, replicas),
        out_shape=(grad, grad, grad, gathered, gathered),
        in_specs=any_specs(12),
        out_specs=tuple(any_specs(5)),
        input_output_aliases={11: 3},
        scratch_shapes=[pltpu.VMEM((units, width), full)] * 3
        + [pltpu.VMEM((units, width), low)] * 3
        + [pltpu.VMEM((2, size, width), low)] * 2
        + [pltpu.VMEM((2, size, units), low)] * 3
        + [pltpu.VMEM((units, size), low)] * 3
        + [
            pltpu.SemaphoreType.DMA((copies,)),
            pltpu.SemaphoreType.DMA((copies,)),
            pltpu.SemaphoreType.DMA((2 * (replicas - 1),)),
            pltpu.SemaphoreType.DMA((2, 5)),
            pltpu.SemaphoreType.DMA((6,)),
        ],
        compiler_params=remote_params(5),
        cost_estimate=pl.CostEstimate(
            flops=2 * (6 * replicas - 3) * tree_rows * units * width,
            bytes_accessed=200 * 2**20,
            transcendentals=0,
        ),
    )(
        mid_near,
        mid_far,
        back_every,
        mid_tree,
        back_tree,
        hidden,
        gate_back,
        up_back,
        gate_w,
        up_w,
        down_w,
        mid_begun,
    )


def last_kernel(
    start_ref,
    mid_ref,
    back_ref,
    gate_hbm,
    up_hbm,
    down_hbm,
    gate_so_far,
    up_so_far,
    down_so_far,
    gate_out,
    up_out,
    down_out,
    gate_sum,
    up_sum,
    down_sum,
    gate_w,
    up_w,
    down_w,
    hidden,
    gate_back,
    up_back,
    sems,
):
    step = pl.program_id(0)
    final = step == pl.num_programs(0) - 1
    units = gate_w.shape[0]
    low = jnp.bfloat16
    weights = [
        pltpu.make_async_copy(source, target, sems.at[at])
        for at, (source, target) in enumerate(
            ((gate_hbm, gate_w), (up_hbm, up_w), (down_hbm, down_w))
        )
    ]
    sums = [
        pltpu.make_async_copy(source, target, sems.at[3 + at])
        for at, (source, target) in enumerate(
            ((down_so_far, down_sum), (gate_so_far, gate_sum), (up_so_far, up_sum))
        )
    ]

    @pl.when(step == 0)
    def _():
        for copy in weights:
            copy.start()
        for copy in weights:
            copy.wait()
        for copy in sums:
            copy.start()

    tile = units // 2
    for at in range(2):
        there = pl.ds(at * tile, tile)
        gelu_value, slope = gelu_parts(dot_nt(gate_w[there, :], mid_ref[...]))
        up_lin = dot_nt(up_w[there, :], mid_ref[...])
        hidden_back = dot_nt(down_w[there, :], back_ref[...]).astype(low).astype(jnp.float32)
        hidden[there, :] = (gelu_value * up_lin).astype(low)
        gate_back[there, :] = (hidden_back * up_lin * slope).astype(low)
        up_back[there, :] = (hidden_back * gelu_value).astype(low)
    stores = []
    for at, (total, lhs, rhs, out) in enumerate(
        (
            (down_sum, hidden, back_ref, down_out),
            (gate_sum, gate_back, mid_ref, gate_out),
            (up_sum, up_back, mid_ref, up_out),
        )
    ):
        pl.when(step == 0)(sums[at].wait)

        def part(at, total=total, lhs=lhs, rhs=rhs):
            total[at, :] += dot_nn(lhs[at, :], rhs[...])

        by_rows(units, part, units // 2)
        stores.append(pltpu.make_async_copy(total, out, sems.at[6 + at]))
        pl.when(final)(stores[-1].start)

    @pl.when(final)
    def _():
        for copy in stores:
            copy.wait()


def last_grads(gate_sum, up_sum, down_sum, mid_rows, back_rows, gate_w, up_w, down_w):
    trees, tree_rows, width = mid_rows.shape
    units = gate_w.shape[0]
    size = tree_rows // 6
    low, full = jnp.bfloat16, jnp.float32
    start = (3 * (1 - lax.axis_index("shard") // 4)).reshape(1)

    def block(step, start_ref):
        return trees - 1, start_ref[0] + step, 0

    grad = jax.ShapeDtypeStruct((units, width), full)
    return pl.pallas_call(
        last_kernel,
        grid_spec=pltpu.PrefetchScalarGridSpec(
            num_scalar_prefetch=1,
            grid=(3,),
            in_specs=[pl.BlockSpec((None, size, width), block)] * 2 + any_specs(6),
            out_specs=tuple(any_specs(3)),
            scratch_shapes=[pltpu.VMEM((units, width), full)] * 3
            + [pltpu.VMEM((units, width), low)] * 3
            + [pltpu.VMEM((units, size), low)] * 3
            + [pltpu.SemaphoreType.DMA((9,))],
        ),
        out_shape=(grad, grad, grad),
        compiler_params=pltpu.CompilerParams(vmem_limit_bytes=VMEM_BYTES),
        cost_estimate=pl.CostEstimate(
            flops=6 * tree_rows * units * width, bytes_accessed=90 * 2**20, transcendentals=0
        ),
    )(start, mid_rows, back_rows, gate_w, up_w, down_w, gate_sum, up_sum, down_sum)


def turn(values, cos, sin):
    half = values.shape[-1] // 2
    first, second = values[:, :half], values[:, half:]
    return first * cos - second * sin, second * cos + first * sin


def turn_back(values, cos, sin):
    half = values.shape[-1] // 2
    first, second = values[:, :half], values[:, half:]
    return first * cos + second * sin, second * cos - first * sin


def allowed_block(query_bits, key_bits, query_start, key_start):
    shape = (query_bits.shape[0], key_bits.shape[1])
    query = query_start + lax.broadcasted_iota(jnp.int32, shape, 0)
    key = key_start + lax.broadcasted_iota(jnp.int32, shape, 1)
    return (((query_bits & key_bits) != 0) & (key < query)) | (key == query)


def attention_forward_kernel(
    stream,
    gain,
    cos_ref,
    sin_ref,
    query_bits,
    key_bits,
    query_w,
    key_own,
    value_own,
    output_w,
    post_gain,
    next_gain,
    valid,
    tree_out,
    query_out,
    key_out,
    value_out,
    attended_out,
    mass_out,
    total,
    middle_out,
    next_out,
    sums_out,
    own,
    tree,
    key_w,
    value_w,
    lin,
    send_sem,
    recv_sem,
    local_sem,
    *scratch,
):
    plane = Plane()
    rows, width = stream.shape
    head = query_w.shape[0]
    block = 2 * rows
    half = head // 2
    low, full = jnp.bfloat16, jnp.float32
    wires = Wires(send_sem, recv_sem)

    def normed(at):
        value = stream[at, :].astype(full)
        own[at, :] = norm_rows(value, gain[...]).astype(low)

    by_rows(rows, normed)
    greet(plane.near())
    mine = block_at(plane.core * half, half)
    key_w[mine, :] = key_own[...]
    value_w[mine, :] = value_own[...]
    tree[block_at(plane.me * rows, rows), :] = own[...]
    halves = [
        wires.send(key_own, key_w.at[mine], plane.mate),
        wires.send(value_own, value_w.at[mine], plane.mate),
    ]
    seen = []

    def use(chip):
        if not seen:
            for copy in halves:
                copy.wait_recv()
        seen.append(chip)
        there = block_at(chip * block, block)
        cos, sin = cos_ref[there, :], sin_ref[there, :]
        lin[...] = dot_nt(tree[there, :], query_w[...])
        first, second = turn(lin[...], cos, sin)
        query_out[there, :half] = (first * head**-0.5).astype(low)
        query_out[there, half:] = (second * head**-0.5).astype(low)
        lin[...] = dot_nt(tree[there, :], key_w[...])
        first, second = turn(lin[...], cos, sin)
        key_out[there, :half] = first.astype(low)
        key_out[there, half:] = second.astype(low)
        value_out[there, :] = dot_nt(tree[there, :], value_w[...]).astype(low)

    gather_tree(wires, plane, own, tree, rows, use)
    store = load(tree, tree_out, local_sem.at[0])
    gathered = list(wires.sent)

    def attend(chip):
        there = block_at(chip * block, block)
        bits = query_bits[there, :]

        def chunk(at, carry):
            result, mass = carry
            keys = block_at(at * block, block)
            scores = dot_nt(query_out[there, :], key_out[keys, :])
            allowed = allowed_block(
                bits, key_bits[:, pl.ds(pl.multiple_of(at * block, 128), block)], chip * block, at * block
            )
            raised = jnp.where(allowed, jnp.exp(score_cap * jnp.tanh(scores / score_cap)), 0.0)
            result += dot_nn(raised.astype(low), value_out[keys, :])
            return result, mass + jnp.sum(raised, axis=1, keepdims=True)

        result, mass = lax.fori_loop(
            0,
            chip + 1,
            chunk,
            (jnp.zeros((block, head), full), jnp.zeros((block, 1), full)),
        )
        scale = 1.0 / mass
        attended_out[there, :] = (result * scale).astype(low)
        mass_out[there, :] = jnp.broadcast_to(scale, (block, mass_out.shape[1]))

    def product(chip, columns):
        return dot_nn(attended_out[block_at(chip * block, block), :], output_w[:, columns])

    scatter_sum(wires, plane, scratch, product, total, attend)
    sums_out[...] = jnp.zeros_like(sums_out)

    def finish(at):
        value = stream[at, :].astype(full)
        branch = norm_rows(total[at, :], post_gain[...])
        middle = value + branch
        middle_out[at, :] = middle
        next_out[at, :] = norm_rows(middle, next_gain[...]).astype(low)
        add_row(sums_out, 0, valid[at, :] * value * value)
        add_row(sums_out, 1, valid[at, :] * branch * branch)

    by_rows(rows, finish)
    for copy in gathered:
        copy.wait_send()
    store.wait()


def attention_forward(
    stream,
    gain,
    cos,
    sin,
    query_bits,
    key_bits,
    query_weight,
    key_weight,
    value_weight,
    output_weight,
    post_gain,
    next_gain,
    valid,
):
    rows, width = stream.shape
    head = query_weight.shape[0]
    tree_rows = cos.shape[0]
    low, full = jnp.bfloat16, jnp.float32
    copies = GATHER_COPIES + SCATTER_COPIES + 2
    heads = jax.ShapeDtypeStruct((tree_rows, head), low)
    return pl.pallas_call(
        attention_forward_kernel,
        out_shape=(
            jax.ShapeDtypeStruct((tree_rows, width), low),
            heads,
            heads,
            heads,
            heads,
            jax.ShapeDtypeStruct((tree_rows, 128), full),
            jax.ShapeDtypeStruct((rows, width), full),
            jax.ShapeDtypeStruct((rows, width), full),
            jax.ShapeDtypeStruct((rows, width), low),
            jax.ShapeDtypeStruct((8, width), full),
        ),
        in_specs=vmem_specs(13),
        out_specs=tuple(any_specs(1) + vmem_specs(9)),
        scratch_shapes=[
            pltpu.VMEM((rows, width), low),
            pltpu.VMEM((tree_rows, width), low),
            pltpu.VMEM((head, width), low),
            pltpu.VMEM((head, width), low),
            pltpu.VMEM((2 * rows, head), full),
            pltpu.SemaphoreType.DMA((copies,)),
            pltpu.SemaphoreType.DMA((copies,)),
            pltpu.SemaphoreType.DMA((1,)),
        ]
        + scatter_scratch(rows, width),
        compiler_params=remote_params(3),
        cost_estimate=pl.CostEstimate(
            flops=10 * tree_rows * head * width, bytes_accessed=20 * 2**20, transcendentals=0
        ),
    )(
        stream,
        gain[None],
        cos,
        sin,
        query_bits,
        key_bits,
        query_weight,
        key_weight,
        value_weight,
        output_weight,
        post_gain[None],
        next_gain[None],
        valid,
    )


def attention_backward_kernel(
    replicas,
    own,
    cos_ref,
    sin_ref,
    query_bits,
    key_bits,
    weights,
    output_w,
    queries,
    keys_ref,
    values,
    attended,
    mass,
    gain,
    valid,
    first_sums,
    second_sums,
    third_sums,
    stream_hbm,
    middle_back_hbm,
    normed_hbm,
    mid_near,
    ffn_own,
    tree_out,
    mid_rows,
    every_out,
    back_out,
    grads_out,
    input_out,
    sums_out,
    total,
    tree,
    normed,
    attended_back,
    query_sum,
    key_sum,
    value_sum,
    mate_out,
    mate_in,
    send_sem,
    recv_sem,
    local_sem,
    mid_send_sem,
    mid_recv_sem,
    *scratch,
):
    plane = Plane()
    rows, width = own.shape
    head = output_w.shape[0]
    half = head // 2
    block = 2 * rows
    low, full = jnp.bfloat16, jnp.float32
    wires = Wires(send_sem, recv_sem)
    normed_load = load(normed_hbm, normed, local_sem.at[1])
    mid_gather = PlaneGather(
        plane,
        lambda: mid_near.at[0],
        mid_rows.at[0],
        rows,
        mid_send_sem,
        mid_recv_sem,
        local_sem.at[2],
        0,
    )
    steps = list(range(1, replicas))
    greet(plane.near() + [replica_device(replicas, step) for step in steps])
    over = send_over(wires, ffn_own, every_out, replicas, steps)
    tree[block_at(plane.me * rows, rows), :] = own[...]
    key_sum[...] = jnp.zeros_like(key_sum)
    value_sum[...] = jnp.zeros_like(value_sum)

    seen = []

    def use(chip):
        seen.append(chip)
        if len(seen) == 3:
            mid_gather.begin()
        there = block_at(chip * block, block)
        attended_back[there, :] = dot_nt(tree[there, :], output_w[...]).astype(low)
        inner = jnp.sum(
            attended_back[there, :].astype(full) * attended[there, :].astype(full),
            axis=1,
            keepdims=True,
        )
        bits = query_bits[there, :]
        scale = mass[there, :1]

        def chunk(at, result):
            here = block_at(at * block, block)
            tanh_value = jnp.tanh(dot_nt(queries[there, :], keys_ref[here, :]) / score_cap)
            allowed = allowed_block(
                bits, key_bits[:, pl.ds(pl.multiple_of(at * block, 128), block)], chip * block, at * block
            )
            probs = jnp.where(allowed, jnp.exp(score_cap * tanh_value) * scale, 0.0)
            prob_grads = dot_nt(attended_back[there, :], values[here, :])
            score_back = (probs * (prob_grads - inner) * (1.0 - tanh_value * tanh_value)).astype(low)
            value_sum[here, :] += dot_tn(probs.astype(low), attended_back[there, :])
            key_sum[here, :] += dot_tn(score_back, queries[there, :])
            return result + dot_nn(score_back, keys_ref[here, :])

        result = lax.fori_loop(0, chip + 1, chunk, jnp.zeros((block, head), full))
        first, second = turn_back(result * head**-0.5, cos_ref[there, :], sin_ref[there, :])
        query_sum[there, :half] = first.astype(low)
        query_sum[there, half:] = second.astype(low)

    gather_tree(wires, plane, own, tree, rows, use)
    store = load(tree, tree_out, local_sem.at[0])
    back_out[:, :head] = query_sum[...]
    first_core = plane.core == 0

    def exchange(at):
        first, second = turn_back(key_sum[at, :], cos_ref[at, :], sin_ref[at, :])
        key_sum[at, :half] = jnp.where(first_core, first, second)
        mate_out[at, :half] = jnp.where(first_core, second, first)
        first, second = value_sum[at, :half], value_sum[at, half:]
        value_sum[at, :half] = jnp.where(first_core, first, second)
        mate_out[at, half:] = jnp.where(first_core, second, first)

    by_rows(tree.shape[0], exchange)
    swap = wires.send(mate_out, mate_in, plane.mate)
    swap.wait_recv()

    def finish(at):
        back_out[at, head : head + half] = (key_sum[at, :half] + mate_in[at, :half]).astype(low)
        back_out[at, head + half :] = (value_sum[at, :half] + mate_in[at, half:]).astype(low)

    by_rows(tree.shape[0], finish)
    gathered = list(wires.sent)

    def product(chip, columns):
        return dot_nn(back_out[block_at(chip * block, block), :], weights[:, columns])

    def projection_grads():
        mid_gather.turn()
        mid_gather.to_mates()
        normed_load.wait()

        def tile(columns):
            grads_out[: 2 * head, columns] = dot_tn(back_out[...], normed[:, columns]).astype(low)

        by_columns(width, tile)

    def output_grads():
        mid_gather.turned()

        def tile(columns):
            grads_out[2 * head :, columns] = dot_tn(attended[...], tree[:, columns]).astype(low)

        by_columns(width, tile)

    scatter_sum(
        wires, plane, scratch, product, total, meanwhile=(projection_grads, output_grads)
    )
    sums_out[...] = jnp.zeros_like(sums_out)

    stream, middle_back = scratch[2].at[0], scratch[0].at[1]
    late = [
        load(stream_hbm, stream, local_sem.at[3]),
        load(middle_back_hbm, middle_back, local_sem.at[4]),
    ]
    for copy in late:
        copy.wait()

    def input_rows(at):
        back, gain_terms = norm_back(stream[at, :].astype(full), gain[...], total[at, :])
        input_out[at, :] = middle_back[at, :] + back
        add_row(sums_out, 0, gain_terms)

    by_rows(rows, input_rows)
    sums_out[1:3, :] = third_sums[0:2, :]
    sums_out[3:6, :] = second_sums[0:3, :]
    sums_out[6:8, :] = first_sums[0:2, :]
    sums_out[8:9, :] = jnp.broadcast_to(jnp.sum(valid[...], axis=0, keepdims=True), (1, width))
    mid_gather.near_rows()
    mid_gather.far_rows()
    mid_gather.finish()
    for copy in over:
        copy.wait_recv()
    for copy in gathered:
        copy.wait_send()
    store.wait()


def attention_backward(
    own, cos, sin, query_bits, key_bits, weights, output_weight, queries, keys, values, attended, mass,
    stream, gain, middle_back, valid, sums, normed, mid_near, ffn_own,
):
    rows, width = own.shape
    head = output_weight.shape[0]
    tree_rows = cos.shape[0]
    replicas = lax.axis_size("replica")
    low, full = jnp.bfloat16, jnp.float32
    copies = GATHER_COPIES + SCATTER_COPIES + replicas
    return pl.pallas_call(
        functools.partial(attention_backward_kernel, replicas),
        out_shape=(
            jax.ShapeDtypeStruct((tree_rows, width), low),
            jax.ShapeDtypeStruct((replicas - 1, tree_rows, width), low),
            jax.ShapeDtypeStruct((replicas - 1, rows, width), low),
            jax.ShapeDtypeStruct((tree_rows, 2 * head), low),
            jax.ShapeDtypeStruct((3 * head, width), low),
            jax.ShapeDtypeStruct((rows, width), full),
            jax.ShapeDtypeStruct((16, width), full),
        ),
        in_specs=vmem_specs(17) + any_specs(5),
        out_specs=tuple(any_specs(3) + vmem_specs(4)),
        scratch_shapes=[
            pltpu.VMEM((rows, width), full),
            pltpu.VMEM((tree_rows, width), low),
            pltpu.VMEM((tree_rows, width), low),
            pltpu.VMEM((tree_rows, head), low),
            pltpu.VMEM((tree_rows, head), low),
            pltpu.VMEM((tree_rows, head), full),
            pltpu.VMEM((tree_rows, head), full),
            pltpu.VMEM((tree_rows, head), full),
            pltpu.VMEM((tree_rows, head), full),
            pltpu.SemaphoreType.DMA((copies,)),
            pltpu.SemaphoreType.DMA((copies,)),
            pltpu.SemaphoreType.DMA((5,)),
            pltpu.SemaphoreType.DMA((GATHER_COPIES,)),
            pltpu.SemaphoreType.DMA((GATHER_COPIES,)),
        ]
        + scatter_scratch(rows, width),
        compiler_params=remote_params(4),
        cost_estimate=pl.CostEstimate(
            flops=10 * tree_rows * head * width, bytes_accessed=20 * 2**20, transcendentals=0
        ),
    )(own, cos, sin, query_bits, key_bits, weights, output_weight, queries, keys, values, attended, mass, gain[None], valid, *sums, stream, middle_back, normed, mid_near, ffn_own)


def shards_heads(
    hidden_in,
    cotangent,
    token_segment,
    token_valid,
    segment_parent,
    query_weight,
    key_weight,
    value_weight,
    output_weight,
    gate_weight,
    up_weight,
    down_weight,
    attention_gain,
    attention_post_gain,
    feedforward_gain,
    feedforward_post_gain,
):
    row_count, model_width = hidden_in.shape
    shard = lax.axis_index("shard")
    row_start = shard * row_count
    position, parent_tok, grand_tok = tree_tables(token_segment, token_valid, segment_parent[0])
    key_bits = jnp.where(token_valid == 1, 1 << token_segment, 0)[None]
    query_bits = ((1 << token_segment) | (1 << parent_tok) | (1 << grand_tok))[:, None]
    cos_table, sin_table = rope_tables(position, HEAD)
    cos_table, sin_table = cos_table[:, 0, : HEAD // 2], sin_table[:, 0, : HEAD // 2]
    valid_rows = lax.dynamic_slice_in_dim(token_valid, row_start, row_count)
    valid_rows = valid_rows.astype(jnp.float32)[:, None]
    (
        normed_in,
        queries,
        keys,
        values,
        attended,
        mass,
        attention_pre,
        middle,
        normed_mid,
        first_sums,
    ) = attention_forward(
        hidden_in,
        attention_gain,
        cos_table,
        sin_table,
        query_bits,
        key_bits,
        query_weight,
        key_weight,
        value_weight,
        output_weight,
        attention_post_gain,
        feedforward_gain,
        valid_rows,
    )
    mid_tree, hidden, mix, gelu_value, mid_near, block_out, ffpre_low, second_sums = (
        feedforward_forward(
            normed_mid,
            middle,
            cotangent,
            valid_rows,
            feedforward_post_gain,
            gate_weight,
            up_weight,
            down_weight,
        )
    )
    ffpre_tree, gate_back, up_back, mid_far, middle_back, pre_low, third_sums = (
        feedforward_backward(
            ffpre_low,
            middle,
            attention_pre,
            cotangent,
            valid_rows,
            feedforward_gain,
            attention_post_gain,
            normed_mid,
            gate_weight,
            up_weight,
            down_weight,
            mix,
            gelu_value,
        )
    )
    (
        pre_tree,
        mid_begun,
        ffpre_every,
        projection_back,
        attention_grads,
        input_grad,
        sums,
    ) = attention_backward(
        pre_low,
        cos_table,
        sin_table,
        query_bits,
        key_bits,
        jnp.concatenate([query_weight, key_weight, value_weight]),
        output_weight,
        queries,
        keys,
        values,
        attended,
        mass,
        hidden_in,
        attention_gain,
        middle_back,
        valid_rows,
        (first_sums, second_sums, third_sums),
        normed_in,
        mid_near,
        ffpre_low,
    )
    attention_grads = lax.psum(attention_grads, "replica").astype(jnp.float32)
    sizes = [query_weight.shape[0], key_weight.shape[0], value_weight.shape[0]]
    query_sum, key_sum, value_sum, output_sum = jnp.split(
        attention_grads, [sizes[0], sizes[0] + sizes[1], sum(sizes)]
    )
    gate_sum, up_sum, down_sum, mid_rows, back_rows = feedforward_grads(
        mid_near,
        mid_far,
        ffpre_every,
        mid_tree,
        ffpre_tree,
        hidden,
        gate_back,
        up_back,
        gate_weight,
        up_weight,
        down_weight,
        mid_begun,
    )
    gate_sum, up_sum, down_sum = last_grads(
        gate_sum, up_sum, down_sum, mid_rows, back_rows, gate_weight, up_weight, down_weight
    )
    smalls = jnp.sum(lax.all_gather(sums, ("replica", "shard")), axis=0)
    gain_one, gain_three, gain_two, gain_four = smalls[0], smalls[1], smalls[2], smalls[3]
    totals = jnp.sum(smalls[4:], axis=1)
    squares_all = jnp.stack([totals[2], totals[3], totals[0], totals[1]])
    valid_all = totals[4]
    stream_rms = jnp.sqrt(squares_all / valid_all)
    return (
        block_out,
        input_grad,
        query_sum,
        key_sum,
        value_sum,
        output_sum,
        gate_sum,
        up_sum,
        down_sum,
        gain_one,
        gain_two,
        gain_three,
        gain_four,
        stream_rms,
    )


def solution(mesh):
    heads_fit = mesh.shape["shard"] == HEADS and mesh.shape["replica"] > 2
    return jax.shard_map(
        shards_heads if heads_fit else shards_generic,
        mesh=mesh,
        in_specs=(
            P(("replica", "shard"), None),
            P(("replica", "shard"), None),
            P("replica"),
            P("replica"),
            P("replica", None),
            P("shard", None),
            P("shard", None),
            P("shard", None),
            P("shard", None),
            P("shard", None),
            P("shard", None),
            P("shard", None),
            P(),
            P(),
            P(),
            P(),
        ),
        out_specs=(
            P(("replica", "shard"), None),
            P(("replica", "shard"), None),
            P("shard", None),
            P("shard", None),
            P("shard", None),
            P("shard", None),
            P("shard", None),
            P("shard", None),
            P("shard", None),
            P(),
            P(),
            P(),
            P(),
            P(),
        ),
        check_vma=False,
    )
```
